32 devices in a mesh: replica: 4 (over x, core), group: 8 (over z, y).
Axes of the slice: x: 2, y: 2, z: 4, core: 2. Of those that a mesh axis runs over, the one named last changes fastest.
Arguments:
- block_input: bfloat16 [24576, 768], P(('replica', 'group')), may hold values from -6 to 6
- out_grad: bfloat16 [24576, 768], P(('replica', 'group')), may hold values from -6 to 6
- image_pos: int32 [24576, 2], P(('replica', 'group')), may hold values from 0 to 197, as said below
- routes: int32 [24576, 2], P(('replica', 'group')), may hold values from 0 to 3, all different within a row; in each aligned block of 768 rows (0 to 767, 768 to 1535, ...) at most 480 rows name the same one
- norm_weight: float32 [4, 768], P(None, 'group'), as said below
- norm_moment: float32 [4, 768], P(None, 'group')
- norm_squares: float32 [4, 768], P(None, 'group'), as said below
- qkv_weight: float32 [768, 2304], P('group'), may hold values from -0.21875 to 0.21875
- qkv_moment: float32 [768, 2304], P('group')
- qkv_squares: float32 [768, 2304], P('group'), as said below
- proj_weight: float32 [768, 768], P('group'), may hold values from -1.75 to 1.75
- proj_moment: float32 [768, 768], P('group')
- proj_squares: float32 [768, 768], P('group'), as said below
- router_weight: float32 [768, 4], P('group'), may hold values from -0.15625 to 0.15625
- router_moment: float32 [768, 4], P('group')
- router_squares: float32 [768, 4], P('group'), as said below
- inner_weight: float32 [4, 768, 3072], P(None, 'group'), may hold values from -0.21875 to 0.21875
- inner_moment: float32 [4, 768, 3072], P(None, 'group')
- inner_squares: float32 [4, 768, 3072], P(None, 'group'), as said below
- outer_weight: float32 [4, 3072, 768], P(None, None, 'group'), may hold values from -0.4375 to 0.4375
- outer_moment: float32 [4, 3072, 768], P(None, None, 'group')
- outer_squares: float32 [4, 3072, 768], P(None, None, 'group'), as said below
Outputs:
- block_output: bfloat16 [24576, 768], P(('replica', 'group'))
- input_grad: bfloat16 [24576, 768], P(('replica', 'group'))
- norm_drift: float32 [4, 768], P(None, 'group')
- norm_energy: float32 [4, 768], P(None, 'group')
- norm_after: float32 [4, 768], P(None, 'group')
- qkv_drift: float32 [768, 2304], P('group')
- qkv_energy: float32 [768, 2304], P('group')
- qkv_after: float32 [768, 2304], P('group')
- proj_drift: float32 [768, 768], P('group')
- proj_energy: float32 [768, 768], P('group')
- proj_after: float32 [768, 768], P('group')
- router_drift: float32 [768, 4], P('group')
- router_energy: float32 [768, 4], P('group')
- router_after: float32 [768, 4], P('group')
- inner_drift: float32 [4, 768, 3072], P(None, 'group')
- inner_energy: float32 [4, 768, 3072], P(None, 'group')
- inner_after: float32 [4, 768, 3072], P(None, 'group')
- outer_drift: float32 [4, 3072, 768], P(None, None, 'group')
- outer_energy: float32 [4, 3072, 768], P(None, None, 'group')
- outer_after: float32 [4, 3072, 768], P(None, None, 'group')
The draws below stay inside these ranges and needn't reach their ends.
Inputs may be any that keep to these rules, and one draw needn't show every extreme that they name: `image_pos`: rows are laid out image after image in row order; images hold 98 to 197 tokens; column 1 is the length of the row's image and the same on all its rows; column 0 rises by one from row to row and returns to 0 where the next image begins; no image begins at a row that is a multiple of 768 other than row 0; the first image may begin before row 0 and the last may end after the last row. `routes`: a token's two experts differ; within the rows of one device no expert is named by more than 480 tokens. `norm_weight`: rows 0 and 2 are gains, rows 1 and 3 biases. `norm_squares`: positive. `qkv_squares`: positive. `proj_squares`: positive. `router_squares`: positive. `inner_squares`: positive. `outer_squares`: positive.
All inputs are finite; a program needn't handle non-finite values.
Results may differ from the reference program's by a relative error of at most 0.025.
Values may be sent and summed in bfloat16 or wider, within the bound.
No kernel may reach another device: no remote copies, remote signals or barrier semaphores. Data moves between devices by JAX's collectives and lax.ppermute only.
A program may use at most 384 MiB of HBM per device.

```python
import math
from functools import partial
import jax
import jax.numpy as jnp
import numpy as np
from jax import lax

D = 768
HEADS = 12
FF = 3072
EXPERTS = 4
TOPK = 2
IMG = 197
STEP = 10
TOK_DEV = 768
CAP = 480
ROWS = 24576


def moment_values(key, shape, grad_size):
    values = jax.random.normal(key, shape, jnp.float32)
    return 0.11 * grad_size * jnp.clip(values, -4.0, 4.0)


def square_values(key, shape, grad_size):
    spread = jax.random.uniform(key, shape, jnp.float32)
    return 0.001 * grad_size * grad_size * jnp.exp(spread * math.log(4.0))


def draw_image_pos(key, part):
    key = jax.random.fold_in(key, 1)
    length_key, full_key, offset_key = jax.random.split(key, 3)
    image_count = ROWS // (IMG // 2) + 2
    lengths = jax.random.randint(length_key, (image_count,), IMG // 2, IMG + 1, dtype=jnp.int32)
    full_image = jax.random.randint(full_key, (), 1, max(ROWS // IMG, 2), dtype=jnp.int32)
    lengths = lengths.at[full_image].set(IMG).at[full_image + 1].set(IMG).astype(jnp.int32)
    offset = jax.random.randint(offset_key, (), 0, IMG // 2, dtype=jnp.int32)

    def place(start, length):
        finish = start + length
        on_edge = finish % TOK_DEV == 0
        moved = jnp.where(length < IMG, length + 1, length - 1).astype(jnp.int32)
        used = jnp.where(on_edge, moved, length).astype(jnp.int32)
        return ((start + used).astype(jnp.int32), used)
    first_start = (jnp.zeros((), jnp.int32) - offset).astype(jnp.int32)
    last_end, used_lengths = lax.scan(place, first_start, lengths)
    ends = (jnp.cumsum(used_lengths).astype(jnp.int32) - offset).astype(jnp.int32)
    row_index = jnp.arange(ROWS, dtype=jnp.int32)
    image_id = jnp.searchsorted(ends, row_index, side='right').astype(jnp.int32)
    row_length = used_lengths[image_id]
    position = (row_index - (ends[image_id] - row_length)).astype(jnp.int32)
    return jnp.stack([position, row_length], axis=1).astype(jnp.int32)


def draw_norm_weight(key, part):
    key = jax.random.fold_in(key, 2)
    gain_key, bias_key = jax.random.split(key)
    gains = 0.7 + 0.6 * jax.random.uniform(gain_key, (4, D), jnp.float32)
    biases = 0.2 * jnp.clip(jax.random.normal(bias_key, (4, D), jnp.float32), -4.0, 4.0)
    row_ids = lax_rows(4, D)
    return jnp.where(row_ids % 2 == 0, gains, biases)


def lax_rows(height, width):
    return jnp.arange(height, dtype=jnp.int32)[:, None] + jnp.zeros((height, width), jnp.int32)


def draw_norm_moment(key, part):
    key = jax.random.fold_in(key, 3)
    return moment_values(key, (4, D), 2.0 * math.sqrt(ROWS))


def draw_norm_squares(key, part):
    key = jax.random.fold_in(key, 4)
    return square_values(key, (4, D), 2.0 * math.sqrt(ROWS))


def draw_qkv_moment(key, part):
    key = jax.random.fold_in(key, 5)
    return moment_values(key, (D, 3 * D), 1.5 * math.sqrt(ROWS))


def draw_qkv_squares(key, part):
    key = jax.random.fold_in(key, 6)
    return square_values(key, (D, 3 * D), 1.5 * math.sqrt(ROWS))


def draw_proj_moment(key, part):
    key = jax.random.fold_in(key, 7)
    return moment_values(key, (D, D), 0.2 * math.sqrt(ROWS))


def draw_proj_squares(key, part):
    key = jax.random.fold_in(key, 8)
    return square_values(key, (D, D), 0.2 * math.sqrt(ROWS))


def draw_router_moment(key, part):
    key = jax.random.fold_in(key, 9)
    return moment_values(key, (D, EXPERTS), 18.0 * math.sqrt(ROWS))


def draw_router_squares(key, part):
    key = jax.random.fold_in(key, 10)
    return square_values(key, (D, EXPERTS), 18.0 * math.sqrt(ROWS))


def draw_inner_moment(key, part):
    key = jax.random.fold_in(key, 11)
    return moment_values(key, (EXPERTS, D, FF), 0.25 * math.sqrt(ROWS))


def draw_inner_squares(key, part):
    key = jax.random.fold_in(key, 12)
    return square_values(key, (EXPERTS, D, FF), 0.25 * math.sqrt(ROWS))


def draw_outer_moment(key, part):
    key = jax.random.fold_in(key, 13)
    return moment_values(key, (EXPERTS, FF, D), 0.12 * math.sqrt(ROWS))


def draw_outer_squares(key, part):
    key = jax.random.fold_in(key, 14)
    return square_values(key, (EXPERTS, FF, D), 0.12 * math.sqrt(ROWS))


def block_scale(own_key, shape, shards, smallest, high):
    level, own = 1.0, jax.random.fold_in(own_key, 6)
    for axis_at, shards_of in shards:
        draws = jnp.exp(jax.random.uniform(jax.random.fold_in(own, axis_at), (shards_of,), jnp.float32, smallest / len(shards), high / len(shards)))
        level = level * jnp.repeat(draws, shape[axis_at] // shards_of).reshape([-1 if axis == axis_at else 1 for axis in range(len(shape))])
    return level


def assign_block(stream_key, own, number, rows, number_of, top, reach, lean):
    ranking = jax.random.permutation(stream_key, number_of)
    packed, common = load_shares(number_of, rows * top, reach, lean, True), load_shares(number_of, rows * top, reach, lean, False)
    places = jnp.arange(number_of)

    def named(tallies, offset_by):
        used = int((tallies > 0).sum())
        fixed = max(1, used // 4)
        passed = fixed + (places - fixed + offset_by * (used - fixed)) % max(1, number_of - fixed)
        return jnp.zeros((number_of,), jnp.int32).at[ranking[jnp.where(places < fixed, places, passed)]].set(jnp.asarray(tallies, jnp.int32))

    tallies = jnp.where(number % 4 == 0, named(packed, number // 4), named(common, number - number // 4 - 1))
    mixed = jax.random.permutation(jax.random.fold_in(own, 3), number_of)
    donor, receiver = mixed[0:number_of // 2 * 2:2], mixed[1:number_of // 2 * 2:2]
    margin = jnp.minimum(tallies[donor] - 1, reach - tallies[receiver]) // 2
    margin = jnp.where((donor == ranking[0]) | (receiver == ranking[0]) | (tallies[receiver] == 0), 0, jnp.maximum(margin, 0))
    passed = jax.random.randint(jax.random.fold_in(own, 4), (number_of // 2,), 0, 1 << 20) % (margin + 1)
    tallies = tallies.at[donor].add(-passed).at[receiver].add(passed)
    items = jnp.searchsorted(jnp.cumsum(tallies), jnp.arange(rows * top), side="right").astype(jnp.int32)
    table = items.reshape(top, rows).T
    table = table[jax.random.permutation(jax.random.fold_in(own, 1), rows)]
    offset_by = jax.random.randint(jax.random.fold_in(own, 2), (rows, 1), 0, top)
    return jnp.take_along_axis(table, (jnp.arange(top)[None, :] + offset_by) % top, axis=1)


def load_shares(amount, total, limit, slope, full):
    loads = [(1 << 20) // math.isqrt(rank ** slope) + 1 for rank in range(1, amount + 1)]
    largest = limit if full else min(limit, max(-(-total // amount), total * loads[0] // sum(loads)))
    least = 1 if total - largest >= amount - 1 else 0
    holding, surplus = [largest] + [least] * (amount - 1), total - largest - least * (amount - 1)
    while surplus > 0:
        free = [i for i in range(1, amount) if holding[i] < largest] or [i for i in range(1, amount) if holding[i] < limit]
        whole, remaining = sum([loads[i] for i in free]), surplus
        for i in free:
            extra = min(limit - holding[i], max(1, remaining * loads[i] // whole), surplus)
            holding[i] = holding[i] + extra
            surplus = surplus - extra
    return np.array(holding)


def bell_draw(stream_key, dims, scale, bound, shards=(), kind=jnp.bfloat16):
    values = jax.random.normal(stream_key, dims, jnp.float32) * scale
    if len(shards) > 0:
        values = block_scale(stream_key, dims, shards, -0.22, 0.18) * values
    return jnp.clip(values, min=-bound, max=bound).astype(kind)


def setup_inputs(seed: int = 0) -> dict:
    streams_of = jax.random.split(jax.random.key(seed), 23)
    block_input = bell_draw(streams_of[0], (ROWS, D), 1.0, 6.0, ((0, 32),))
    out_grad = bell_draw(streams_of[1], (ROWS, D), 1.0, 6.0, ((0, 32),))
    image_pos = draw_image_pos(jax.random.fold_in(streams_of[22], 71), 0)
    routes_keys = jax.random.split(jax.random.fold_in(streams_of[3], 1), ROWS // TOK_DEV)
    routes_turns = jax.random.permutation(jax.random.fold_in(streams_of[3], 3), ROWS // TOK_DEV)
    routes = jax.vmap(lambda own, number: assign_block(jax.random.fold_in(streams_of[3], 2), own, number, TOK_DEV, EXPERTS, TOPK, CAP, 2))(routes_keys, routes_turns).reshape((ROWS, TOPK))
    norm_weight = draw_norm_weight(jax.random.fold_in(streams_of[22], 71), 0)
    norm_moment = draw_norm_moment(jax.random.fold_in(streams_of[22], 71), 0)
    norm_squares = draw_norm_squares(jax.random.fold_in(streams_of[22], 71), 0)
    qkv_weight = bell_draw(streams_of[7], (D, 3 * D), D ** -0.5, 0.21875, ((0, 8),), jnp.float32)
    qkv_moment = draw_qkv_moment(jax.random.fold_in(streams_of[22], 71), 0)
    qkv_squares = draw_qkv_squares(jax.random.fold_in(streams_of[22], 71), 0)
    proj_weight = bell_draw(streams_of[10], (D, D), (D // 64) ** -0.5, 1.75, ((0, 8),), jnp.float32)
    proj_moment = draw_proj_moment(jax.random.fold_in(streams_of[22], 71), 0)
    proj_squares = draw_proj_squares(jax.random.fold_in(streams_of[22], 71), 0)
    router_weight = bell_draw(streams_of[13], (D, EXPERTS), (2 * D) ** -0.5, 0.15625, ((0, 8),), jnp.float32)
    router_moment = draw_router_moment(jax.random.fold_in(streams_of[22], 71), 0)
    router_squares = draw_router_squares(jax.random.fold_in(streams_of[22], 71), 0)
    inner_weight = bell_draw(streams_of[16], (EXPERTS, D, FF), D ** -0.5, 0.21875, ((1, 8),), jnp.float32)
    inner_moment = draw_inner_moment(jax.random.fold_in(streams_of[22], 71), 0)
    inner_squares = draw_inner_squares(jax.random.fold_in(streams_of[22], 71), 0)
    outer_weight = bell_draw(streams_of[19], (EXPERTS, FF, D), (FF // 16) ** -0.5, 0.4375, ((2, 8),), jnp.float32)
    outer_moment = draw_outer_moment(jax.random.fold_in(streams_of[22], 71), 0)
    outer_squares = draw_outer_squares(jax.random.fold_in(streams_of[22], 71), 0)
    return {"block_input": block_input, "out_grad": out_grad, "image_pos": image_pos, "routes": routes, "norm_weight": norm_weight, "norm_moment": norm_moment, "norm_squares": norm_squares, "qkv_weight": qkv_weight, "qkv_moment": qkv_moment, "qkv_squares": qkv_squares, "proj_weight": proj_weight, "proj_moment": proj_moment, "proj_squares": proj_squares, "router_weight": router_weight, "router_moment": router_moment, "router_squares": router_squares, "inner_weight": inner_weight, "inner_moment": inner_moment, "inner_squares": inner_squares, "outer_weight": outer_weight, "outer_moment": outer_moment, "outer_squares": outer_squares}


@jax.custom_vjp
def low(v):
    return lax.optimization_barrier(v.astype(jnp.bfloat16)).astype(jnp.float32)

@jax.custom_vjp
def low_back(v):
    return v

def low_keep(v):
    return (low(v), None)

def low_pass(kept, grad):
    return (grad,)

def back_keep(v):
    return (v, None)

def back_low(kept, grad):
    return (low(grad),)
low.defvjp(low_keep, low_pass)
low_back.defvjp(back_keep, back_low)
NORM_EPS = 1e-06
MASKED = -1e+30
HIGH = lax.Precision.HIGHEST
RATES = (0.5, 0.08, 0.6, 0.06, 0.08, 0.15)

def standardize(values):
    centre = lax.optimization_barrier(jnp.mean(values, axis=-1, keepdims=True))
    shifted = values - centre
    row_scale = lax.rsqrt(lax.optimization_barrier(jnp.mean(shifted * shifted, axis=-1, keepdims=True)) + NORM_EPS)
    return shifted * row_scale

def softmax_rows(values):
    shifted = values - lax.optimization_barrier(jnp.max(values, axis=-1, keepdims=True))
    expo_values = jnp.exp(shifted)
    return expo_values / lax.optimization_barrier(jnp.sum(expo_values, axis=-1, keepdims=True))

def window_mask(positions, first_row, row_count, all_rows):
    halo_width = IMG - 1
    key_count = row_count + 2 * halo_width
    query_index = lax.broadcasted_iota(jnp.int32, (row_count, key_count), 0)
    key_index = lax.broadcasted_iota(jnp.int32, (row_count, key_count), 1)
    offset = key_index - halo_width - query_index + positions[:, 0:1]
    global_key = first_row - halo_width + key_index
    return (offset >= 0) & (offset < positions[:, 1:2]) & (global_key >= 0) & (global_key < all_rows)

def route_slots(routes, expert_count, capacity):
    row_count, route_count = routes.shape
    chosen = routes[:, :, None] == jnp.arange(expert_count, dtype=jnp.int32)[None, None, :]
    chosen_int = chosen.astype(jnp.int32)
    per_expert = lax.optimization_barrier(jnp.sum(chosen_int, axis=1)).astype(jnp.int32)
    before = (jnp.cumsum(per_expert, axis=0).astype(jnp.int32) - per_expert).astype(jnp.int32)
    slot_rank = lax.optimization_barrier(jnp.sum(chosen_int * before[:, None, :], axis=-1)).astype(jnp.int32)
    slot_index = (routes * capacity + slot_rank).astype(jnp.int32)
    flat_slots = slot_index.reshape(-1)
    row_ids = jnp.repeat(jnp.arange(row_count, dtype=jnp.int32), route_count)
    source_row = jnp.zeros((expert_count * capacity,), jnp.int32).at[flat_slots].set(row_ids)
    occupied = jnp.zeros((expert_count * capacity,), jnp.bool_).at[flat_slots].set(True)
    return (chosen, slot_index, source_row, occupied)

def forward(x_float, weights, image_pos, routes):
    norms, qkv_w, proj_w, router_w, inner_w, outer_w = [low(weight) for weight in weights]
    all_rows, model_width = x_float.shape
    head_size = model_width // HEADS
    halo_width = IMG - 1
    block_total = all_rows // TOK_DEV
    expert_count = inner_w.shape[0]
    capacity = 5 * TOK_DEV // 8
    score_scale = head_size ** (-0.5)
    first_in = low(standardize(x_float) * norms[0] + norms[1])
    qkv_rows = low(low_back(jnp.dot(first_in, qkv_w, precision=HIGH)))
    kv_padded = jnp.pad(qkv_rows[:, model_width:], ((halo_width, halo_width), (0, 0)))
    query_blocks = qkv_rows[:, :model_width].reshape(block_total, TOK_DEV, HEADS, head_size)
    pos_blocks = image_pos.reshape(block_total, TOK_DEV, 2)
    starts = (jnp.arange(block_total, dtype=jnp.int32) * TOK_DEV).astype(jnp.int32)

    def block_attend(inputs):
        queries, positions, first_row = inputs
        window = lax.dynamic_slice_in_dim(kv_padded, first_row, TOK_DEV + 2 * halo_width, 0)
        keys_win = window[:, :model_width].reshape(-1, HEADS, head_size)
        values_win = window[:, model_width:].reshape(-1, HEADS, head_size)
        allowed = window_mask(positions, first_row, TOK_DEV, all_rows)
        raw = jnp.einsum('qhd,khd->hqk', queries, keys_win, precision=HIGH) * score_scale
        scores = jnp.where(allowed[None], low_back(raw), MASKED)
        probs = low(softmax_rows(scores))
        mixed = jnp.einsum('hqk,khd->qhd', probs, values_win, precision=HIGH)
        return low(low_back(mixed)).reshape(TOK_DEV, model_width)
    context = lax.map(jax.checkpoint(block_attend), (query_blocks, pos_blocks, starts))
    context = context.reshape(all_rows, model_width)
    residual = x_float + low_back(jnp.dot(context, proj_w, precision=HIGH))
    second_in = low(standardize(residual) * norms[2] + norms[3])
    logits = low_back(jnp.dot(second_in, router_w, precision=HIGH))
    gate_probs = softmax_rows(logits)

    def block_experts(inputs):
        second_rows, route_rows, prob_rows = inputs
        chosen, slot_index, source_row, occupied = route_slots(route_rows, expert_count, capacity)
        slot_input = jnp.where(occupied[:, None], second_rows[source_row], 0.0)
        slot_input = slot_input.reshape(expert_count, capacity, model_width)
        pre_act = low_back(jnp.einsum('ecd,edf->ecf', slot_input, inner_w, precision=HIGH))
        activated = low(jax.nn.gelu(pre_act, approximate=False))
        expert_out = low_back(jnp.einsum('ecf,efd->ecd', activated, outer_w, precision=HIGH))
        token_out = expert_out.reshape(-1, model_width)[slot_index]
        gate_values = lax.optimization_barrier(jnp.sum(jnp.where(chosen, prob_rows[:, None, :], 0.0), axis=-1))
        return lax.optimization_barrier(jnp.sum(gate_values[:, :, None] * token_out, axis=1))
    mixture = lax.map(jax.checkpoint(block_experts), (second_in.reshape(block_total, TOK_DEV, model_width), routes.reshape(block_total, TOK_DEV, -1), gate_probs.reshape(block_total, TOK_DEV, -1)))
    return residual + mixture.reshape(all_rows, model_width)

def adam_step(weight, moment, squares, gradient, rate_value):
    drift = 0.9 * moment + 0.1 * gradient
    energy = 0.999 * squares + 0.001 * gradient * gradient
    first_hat = drift / (1.0 - 0.9 ** STEP)
    second_hat = energy / (1.0 - 0.999 ** STEP)
    after = weight - rate_value * (first_hat / (jnp.sqrt(second_hat) + 1e-08) + 0.1 * weight)
    return (drift, energy, after)

def reference(block_input, out_grad, image_pos, routes, norm_weight, norm_moment, norm_squares, qkv_weight, qkv_moment, qkv_squares, proj_weight, proj_moment, proj_squares, router_weight, router_moment, router_squares, inner_weight, inner_moment, inner_squares, outer_weight, outer_moment, outer_squares):
    weights = (norm_weight, qkv_weight, proj_weight, router_weight, inner_weight, outer_weight)
    x_float = block_input.astype(jnp.float32)
    result, backward = jax.vjp(partial(forward, image_pos=image_pos, routes=routes), x_float, weights)
    input_grad, grads = backward(out_grad.astype(jnp.float32))
    norm_drift, norm_energy, norm_after = adam_step(norm_weight, norm_moment, norm_squares, grads[0], RATES[0])
    qkv_drift, qkv_energy, qkv_after = adam_step(qkv_weight, qkv_moment, qkv_squares, grads[1], RATES[1])
    proj_drift, proj_energy, proj_after = adam_step(proj_weight, proj_moment, proj_squares, grads[2], RATES[2])
    router_drift, router_energy, router_after = adam_step(router_weight, router_moment, router_squares, grads[3], RATES[3])
    inner_drift, inner_energy, inner_after = adam_step(inner_weight, inner_moment, inner_squares, grads[4], RATES[4])
    outer_drift, outer_energy, outer_after = adam_step(outer_weight, outer_moment, outer_squares, grads[5], RATES[5])
    return (result.astype(jnp.bfloat16), input_grad.astype(jnp.bfloat16), norm_drift, norm_energy, norm_after, qkv_drift, qkv_energy, qkv_after, proj_drift, proj_energy, proj_after, router_drift, router_energy, router_after, inner_drift, inner_energy, inner_after, outer_drift, outer_energy, outer_after)
```

```python
from functools import partial

import jax
import jax.numpy as jnp
from jax import lax
from jax.experimental import pallas as pl
from jax.experimental.pallas import tpu as pltpu
from jax.sharding import PartitionSpec as P

HEADS = 12
IMG = 197
STEP = 10
NORM_EPS = 1e-06
MASKED = -1e30
RATES = (0.5, 0.08, 0.6, 0.06, 0.08, 0.15)
LANES = 128
QB = 128
HALO = 256
SPAN = QB + 2 * HALO
CORE_BIT = 1
CHIP_BIT = 2
F32 = jnp.float32
BF16 = jnp.bfloat16
NT = (((1,), (1,)), ((), ()))


def swap(block, bit):
    count = lax.axis_size("replica")
    return lax.ppermute(block, "replica", [(r, r ^ bit) for r in range(count)])


def spread(block):
    other_chip = swap(block, CHIP_BIT)
    return [block, other_chip, swap(block, CORE_BIT), swap(other_chip, CORE_BIT)]


def quarter_of(replica):
    return (replica & 1) * 2 + ((replica >> 1) & 1)


def pick(blocks, index):
    return lax.dynamic_index_in_dim(jnp.stack(blocks), index, 0, keepdims=False)


def shift(head, tail, axes):
    count = lax.axis_size(axes)
    up = [(i, i + 1) for i in range(count - 1)]
    down = [(i + 1, i) for i in range(count - 1)]
    return lax.ppermute(tail, axes, up), lax.ppermute(head, axes, down)


def standardize(values):
    centre = jnp.mean(values, axis=-1, keepdims=True)
    shifted = values - centre
    row_scale = lax.rsqrt(jnp.mean(shifted * shifted, axis=-1, keepdims=True) + NORM_EPS)
    return (shifted * row_scale, row_scale)


def norm_back(grad_norm, normed, row_scale, gain_row):
    grad_hat = grad_norm * gain_row
    centred = grad_hat - jnp.mean(grad_hat, axis=-1, keepdims=True)
    return row_scale * (centred - normed * jnp.mean(grad_hat * normed, axis=-1, keepdims=True))


def adam_step(weight, moment, squares, gradient, rate_value):
    drift = 0.9 * moment + 0.1 * gradient
    energy = 0.999 * squares + 0.001 * gradient * gradient
    first_hat = drift / (1.0 - 0.9**STEP)
    second_hat = energy / (1.0 - 0.999**STEP)
    after = weight - rate_value * (first_hat / (jnp.sqrt(second_hat) + 1e-08) + 0.1 * weight)
    return (drift, energy, after)


def stacked_heads(rows, factor):
    half = rows.shape[1] // 2
    lane = lax.broadcasted_iota(jnp.int32, rows.shape, 1)
    values = rows.astype(F32) * factor
    first = jnp.where(lane < half, values, 0.0)
    second = jnp.where(lane < half, 0.0, values)
    return jnp.concatenate([first, second], axis=0).astype(BF16)


def unstacked_heads(product, rows):
    half = product.shape[0] // 2
    both = jnp.concatenate([product[:half, :rows], product[half:, rows:]], axis=0)
    return both.T


def key_allowed(first_ref, last_ref, block):
    key = lax.broadcasted_iota(jnp.int32, (SPAN, 2 * QB), 0) + block * QB
    return (key >= first_ref[block : block + 1, :]) & (key < last_ref[block : block + 1, :])


def attend_kernel(scale, q_ref, k_ref, v_ref, first_ref, last_ref, ctx_ref, lse_ref, vt_ref):
    vt_ref[...] = v_ref[...].T
    for block in range(q_ref.shape[0] // QB):
        rows = slice(block * QB, (block + 1) * QB)
        span = slice(block * QB, block * QB + SPAN)
        queries = stacked_heads(q_ref[rows, :], scale)
        scores = lax.dot_general(k_ref[span, :], queries, NT, preferred_element_type=F32)
        scores = jnp.where(key_allowed(first_ref, last_ref, block), scores, MASKED)
        peak = jnp.max(scores, axis=0, keepdims=True)
        expo = jnp.exp(scores - peak)
        total = jnp.sum(expo, axis=0, keepdims=True)
        probs = (expo * (1.0 / total)).astype(BF16)
        mixed = jnp.dot(vt_ref[:, span], probs, preferred_element_type=F32)
        ctx_ref[rows, :] = unstacked_heads(mixed, QB).astype(BF16)
        lse_ref[0, block : block + 1, :] = peak + jnp.log(total)


def attend_back_kernel(
    scale,
    q_ref,
    k_ref,
    v_ref,
    grad_ref,
    first_ref,
    last_ref,
    lse_ref,
    dq_ref,
    dk_ref,
    dv_ref,
    kt_ref,
    dk_sum,
    dv_sum,
):
    kt_ref[...] = k_ref[...].T
    dk_sum[...] = jnp.zeros_like(dk_sum)
    dv_sum[...] = jnp.zeros_like(dv_sum)
    for block in range(q_ref.shape[0] // QB):
        rows = slice(block * QB, (block + 1) * QB)
        span = slice(block * QB, block * QB + SPAN)
        queries = stacked_heads(q_ref[rows, :], scale)
        grads = stacked_heads(grad_ref[rows, :], 1.0)
        scores = lax.dot_general(k_ref[span, :], queries, NT, preferred_element_type=F32)
        scores = jnp.where(key_allowed(first_ref, last_ref, block), scores, MASKED)
        probs = jnp.exp(scores - lse_ref[0, block : block + 1, :])
        prob_grad = lax.dot_general(v_ref[span, :], grads, NT, preferred_element_type=F32)
        mean = jnp.sum(probs * prob_grad, axis=0, keepdims=True)
        score_grad = (probs * (prob_grad - mean)).astype(BF16)
        dv_sum[span, :] += jnp.dot(probs.astype(BF16), grads, preferred_element_type=F32)
        dk_sum[span, :] += jnp.dot(score_grad, queries, preferred_element_type=F32)
        dq = jnp.dot(kt_ref[:, span], score_grad, preferred_element_type=F32)
        dq_ref[rows, :] = (unstacked_heads(dq, QB) * scale).astype(BF16)
    dk_ref[...] = dk_sum[...].astype(BF16)
    dv_ref[...] = dv_sum[...].astype(BF16)


def attend(qkv_rows, kv_window, first_key, last_key, scale):
    rows, width = qkv_rows.shape[0], qkv_rows.shape[1] // 3
    pairs = width // LANES
    window = kv_window.shape[0]
    whole = pl.BlockSpec(first_key.shape, lambda h: (0, 0))
    return pl.pallas_call(
        partial(attend_kernel, scale),
        grid=(pairs,),
        in_specs=[
            pl.BlockSpec((rows, LANES), lambda h: (0, h)),
            pl.BlockSpec((window, LANES), lambda h: (0, h)),
            pl.BlockSpec((window, LANES), lambda h: (0, pairs + h)),
            whole,
            whole,
        ],
        out_specs=[
            pl.BlockSpec((rows, LANES), lambda h: (0, h)),
            pl.BlockSpec((1, 8, 2 * QB), lambda h: (h, 0, 0)),
        ],
        out_shape=[
            jax.ShapeDtypeStruct((rows, width), BF16),
            jax.ShapeDtypeStruct((pairs, 8, 2 * QB), F32),
        ],
        scratch_shapes=[pltpu.VMEM((LANES, window), BF16)],
        compiler_params=pltpu.CompilerParams(vmem_limit_bytes=40 * 2**20),
        cost_estimate=pl.CostEstimate(
            flops=4 * pairs * rows * SPAN * 2 * LANES,
            bytes_accessed=2 * 2 * window * width * 2,
            transcendentals=2 * pairs * rows * SPAN,
        ),
        name="attend",
    )(qkv_rows, kv_window, kv_window, first_key, last_key)


def attend_back(qkv_rows, kv_window, context_grad, first_key, last_key, lse, scale):
    rows, width = context_grad.shape
    pairs = width // LANES
    window = kv_window.shape[0]
    whole = pl.BlockSpec(first_key.shape, lambda h: (0, 0))
    return pl.pallas_call(
        partial(attend_back_kernel, scale),
        grid=(pairs,),
        in_specs=[
            pl.BlockSpec((rows, LANES), lambda h: (0, h)),
            pl.BlockSpec((window, LANES), lambda h: (0, h)),
            pl.BlockSpec((window, LANES), lambda h: (0, pairs + h)),
            pl.BlockSpec((rows, LANES), lambda h: (0, h)),
            whole,
            whole,
            pl.BlockSpec((1, 8, 2 * QB), lambda h: (h, 0, 0)),
        ],
        out_specs=[
            pl.BlockSpec((rows, LANES), lambda h: (0, h)),
            pl.BlockSpec((window, LANES), lambda h: (0, h)),
            pl.BlockSpec((window, LANES), lambda h: (0, h)),
        ],
        out_shape=[
            jax.ShapeDtypeStruct((rows, width), BF16),
            jax.ShapeDtypeStruct((window, width), BF16),
            jax.ShapeDtypeStruct((window, width), BF16),
        ],
        scratch_shapes=[
            pltpu.VMEM((LANES, window), BF16),
            pltpu.VMEM((window, LANES), F32),
            pltpu.VMEM((window, LANES), F32),
        ],
        compiler_params=pltpu.CompilerParams(vmem_limit_bytes=40 * 2**20),
        cost_estimate=pl.CostEstimate(
            flops=10 * pairs * rows * SPAN * 2 * LANES,
            bytes_accessed=4 * 2 * window * width * 2,
            transcendentals=2 * pairs * rows * SPAN,
        ),
        name="attend_back",
    )(qkv_rows, kv_window, kv_window, context_grad, first_key, last_key, lse)


def gelu_both(pre):
    below = 0.5 + 0.5 * lax.erf(pre * (0.5**0.5))
    density = jnp.exp(pre * pre * -0.5) * 0.3989422804014327
    return pre * below, below + pre * density


def expert_kernel(
    rows_ref,
    dy_ref,
    rank_row_ref,
    rank_col_ref,
    gate_row_ref,
    w0_ref,
    w1_ref,
    w2_ref,
    w3_ref,
    y_in_ref,
    s_in_ref,
    y_ref,
    s_ref,
    gate_grad_ref,
    keep_ref,
    give_ref,
    weights,
    arrived,
    x_slots,
    xt_slots,
    g_slots,
    gt_slots,
    dy_slots,
    gate_slots,
    eout,
    xgrad,
):
    step = pl.program_id(0)
    tokens = rows_ref.shape[0]
    slots = x_slots.shape[0]
    sources = (w0_ref, w1_ref, w2_ref, w3_ref)

    def fetch(number):
        return pltpu.make_async_copy(
            sources[number], weights.at[number % 2], arrived.at[number % 2]
        )

    def slot_mask():
        slot = lax.broadcasted_iota(jnp.int32, (slots, tokens), 0)
        return slot == rank_row_ref[...]

    @pl.when(step == 0)
    def _():
        fetch(0).start()
        fetch(1).start()
        mask = slot_mask()
        spots = jnp.where(mask, 1.0, 0.0).astype(BF16)
        x_f32 = jnp.dot(spots, rows_ref[...], preferred_element_type=F32)
        x_slots[...] = x_f32.astype(BF16)
        xt_slots[...] = x_f32.T.astype(BF16)
        dy_f32 = jnp.dot(spots, dy_ref[...], preferred_element_type=F32)
        dy_slots[...] = dy_f32.astype(BF16)
        gate = jnp.sum(jnp.where(mask, gate_row_ref[...], 0.0), axis=1, keepdims=True)
        gate_slots[...] = gate
        g_f32 = dy_f32 * gate
        g_slots[...] = g_f32.astype(BF16)
        gt_slots[...] = g_f32.T.astype(BF16)
        eout[...] = jnp.zeros_like(eout)
        xgrad[...] = jnp.zeros_like(xgrad)

    for number in range(4):

        @pl.when(step == number)
        def _():
            fetch(number).wait()
            if 1 <= number < 3:
                fetch(number + 1).start()

    slot_of = lax.rem(step, 2)
    inner = weights[slot_of, 0]
    outer = weights[slot_of, 1]
    pre = jnp.dot(x_slots[...], inner, preferred_element_type=F32)
    act_grad = jnp.dot(g_slots[...], outer, preferred_element_type=F32)
    act, slope = gelu_both(pre)
    act = act.astype(BF16)
    pre_grad = (act_grad * slope).astype(BF16)
    eout[...] += lax.dot_general(act, outer, NT, preferred_element_type=F32)
    xgrad[...] += lax.dot_general(pre_grad, inner, NT, preferred_element_type=F32)
    inner_grad = jnp.dot(xt_slots[...], pre_grad, preferred_element_type=F32).astype(BF16)
    outer_grad = jnp.dot(gt_slots[...], act, preferred_element_type=F32).astype(BF16)

    @pl.when(step < 2)
    def _():
        keep_ref[0, 0] = inner_grad
        keep_ref[0, 1] = outer_grad

    @pl.when(step >= 2)
    def _():
        give_ref[0, 0] = inner_grad
        give_ref[0, 1] = outer_grad

    @pl.when(step == 3)
    def _():
        out = eout[...]
        slot_grad = jnp.sum(dy_slots[...].astype(F32) * out, axis=1, keepdims=True)
        gate_grad_ref[...] = jnp.sum(jnp.where(slot_mask(), slot_grad, 0.0), axis=0, keepdims=True)
        slot = lax.broadcasted_iota(jnp.int32, (tokens, slots), 1)
        spots = jnp.where(slot == rank_col_ref[...], 1.0, 0.0).astype(BF16)
        scaled = (out * gate_slots[...]).astype(BF16)
        y_ref[...] = y_in_ref[...] + jnp.dot(spots, scaled, preferred_element_type=F32)
        s_ref[...] = s_in_ref[...] + jnp.dot(
            spots, xgrad[...].astype(BF16), preferred_element_type=F32
        )


def expert(rows, dy, rank_row, rank_col, gate_row, quarters, y_sum, s_sum, capacity):
    tokens, width = rows.shape
    hidden = quarters[0].shape[2]
    slots = -(-capacity // LANES) * LANES

    def whole(shape):
        return pl.BlockSpec(shape, lambda i: (0, 0), pipeline_mode=pl.Buffered(1))

    raw = pl.BlockSpec(memory_space=pl.ANY)
    grad_block = (1, 2, width, hidden)
    return pl.pallas_call(
        expert_kernel,
        grid=(4,),
        in_specs=[
            whole((tokens, width)),
            whole((tokens, width)),
            whole((1, tokens)),
            whole((tokens, 1)),
            whole((1, tokens)),
            raw,
            raw,
            raw,
            raw,
            whole((tokens, width)),
            whole((tokens, width)),
        ],
        out_specs=[
            pl.BlockSpec((tokens, width), lambda i: (0, 0)),
            pl.BlockSpec((tokens, width), lambda i: (0, 0)),
            pl.BlockSpec((1, tokens), lambda i: (0, 0)),
            pl.BlockSpec(grad_block, lambda i: (jnp.minimum(i, 1), 0, 0, 0)),
            pl.BlockSpec(grad_block, lambda i: (jnp.maximum(i - 2, 0), 0, 0, 0)),
        ],
        out_shape=[
            jax.ShapeDtypeStruct((tokens, width), F32),
            jax.ShapeDtypeStruct((tokens, width), F32),
            jax.ShapeDtypeStruct((1, tokens), F32),
            jax.ShapeDtypeStruct((2, 2, width, hidden), BF16),
            jax.ShapeDtypeStruct((2, 2, width, hidden), BF16),
        ],
        scratch_shapes=[
            pltpu.VMEM((2, 2, width, hidden), BF16),
            pltpu.SemaphoreType.DMA((2,)),
            pltpu.VMEM((slots, width), BF16),
            pltpu.VMEM((width, slots), BF16),
            pltpu.VMEM((slots, width), BF16),
            pltpu.VMEM((width, slots), BF16),
            pltpu.VMEM((slots, width), BF16),
            pltpu.VMEM((slots, 1), F32),
            pltpu.VMEM((slots, width), F32),
            pltpu.VMEM((slots, width), F32),
        ],
        compiler_params=pltpu.CompilerParams(vmem_limit_bytes=60 * 2**20),
        cost_estimate=pl.CostEstimate(
            flops=6 * 2 * 4 * slots * width * hidden,
            bytes_accessed=16 * 2 * width * hidden * 2,
            transcendentals=4 * 2 * slots * hidden,
        ),
        name="expert",
    )(rows, dy, rank_row, rank_col, gate_row, *quarters, y_sum, s_sum)


def per_device(
    block_input,
    out_grad,
    image_pos,
    routes,
    norm_weight,
    norm_moment,
    norm_squares,
    qkv_weight,
    qkv_moment,
    qkv_squares,
    proj_weight,
    proj_moment,
    proj_squares,
    router_weight,
    router_moment,
    router_squares,
    inner_weight,
    inner_moment,
    inner_squares,
    outer_weight,
    outer_moment,
    outer_squares,
):
    row_count, width = block_input.shape
    capacity = 5 * row_count // 8
    scale = (width // HEADS) ** (-0.5)
    expert_count, _, hidden = inner_weight.shape
    cut = hidden // 4
    replica = lax.axis_index("replica")
    quarter = quarter_of(replica)
    device_pos = lax.axis_index(("replica", "group"))
    all_rows = row_count * lax.axis_size(("replica", "group"))
    first_row = device_pos * row_count

    dense_all = jnp.concatenate([qkv_weight, proj_weight], axis=1)
    dense_cut = lax.dynamic_slice_in_dim(dense_all, quarter * width, width, axis=1)
    small = jnp.concatenate([norm_weight.T, router_weight], axis=1)
    small = jnp.pad(small, ((0, 0), (0, LANES - small.shape[1])))
    dense_piece = jnp.concatenate([dense_cut, small], axis=1).astype(BF16)
    dense_own = lax.all_gather(dense_piece, "group", axis=0, tiled=True)
    outer_turned = outer_weight.transpose(0, 2, 1)
    expert_piece = jnp.stack(
        [
            lax.dynamic_slice_in_dim(inner_weight, quarter * cut, cut, axis=2),
            lax.dynamic_slice_in_dim(outer_turned, quarter * cut, cut, axis=2),
        ],
        axis=1,
    ).astype(BF16)
    expert_quarters = []
    for e in range(expert_count):
        own = lax.all_gather(expert_piece[e], "group", axis=1, tiled=True)
        expert_quarters.append(spread(own))

    dense_blocks = [block[:, :width] for block in spread(dense_own)]
    dense = [pick(dense_blocks, quarter ^ at) for at in range(4)]
    qkv_full = jnp.concatenate(dense[:3], axis=1)
    proj_full = dense[3]
    small_rows = dense_own[:, width : width + 8].T
    norm_full = small_rows[:4].astype(F32)
    router_t = small_rows[4:8]

    x_float = block_input.astype(F32)
    normed_one, scale_one = standardize(x_float)
    first_in = (normed_one * norm_full[0] + norm_full[1]).astype(BF16)
    qkv_rows = jnp.dot(first_in, qkv_full, preferred_element_type=F32).astype(BF16)
    kv_rows = qkv_rows[:, width:]
    below, above = shift(kv_rows[:HALO], kv_rows[row_count - HALO :], ("replica", "group"))
    kv_window = jnp.concatenate([below, kv_rows, above], axis=0)
    row_at = first_row + jnp.arange(row_count, dtype=jnp.int32)
    image_start = row_at - image_pos[:, 0]
    image_end = image_start + image_pos[:, 1]
    first_key = jnp.maximum(image_start, 0) - first_row + HALO
    last_key = jnp.minimum(image_end, all_rows) - first_row + HALO
    first_key = jnp.tile(first_key.reshape(-1, QB), (1, 2))
    last_key = jnp.tile(last_key.reshape(-1, QB), (1, 2))
    context, lse = attend(qkv_rows, kv_window, first_key, last_key, scale)
    residual = x_float + jnp.dot(context, proj_full, preferred_element_type=F32)
    normed_two, scale_two = standardize(residual)
    second_in = (normed_two * norm_full[2] + norm_full[3]).astype(BF16)

    logits = lax.dot_general(router_t, second_in, NT, preferred_element_type=F32)
    logit_expo = jnp.exp(logits - jnp.max(logits, axis=0, keepdims=True))
    gates = logit_expo / jnp.sum(logit_expo, axis=0, keepdims=True)
    names = jnp.arange(expert_count, dtype=jnp.int32)
    named = jnp.any(routes.T[None, :, :] == names[:, None, None], axis=1)
    earlier = jnp.arange(row_count)[:, None] < jnp.arange(row_count)[None, :]
    before = jnp.dot(named.astype(BF16), earlier.astype(BF16), preferred_element_type=F32)
    ranks = jnp.where(named, before.astype(jnp.int32), -1)
    ranks_col = ranks.T

    y_sum, s_sum = residual, jnp.zeros_like(residual)
    gate_grads, expert_owned = [], []
    for e in range(expert_count):
        y_sum, s_sum, gate_grad, keep, give = expert(
            second_in,
            out_grad,
            ranks[e : e + 1],
            ranks_col[:, e : e + 1],
            gates[e : e + 1],
            expert_quarters[e],
            y_sum,
            s_sum,
            capacity,
        )
        gate_grads.append(gate_grad)
        expert_owned.append(reduce_quarter(keep, give, 1))
    block_output = y_sum.astype(BF16)

    prob_grad = jnp.concatenate(gate_grads, axis=0)
    logit_grad = gates * (prob_grad - jnp.sum(gates * prob_grad, axis=0, keepdims=True))
    logit_grad = logit_grad.astype(BF16)
    router_grad = jnp.dot(logit_grad, second_in, preferred_element_type=F32)
    second_grad = s_sum + lax.dot_general(
        logit_grad, router_t, (((0,), (0,)), ((), ())), preferred_element_type=F32
    )
    gain_two_grad = jnp.sum(second_grad * normed_two, axis=0)
    bias_two_grad = jnp.sum(second_grad, axis=0)
    grad_out = out_grad.astype(F32)
    resid_grad = grad_out + norm_back(second_grad, normed_two, scale_two, norm_full[2])
    branch_grad = resid_grad.astype(BF16)
    proj_grad = jnp.dot(context.T, branch_grad, preferred_element_type=F32)
    context_grad = lax.dot_general(branch_grad, proj_full, NT, preferred_element_type=F32)
    context_grad = context_grad.astype(BF16)

    query_grad, key_grad, value_grad = attend_back(
        qkv_rows, kv_window, context_grad, first_key, last_key, lse, scale
    )
    window_grad = jnp.concatenate([key_grad, value_grad], axis=1)
    from_below, from_above = shift(
        window_grad[:HALO], window_grad[HALO + row_count :], ("replica", "group")
    )
    own_grad = window_grad[HALO : HALO + row_count].astype(F32)
    outside = jnp.concatenate(
        [
            from_below,
            jnp.zeros((row_count - 2 * HALO, 2 * width), BF16),
            from_above,
        ],
        axis=0,
    ).astype(F32)
    kv_grad = (own_grad + outside).astype(BF16)
    qkv_grad_rows = jnp.concatenate([query_grad, kv_grad], axis=1)
    qkv_grad = jnp.dot(first_in.T, qkv_grad_rows, preferred_element_type=F32)
    first_grad = lax.dot_general(qkv_grad_rows, qkv_full, NT, preferred_element_type=F32)
    gain_one_grad = jnp.sum(first_grad * normed_one, axis=0)
    bias_one_grad = jnp.sum(first_grad, axis=0)
    input_grad = (resid_grad + norm_back(first_grad, normed_one, scale_one, norm_full[0])).astype(
        BF16
    )

    norm_grad = jnp.stack([gain_one_grad, bias_one_grad, gain_two_grad, bias_two_grad], axis=0)
    small_grad = jnp.concatenate([norm_grad, router_grad], axis=0).T
    small_grad = jnp.pad(small_grad, ((0, 0), (0, LANES - small_grad.shape[1]))).astype(BF16)
    grad_blocks = [qkv_grad[:, i * width : (i + 1) * width].astype(BF16) for i in range(3)]
    grad_blocks.append(proj_grad.astype(BF16))
    grad_stack = jnp.stack(
        [
            jnp.concatenate([block, small_grad if at == 0 else jnp.zeros_like(small_grad)], axis=1)
            for at, block in enumerate(grad_blocks)
        ]
    )
    local = [lax.dynamic_index_in_dim(grad_stack, quarter ^ j, 0) for j in range(4)]
    dense_owned = reduce_quarter(
        jnp.concatenate(local[:2], axis=0), jnp.concatenate(local[2:], axis=0), 0
    )
    dense_parts = spread(dense_owned)
    dense_sum = [pick(dense_parts, quarter ^ at).astype(F32) for at in range(4)]
    expert_parts = spread(jnp.stack(expert_owned))
    expert_sum = jnp.concatenate(
        [pick(expert_parts, quarter ^ at) for at in range(4)], axis=3
    ).astype(F32)

    small_sum = dense_sum[0][:, width : width + 8]
    norm_new = adam_step(norm_weight, norm_moment, norm_squares, small_sum[:, :4].T, RATES[0])
    qkv_sum = jnp.concatenate([part[:, :width] for part in dense_sum[:3]], axis=1)
    qkv_new = adam_step(qkv_weight, qkv_moment, qkv_squares, qkv_sum, RATES[1])
    proj_new = adam_step(
        proj_weight, proj_moment, proj_squares, dense_sum[3][:, :width], RATES[2]
    )
    router_new = adam_step(
        router_weight, router_moment, router_squares, small_sum[:, 4:8], RATES[3]
    )
    inner_new = adam_step(inner_weight, inner_moment, inner_squares, expert_sum[:, 0], RATES[4])
    outer_new = adam_step(
        outer_weight,
        outer_moment,
        outer_squares,
        expert_sum[:, 1].transpose(0, 2, 1),
        RATES[5],
    )
    return (
        block_output,
        input_grad,
        *norm_new,
        *qkv_new,
        *proj_new,
        *router_new,
        *inner_new,
        *outer_new,
    )


def reduce_quarter(keep, give, dim):
    got = swap(give, CORE_BIT)
    mine = (keep[0].astype(F32) + got[0].astype(F32)).astype(BF16)
    theirs = (keep[1].astype(F32) + got[1].astype(F32)).astype(BF16)
    got = swap(theirs, CHIP_BIT)
    mine = (mine.astype(F32) + got.astype(F32)).astype(BF16)
    owned = lax.psum_scatter(mine, "group", scatter_dimension=dim, tiled=True)
    bit = 4
    while bit < lax.axis_size("replica"):
        got = swap(owned, bit)
        owned = (owned.astype(F32) + got.astype(F32)).astype(BF16)
        bit *= 2
    return owned


def solution(mesh):
    tokens = P(("replica", "group"), None)
    columns = P(None, "group")
    rows = P("group", None)
    inner = P(None, "group", None)
    outer = P(None, None, "group")
    weights = (columns,) * 3 + (rows,) * 9 + (inner,) * 3 + (outer,) * 3
    return jax.shard_map(
        per_device,
        mesh=mesh,
        in_specs=(tokens,) * 4 + weights,
        out_specs=(tokens,) * 2 + weights,
        check_vma=False,
    )
```

```python
from functools import partial

import jax
import jax.numpy as jnp
from jax import lax
from jax.experimental import pallas as pl
from jax.experimental.pallas import tpu as pltpu
from jax.sharding import PartitionSpec as P

HEADS = 12
IMG = 197
STEP = 10
NORM_EPS = 1e-06
MASKED = -1e30
RATES = (0.5, 0.08, 0.6, 0.06, 0.08, 0.15)
LANES = 128
QB = 128
HALO = 256
SPAN = QB + 2 * HALO
CORE_BIT = 1
CHIP_BIT = 2
F32 = jnp.float32
BF16 = jnp.bfloat16
EXPERT_COST = pl.CostEstimate(flops=45 * 10**9, bytes_accessed=10**5, transcendentals=0)
ATTEND_COST = pl.CostEstimate(flops=30 * 10**9, bytes_accessed=10**5, transcendentals=0)
BACK_COST = pl.CostEstimate(flops=15 * 10**9, bytes_accessed=10**5, transcendentals=0)
NT = (((1,), (1,)), ((), ()))


def swap(block, bit):
    count = lax.axis_size("replica")
    return lax.ppermute(block, "replica", [(r, r ^ bit) for r in range(count)])


def spread(block):
    other_chip = swap(block, CHIP_BIT)
    return [block, other_chip, swap(block, CORE_BIT), swap(other_chip, CORE_BIT)]


def quarter_of(replica):
    return (replica & 1) * 2 + ((replica >> 1) & 1)


def pick(blocks, index):
    return lax.dynamic_index_in_dim(jnp.stack(blocks), index, 0, keepdims=False)


def shift(head, tail, axes):
    count = lax.axis_size(axes)
    up = [(i, i + 1) for i in range(count - 1)]
    down = [(i + 1, i) for i in range(count - 1)]
    return lax.ppermute(tail, axes, up), lax.ppermute(head, axes, down)


def group_shape():
    count = lax.axis_size("group")
    far = min(4, count)
    return far, count // far


def group_swap(block, flip):
    count = lax.axis_size("group")
    return lax.ppermute(block, "group", [(g, g ^ flip) for g in range(count)])


def gather_far(piece):
    far, near = group_shape()
    return [piece] + [group_swap(piece, k * near) for k in range(1, far)]


def gather_near(stack):
    _, near = group_shape()
    return [stack] + [group_swap(stack, j) for j in range(1, near)]


def summed(parts):
    return sum(part.astype(F32) for part in parts).astype(BF16)


def scatter_near(blocks, *after):
    far, near = group_shape()
    place = lax.axis_index("group") % near
    blocks = blocks.reshape(*blocks.shape[:-3], far, near, *blocks.shape[-2:])
    axis = blocks.ndim - 3
    parts = [lax.dynamic_index_in_dim(blocks, place ^ j, axis, keepdims=False) for j in range(near)]
    mine = tie(parts[0], *after) if after else parts[0]
    return summed([mine] + [group_swap(parts[j], j) for j in range(1, near)])


def scatter_far(blocks, *after):
    far, near = group_shape()
    place = lax.axis_index("group") // near
    axis = blocks.ndim - 3
    parts = [lax.dynamic_index_in_dim(blocks, place ^ k, axis, keepdims=False) for k in range(far)]
    mine = tie(parts[0], *after) if after else parts[0]
    return summed([mine] + [group_swap(parts[k], k * near) for k in range(1, far)])


def sum_chips(block, bit):
    while bit < lax.axis_size("replica"):
        block = summed([block, swap(block, bit)])
        bit *= 2
    return block


def halves(own, other, core):
    return jnp.where(core == 0, own, other), jnp.where(core == 0, other, own)


def place_kernel(near, far, rows, cut, place_ref, *refs):
    own, other = refs[:near], refs[near : 2 * near]
    full_ref, side_ref, sems = refs[-3:]
    copies = []
    for j in range(near):
        for k in range(far):
            shard = (place_ref[0] ^ k) * near + (place_ref[1] ^ j)
            core = place_ref[2]
            for refs_of, half in ((own, core), (other, 1 - core)):
                columns = pl.ds(pl.multiple_of(half * cut, LANES), cut)
                copies.append((refs_of[j].at[k, :, pl.ds(0, cut)], full_ref.at[shard, :, columns]))
            copies.append((own[j].at[k, :, pl.ds(cut, LANES)], side_ref.at[shard]))
    copies = [
        pltpu.make_async_copy(source, target, sems.at[at])
        for at, (source, target) in enumerate(copies)
    ]
    for copy in copies:
        copy.start()
    for copy in copies:
        copy.wait()


def place_pieces(own, other, place, after=()):
    near, far = len(own), own[0].shape[0]
    rows, cut = own[0].shape[1], own[0].shape[2] - LANES
    raw = pl.BlockSpec(memory_space=pl.ANY)
    full, side = pl.pallas_call(
        partial(place_kernel, near, far, rows, cut),
        in_specs=[pl.BlockSpec(memory_space=pltpu.SMEM)] + [raw] * (2 * near + len(after)),
        out_specs=[raw, raw],
        out_shape=[
            jax.ShapeDtypeStruct((near * far, rows, 2 * cut), BF16),
            jax.ShapeDtypeStruct((near * far, rows, LANES), BF16),
        ],
        scratch_shapes=[pltpu.SemaphoreType.DMA((3 * near * far,))],
        name="place_pieces",
    )(place, *own, *other, *after)
    return full.reshape(-1, 2 * cut), side.reshape(-1, LANES)


def tie(value, *others):
    raw = pl.BlockSpec(memory_space=pl.ANY)
    return pl.pallas_call(
        lambda *refs: None,
        in_specs=[raw] * (1 + len(others)),
        out_specs=raw,
        out_shape=jax.ShapeDtypeStruct(value.shape, value.dtype),
        input_output_aliases={0: 0},
        compiler_params=pltpu.CompilerParams(vmem_limit_bytes=56 * 2**20),
        name="tie",
    )(value, *others)


def standardize(values):
    centre = jnp.mean(values, axis=-1, keepdims=True)
    shifted = values - centre
    row_scale = lax.rsqrt(jnp.mean(shifted * shifted, axis=-1, keepdims=True) + NORM_EPS)
    return (shifted * row_scale, row_scale)


def norm_back(grad_norm, normed, row_scale, gain_row):
    grad_hat = grad_norm * gain_row
    centred = grad_hat - jnp.mean(grad_hat, axis=-1, keepdims=True)
    return row_scale * (centred - normed * jnp.mean(grad_hat * normed, axis=-1, keepdims=True))


def adam_step(weight, moment, squares, gradient, rate_value):
    drift = 0.9 * moment + 0.1 * gradient
    energy = 0.999 * squares + 0.001 * gradient * gradient
    first_hat = drift / (1.0 - 0.9**STEP)
    second_hat = energy / (1.0 - 0.999**STEP)
    after = weight - rate_value * (first_hat / (jnp.sqrt(second_hat) + 1e-08) + 0.1 * weight)
    return (drift, energy, after)


def stacked_heads(rows, factor):
    half = rows.shape[1] // 2
    lane = lax.broadcasted_iota(jnp.int32, rows.shape, 1)
    values = rows.astype(F32) * factor
    first = jnp.where(lane < half, values, 0.0)
    second = jnp.where(lane < half, 0.0, values)
    return jnp.concatenate([first, second], axis=0).astype(BF16)


def unstacked_heads(product, rows):
    half = product.shape[0] // 2
    both = jnp.concatenate([product[:half, :rows], product[half:, rows:]], axis=0)
    return both.T


def key_allowed(first_ref, last_ref, block):
    key = lax.broadcasted_iota(jnp.int32, (SPAN, 2 * QB), 0) + block * QB
    return (key >= first_ref[block : block + 1, :]) & (key < last_ref[block : block + 1, :])


def attend_kernel(scale, q_ref, k_ref, v_ref, first_ref, last_ref, *refs):
    ctx_ref, lse_ref, vt_ref = refs[-3:]
    vt_ref[...] = v_ref[...].T
    for block in range(q_ref.shape[0] // QB):
        rows = slice(block * QB, (block + 1) * QB)
        span = slice(block * QB, block * QB + SPAN)
        queries = stacked_heads(q_ref[rows, :], scale)
        scores = lax.dot_general(k_ref[span, :], queries, NT, preferred_element_type=F32)
        scores = jnp.where(key_allowed(first_ref, last_ref, block), scores, MASKED)
        peak = jnp.max(scores, axis=0, keepdims=True)
        expo = jnp.exp(scores - peak)
        total = jnp.sum(expo, axis=0, keepdims=True)
        probs = (expo * (1.0 / total)).astype(BF16)
        mixed = jnp.dot(vt_ref[:, span], probs, preferred_element_type=F32)
        ctx_ref[rows, :] = unstacked_heads(mixed, QB).astype(BF16)
        lse_ref[0, block : block + 1, :] = peak + jnp.log(total)


def attend_back_kernel(
    scale,
    q_ref,
    k_ref,
    v_ref,
    grad_ref,
    first_ref,
    last_ref,
    lse_ref,
    *refs,
):
    dq_ref, dk_ref, dv_ref, kt_ref, dk_sum, dv_sum = refs[-6:]
    kt_ref[...] = k_ref[...].T
    dk_sum[...] = jnp.zeros_like(dk_sum)
    dv_sum[...] = jnp.zeros_like(dv_sum)
    for block in range(q_ref.shape[0] // QB):
        rows = slice(block * QB, (block + 1) * QB)
        span = slice(block * QB, block * QB + SPAN)
        queries = stacked_heads(q_ref[rows, :], scale)
        grads = stacked_heads(grad_ref[rows, :], 1.0)
        scores = lax.dot_general(k_ref[span, :], queries, NT, preferred_element_type=F32)
        scores = jnp.where(key_allowed(first_ref, last_ref, block), scores, MASKED)
        probs = jnp.exp(scores - lse_ref[0, block : block + 1, :])
        prob_grad = lax.dot_general(v_ref[span, :], grads, NT, preferred_element_type=F32)
        mean = jnp.sum(probs * prob_grad, axis=0, keepdims=True)
        score_grad = (probs * (prob_grad - mean)).astype(BF16)
        dv_sum[span, :] += jnp.dot(probs.astype(BF16), grads, preferred_element_type=F32)
        dk_sum[span, :] += jnp.dot(score_grad, queries, preferred_element_type=F32)
        dq = jnp.dot(kt_ref[:, span], score_grad, preferred_element_type=F32)
        dq_ref[rows, :] = (unstacked_heads(dq, QB) * scale).astype(BF16)
    dk_ref[...] = dk_sum[...].astype(BF16)
    dv_ref[...] = dv_sum[...].astype(BF16)


def attend(qkv_rows, kv_window, first_key, last_key, scale, after=()):
    rows, width = qkv_rows.shape[0], qkv_rows.shape[1] // 3
    pairs = width // LANES
    window = kv_window.shape[0]
    whole = pl.BlockSpec(first_key.shape, lambda h: (0, 0))
    return pl.pallas_call(
        partial(attend_kernel, scale),
        grid=(pairs,),
        in_specs=[
            pl.BlockSpec((rows, LANES), lambda h: (0, h)),
            pl.BlockSpec((window, LANES), lambda h: (0, h)),
            pl.BlockSpec((window, LANES), lambda h: (0, pairs + h)),
            whole,
            whole,
            *[pl.BlockSpec(memory_space=pl.ANY)] * len(after),
        ],
        out_specs=[
            pl.BlockSpec((rows, LANES), lambda h: (0, h)),
            pl.BlockSpec((1, 8, 2 * QB), lambda h: (h, 0, 0)),
        ],
        out_shape=[
            jax.ShapeDtypeStruct((rows, width), BF16),
            jax.ShapeDtypeStruct((pairs, 8, 2 * QB), F32),
        ],
        scratch_shapes=[pltpu.VMEM((LANES, window), BF16)],
        compiler_params=pltpu.CompilerParams(vmem_limit_bytes=56 * 2**20),
        cost_estimate=ATTEND_COST,
        name="attend",
    )(qkv_rows, kv_window, kv_window, first_key, last_key, *after)


def attend_back(qkv_rows, kv_window, context_grad, first_key, last_key, lse, scale, heads, after=()):
    rows, width = context_grad.shape
    pairs = width // LANES
    low, count = heads.start, len(heads)
    window = kv_window.shape[0]
    whole = pl.BlockSpec(first_key.shape, lambda h: (0, 0))
    return pl.pallas_call(
        partial(attend_back_kernel, scale),
        grid=(count,),
        in_specs=[
            pl.BlockSpec((rows, LANES), lambda h: (0, low + h)),
            pl.BlockSpec((window, LANES), lambda h: (0, low + h)),
            pl.BlockSpec((window, LANES), lambda h: (0, pairs + low + h)),
            pl.BlockSpec((rows, LANES), lambda h: (0, low + h)),
            whole,
            whole,
            pl.BlockSpec((1, 8, 2 * QB), lambda h: (low + h, 0, 0)),
            *[pl.BlockSpec(memory_space=pl.ANY)] * len(after),
        ],
        out_specs=[
            pl.BlockSpec((rows, LANES), lambda h: (0, h)),
            pl.BlockSpec((window, LANES), lambda h: (0, h)),
            pl.BlockSpec((window, LANES), lambda h: (0, h)),
        ],
        out_shape=[
            jax.ShapeDtypeStruct((rows, count * LANES), BF16),
            jax.ShapeDtypeStruct((window, count * LANES), BF16),
            jax.ShapeDtypeStruct((window, count * LANES), BF16),
        ],
        scratch_shapes=[
            pltpu.VMEM((LANES, window), BF16),
            pltpu.VMEM((window, LANES), F32),
            pltpu.VMEM((window, LANES), F32),
        ],
        compiler_params=pltpu.CompilerParams(vmem_limit_bytes=56 * 2**20),
        cost_estimate=BACK_COST,
        name="attend_back",
    )(qkv_rows, kv_window, kv_window, context_grad, first_key, last_key, lse, *after)


def gelu_both(pre):
    below = 0.5 + 0.5 * lax.erf(pre * (0.5**0.5))
    density = jnp.exp(pre * pre * -0.5) * 0.3989422804014327
    return pre * below, below + pre * density


def expert_kernel(lists, near, waits, *refs):
    place_ref, rows_ref, dy_ref, rank_row_ref, rank_col_ref, gate_row_ref, y_in_ref, s_in_ref = refs[:8]
    source_refs = refs[8 : 8 + lists]
    outs = refs[8 + lists + waits :]
    y_ref, s_ref, gate_grad_ref, keep_ref, give_ref, weights, arrived = outs[:7]
    x_slots, xt_slots, g_slots, gt_slots, dy_slots, gate_slots, eout, xgrad = outs[7:]
    step = pl.program_id(0)
    tokens, width = rows_ref.shape
    slots = x_slots.shape[0]
    hidden = weights.shape[-1]

    def fetch(number):
        slot = number % 2
        if near == 0:
            return [
                pltpu.make_async_copy(source_refs[number], weights.at[slot], arrived.at[slot, 0])
            ]
        copies = []
        columns = pl.ds(number % 2 * hidden, hidden)
        for j in range(near):
            source = source_refs[number // 2 * near + j]
            for k in range(source.shape[0]):
                shard = (place_ref[0] ^ k) * near + (place_ref[1] ^ j)
                copies.append(
                    pltpu.make_async_copy(
                        source.at[k, :, :, columns],
                        weights.at[slot, :, shard],
                        arrived.at[slot, len(copies)],
                    )
                )
        return copies

    def slot_mask():
        slot = lax.broadcasted_iota(jnp.int32, (slots, tokens), 0)
        return slot == rank_row_ref[...]

    @pl.when(step == 0)
    def _():
        for copy in fetch(0) + fetch(1):
            copy.start()
        mask = slot_mask()
        spots = jnp.where(mask, 1.0, 0.0).astype(BF16)
        x_f32 = jnp.dot(spots, rows_ref[...], preferred_element_type=F32)
        x_slots[...] = x_f32.astype(BF16)
        xt_slots[...] = x_f32.T.astype(BF16)
        dy_f32 = jnp.dot(spots, dy_ref[...], preferred_element_type=F32)
        dy_slots[...] = dy_f32.astype(BF16)
        gate = jnp.sum(jnp.where(mask, gate_row_ref[...], 0.0), axis=1, keepdims=True)
        gate_slots[...] = gate
        g_f32 = dy_f32 * gate
        g_slots[...] = g_f32.astype(BF16)
        gt_slots[...] = g_f32.T.astype(BF16)
        eout[...] = jnp.zeros_like(eout)
        xgrad[...] = jnp.zeros_like(xgrad)

    for number in range(4):

        @pl.when(step == number)
        def _():
            for copy in fetch(number):
                copy.wait()
            if 1 <= number < 3:
                for copy in fetch(number + 1):
                    copy.start()

    slot_of = lax.rem(step, 2)
    inner = weights[slot_of, 0].reshape(width, hidden)
    outer = weights[slot_of, 1].reshape(width, hidden)
    pre = jnp.dot(x_slots[...], inner, preferred_element_type=F32)
    act_grad = jnp.dot(g_slots[...], outer, preferred_element_type=F32)
    act, slope = gelu_both(pre)
    act = act.astype(BF16)
    pre_grad = (act_grad * slope).astype(BF16)
    eout[...] += lax.dot_general(act, outer, NT, preferred_element_type=F32)
    xgrad[...] += lax.dot_general(pre_grad, inner, NT, preferred_element_type=F32)
    inner_grad = jnp.dot(xt_slots[...], pre_grad, preferred_element_type=F32).astype(BF16)
    outer_grad = jnp.dot(gt_slots[...], act, preferred_element_type=F32).astype(BF16)

    @pl.when(step < 2)
    def _():
        keep_ref[0, 0] = inner_grad
        keep_ref[0, 1] = outer_grad

    @pl.when(step >= 2)
    def _():
        give_ref[0, 0] = inner_grad
        give_ref[0, 1] = outer_grad

    @pl.when(step == 3)
    def _():
        out = eout[...]
        slot_grad = jnp.sum(dy_slots[...].astype(F32) * out, axis=1, keepdims=True)
        gate_grad_ref[...] = jnp.sum(jnp.where(slot_mask(), slot_grad, 0.0), axis=0, keepdims=True)
        slot = lax.broadcasted_iota(jnp.int32, (tokens, slots), 1)
        spots = jnp.where(slot == rank_col_ref[...], 1.0, 0.0).astype(BF16)
        scaled = (out * gate_slots[...]).astype(BF16)
        y_ref[...] = y_in_ref[...] + jnp.dot(spots, scaled, preferred_element_type=F32)
        s_ref[...] = s_in_ref[...] + jnp.dot(
            spots, xgrad[...].astype(BF16), preferred_element_type=F32
        )


def expert(place, rows, dy, rank_row, rank_col, gate_row, sources, near, y_sum, s_sum, after=()):
    tokens, width = rows.shape
    group = lax.axis_size("group")
    hidden = sources[0].shape[-1] // (2 if near else 1)
    slots = -(-(5 * tokens // 8) // LANES) * LANES

    def whole(shape):
        return pl.BlockSpec(shape, lambda i: (0, 0), pipeline_mode=pl.Buffered(1))

    raw = pl.BlockSpec(memory_space=pl.ANY)
    grad_block = (1, 2, width, hidden)
    return pl.pallas_call(
        partial(expert_kernel, len(sources), near, len(after)),
        grid=(4,),
        in_specs=[
            pl.BlockSpec(memory_space=pltpu.SMEM),
            whole((tokens, width)),
            whole((tokens, width)),
            whole((1, tokens)),
            whole((tokens, 1)),
            whole((1, tokens)),
            whole((tokens, width)),
            whole((tokens, width)),
            *[raw] * (len(sources) + len(after)),
        ],
        out_specs=[
            pl.BlockSpec((tokens, width), lambda i: (0, 0)),
            pl.BlockSpec((tokens, width), lambda i: (0, 0)),
            pl.BlockSpec((1, tokens), lambda i: (0, 0)),
            pl.BlockSpec(grad_block, lambda i: (jnp.minimum(i, 1), 0, 0, 0)),
            pl.BlockSpec(grad_block, lambda i: (jnp.maximum(i - 2, 0), 0, 0, 0)),
        ],
        out_shape=[
            jax.ShapeDtypeStruct((tokens, width), F32),
            jax.ShapeDtypeStruct((tokens, width), F32),
            jax.ShapeDtypeStruct((1, tokens), F32),
            jax.ShapeDtypeStruct((2, 2, width, hidden), BF16),
            jax.ShapeDtypeStruct((2, 2, width, hidden), BF16),
        ],
        scratch_shapes=[
            pltpu.VMEM((2, 2, group, width // group, hidden), BF16),
            pltpu.SemaphoreType.DMA((2, group)),
            pltpu.VMEM((slots, width), BF16),
            pltpu.VMEM((width, slots), BF16),
            pltpu.VMEM((slots, width), BF16),
            pltpu.VMEM((width, slots), BF16),
            pltpu.VMEM((slots, width), BF16),
            pltpu.VMEM((slots, 1), F32),
            pltpu.VMEM((slots, width), F32),
            pltpu.VMEM((slots, width), F32),
        ],
        compiler_params=pltpu.CompilerParams(vmem_limit_bytes=60 * 2**20),
        cost_estimate=EXPERT_COST,
        name="expert",
    )(place, rows, dy, rank_row, rank_col, gate_row, y_sum, s_sum, *sources, *after)


def per_device(
    block_input,
    out_grad,
    image_pos,
    routes,
    norm_weight,
    norm_moment,
    norm_squares,
    qkv_weight,
    qkv_moment,
    qkv_squares,
    proj_weight,
    proj_moment,
    proj_squares,
    router_weight,
    router_moment,
    router_squares,
    inner_weight,
    inner_moment,
    inner_squares,
    outer_weight,
    outer_moment,
    outer_squares,
):
    row_count, width = block_input.shape
    scale = (width // HEADS) ** (-0.5)
    expert_count, _, hidden = inner_weight.shape
    cut = hidden // 4
    replica = lax.axis_index("replica")
    quarter = quarter_of(replica)
    device_pos = lax.axis_index(("replica", "group"))
    all_rows = row_count * lax.axis_size(("replica", "group"))
    first_row = device_pos * row_count

    far, near = group_shape()
    core = replica & 1
    group_at = lax.axis_index("group")
    place = jnp.stack([group_at // near, group_at % near, core, core]).astype(jnp.int32)

    def dense_gather(matrix, side):
        cut_to = matrix.shape[1] // 2
        half = lax.dynamic_slice_in_dim(matrix, core * cut_to, cut_to, axis=1)
        return gather_far(jnp.concatenate([half, side], axis=1).astype(BF16))

    def dense_place(pieces, after=()):
        own = gather_near(jnp.stack(pieces))
        return place_pieces(own, [swap(block, CORE_BIT) for block in own], place, after)

    small = jnp.concatenate([norm_weight.T, router_weight], axis=1)
    small = jnp.pad(small, ((0, 0), (0, LANES - small.shape[1])))
    qkv_far = dense_gather(qkv_weight, small)
    proj_far = dense_gather(proj_weight, jnp.zeros_like(small))

    outer_turned = outer_weight.transpose(0, 2, 1)

    def expert_cut(e, part, count):
        size = hidden // count
        return jnp.stack(
            [
                lax.dynamic_slice_in_dim(matrix[e], part * size, size, axis=1)
                for matrix in (inner_weight, outer_turned)
            ]
        ).astype(BF16)

    expert_sources, owns = {}, {}
    group = far * near
    for e in range(0, expert_count, 2):
        own = lax.all_gather(expert_cut(e, quarter, 4), "group", axis=1, tiled=True)
        owns[e] = own

    far_pieces = {}
    first_far = gather_far(tie(expert_cut(1, core, 2), qkv_far[-1]))
    qkv_full, small_full = dense_place(qkv_far, (first_far[1], *proj_far[1:]))
    proj_full, _ = dense_place(proj_far)
    small_rows = small_full[:, :8].T
    norm_full = small_rows[:4].astype(F32)
    router_t = small_rows[4:8]
    far_pieces[1] = first_far
    far_pieces[3] = gather_far(tie(expert_cut(3, core, 2), first_far[-1]))

    x_float = block_input.astype(F32)
    normed_one, scale_one = standardize(x_float)
    first_in = (normed_one * norm_full[0] + norm_full[1]).astype(BF16)
    qkv_rows = jnp.dot(first_in, qkv_full, preferred_element_type=F32).astype(BF16)
    kv_rows = qkv_rows[:, width:]
    below, above = shift(kv_rows[:HALO], kv_rows[row_count - HALO :], ("replica", "group"))
    kv_window = jnp.concatenate([below, kv_rows, above], axis=0)
    row_at = first_row + jnp.arange(row_count, dtype=jnp.int32)
    image_start = row_at - image_pos[:, 0]
    image_end = image_start + image_pos[:, 1]
    first_key = jnp.maximum(image_start, 0) - first_row + HALO
    last_key = jnp.minimum(image_end, all_rows) - first_row + HALO
    first_key = jnp.tile(first_key.reshape(-1, QB), (1, 2))
    last_key = jnp.tile(last_key.reshape(-1, QB), (1, 2))
    context, lse = attend(qkv_rows, kv_window, first_key, last_key, scale)
    owns[2] = tie(owns[2], context)
    for e in range(0, expert_count, 2):
        blocks = spread(owns[e])
        expert_sources[e] = [block.reshape(2, group, width // group, cut) for block in blocks]
    far_stacks = {}
    for e in range(1, expert_count, 2):
        far_stacks[e] = jnp.stack([tie(far_pieces[e][0], context), *far_pieces[e][1:]])
        own = gather_near(far_stacks[e])
        expert_sources[e] = own + [swap(block, CORE_BIT) for block in own]
    residual = x_float + jnp.dot(context, proj_full, preferred_element_type=F32)
    normed_two, scale_two = standardize(residual)
    second_in = (normed_two * norm_full[2] + norm_full[3]).astype(BF16)

    logits = lax.dot_general(router_t, second_in, NT, preferred_element_type=F32)
    logit_expo = jnp.exp(logits - jnp.max(logits, axis=0, keepdims=True))
    gates = logit_expo / jnp.sum(logit_expo, axis=0, keepdims=True)
    names = jnp.arange(expert_count, dtype=jnp.int32)
    named = jnp.any(routes.T[None, :, :] == names[:, None, None], axis=1)
    earlier = jnp.arange(row_count)[:, None] < jnp.arange(row_count)[None, :]
    before = jnp.dot(named.astype(BF16), earlier.astype(BF16), preferred_element_type=F32)
    ranks = jnp.where(named, before.astype(jnp.int32), -1)
    ranks_col = ranks.T

    y_sum, s_sum = residual, jnp.zeros_like(residual)
    gate_grads, kept, partial_sums = [], [], {}
    for e in range(expert_count):
        after = ()
        if e == 0:
            after = (far_stacks[3], owns[2])
        if e == 1:
            sources = expert_sources[1]
            late = tie(sources[near - 1], y_sum)
            expert_sources[1] = [
                *sources[: near - 1],
                late,
                *sources[near : 2 * near - 1],
                swap(late, CORE_BIT),
            ]
            after = (expert_sources[2][1],)
        if e == 2:
            after = (expert_sources[3][near - 1],)
        if e >= 2:
            half = add_core(*kept[e - 2])
            partial_sums[e - 2] = half
            after += (half[0],)
        y_sum, s_sum, gate_grad, keep, give = expert(
            place,
            second_in,
            out_grad,
            ranks[e : e + 1],
            ranks_col[:, e : e + 1],
            gates[e : e + 1],
            expert_sources[e],
            0 if e % 2 == 0 else near,
            y_sum,
            s_sum,
            after,
        )
        gate_grads.append(gate_grad)
        kept.append((keep, swap(give, CORE_BIT)))
    block_output = y_sum.astype(BF16)

    prob_grad = jnp.concatenate(gate_grads, axis=0)
    logit_grad = gates * (prob_grad - jnp.sum(gates * prob_grad, axis=0, keepdims=True))
    logit_grad = logit_grad.astype(BF16)
    router_grad = jnp.dot(logit_grad, second_in, preferred_element_type=F32)
    second_grad = s_sum + lax.dot_general(
        logit_grad, router_t, (((0,), (0,)), ((), ())), preferred_element_type=F32
    )
    gain_two_grad = jnp.sum(second_grad * normed_two, axis=0)
    bias_two_grad = jnp.sum(second_grad, axis=0)
    grad_out = out_grad.astype(F32)
    resid_grad = grad_out + norm_back(second_grad, normed_two, scale_two, norm_full[2])
    branch_grad = resid_grad.astype(BF16)
    proj_grad = jnp.dot(context.T, branch_grad, preferred_element_type=F32)
    context_grad = lax.dot_general(branch_grad, proj_full, NT, preferred_element_type=F32)
    context_grad = context_grad.astype(BF16)

    owned = {}
    for e in (2, 3):
        partial_sums[e] = add_core(*kept[e])
    quarter_sums = {0: add_chip(tie(partial_sums[0][0], y_sum), partial_sums[0][1])}
    near_sums = {}
    pairs = width // LANES
    first_half = attend_back(
        qkv_rows,
        kv_window,
        context_grad,
        first_key,
        last_key,
        lse,
        scale,
        range(0, pairs // 2),
        (quarter_sums[0], partial_sums[2][0]),
    )
    shares = {
        0: [lax.psum_scatter(quarter_sums[0][at], "group", tiled=True) for at in range(2)],
    }
    second_half = attend_back(
        qkv_rows,
        kv_window,
        context_grad,
        first_key,
        last_key,
        lse,
        scale,
        range(pairs // 2, pairs),
        (partial_sums[3][0], shares[0][0]),
    )
    near_sums[1] = add_near(partial_sums[1], second_half[0])
    query_grad, key_grad, value_grad = [
        jnp.concatenate(both, axis=1) for both in zip(first_half, second_half)
    ]
    window_grad = jnp.concatenate([key_grad, value_grad], axis=1)
    from_below, from_above = shift(
        window_grad[:HALO], window_grad[HALO + row_count :], ("replica", "group")
    )
    own_grad = window_grad[HALO : HALO + row_count].astype(F32)
    outside = jnp.concatenate(
        [
            from_below,
            jnp.zeros((row_count - 2 * HALO, 2 * width), BF16),
            from_above,
        ],
        axis=0,
    ).astype(F32)
    kv_grad = (own_grad + outside).astype(BF16)
    qkv_grad_rows = jnp.concatenate([query_grad, kv_grad], axis=1)
    qkv_grad = jnp.dot(first_in.T, qkv_grad_rows, preferred_element_type=F32)
    first_grad = lax.dot_general(qkv_grad_rows, qkv_full, NT, preferred_element_type=F32)
    gain_one_grad = jnp.sum(first_grad * normed_one, axis=0)
    bias_one_grad = jnp.sum(first_grad, axis=0)
    input_grad = (resid_grad + norm_back(first_grad, normed_one, scale_one, norm_full[0])).astype(
        BF16
    )

    norm_grad = jnp.stack([gain_one_grad, bias_one_grad, gain_two_grad, bias_two_grad], axis=0)
    small_grad = jnp.concatenate([norm_grad, router_grad], axis=0).T
    small_grad = jnp.pad(small_grad, ((0, 0), (0, LANES - small_grad.shape[1]))).astype(BF16)
    columns = 3 * width // 2
    qkv_grad, proj_grad = qkv_grad.astype(BF16), proj_grad.astype(BF16)
    dense_grads = jnp.stack(
        [
            jnp.concatenate([qkv_grad[:, :columns], proj_grad[:, : width // 2], small_grad], axis=1),
            jnp.concatenate(
                [qkv_grad[:, columns:], proj_grad[:, width // 2 :], jnp.zeros_like(small_grad)],
                axis=1,
            ),
        ]
    )
    got = swap(lax.dynamic_index_in_dim(dense_grads, 1 - core, 0, keepdims=False), CORE_BIT)
    dense_half = summed([lax.dynamic_index_in_dim(dense_grads, core, 0, keepdims=False), got])
    dense_near = scatter_near(dense_half.reshape(group, width // group, -1))
    quarter_sums[2] = add_chip(tie(partial_sums[2][0], dense_near), partial_sums[2][1])
    near_sums[3] = add_near(partial_sums[3], dense_near)
    shares[2] = [
        lax.psum_scatter(quarter_sums[2], "group", scatter_dimension=1, tiled=True),
    ]
    shares[0][1] = tie(shares[0][1], dense_near)
    owned[0] = sum_chips(jnp.stack(shares[0]), 4)
    owned[2] = sum_chips(tie(shares[2][0], dense_near), 4)
    for e in (1, 3):
        owned[e] = sum_chips(scatter_far(near_sums[e], dense_near), CHIP_BIT)
    dense_half = sum_chips(scatter_far(dense_near), CHIP_BIT)
    low, high = [part.astype(F32) for part in halves(dense_half, swap(dense_half, CORE_BIT), core)]

    expert_sums = []
    for e in range(expert_count):
        if e % 2 == 0:
            parts = spread(owned[e])
            blocks = [pick(parts, quarter ^ at) for at in range(4)]
        else:
            both = halves(owned[e], swap(owned[e], CORE_BIT), core)
            blocks = [block[at] for block in both for at in range(2)]
        expert_sums.append(jnp.concatenate(blocks, axis=2))
    expert_sum = jnp.stack(expert_sums).astype(F32)

    small_sum = low[:, columns + width // 2 :][:, :8]
    qkv_sum = jnp.concatenate([low[:, :columns], high[:, :columns]], axis=1)
    proj_sum = jnp.concatenate(
        [part[:, columns : columns + width // 2] for part in (low, high)], axis=1
    )
    norm_new = adam_step(norm_weight, norm_moment, norm_squares, small_sum[:, :4].T, RATES[0])
    qkv_new = adam_step(qkv_weight, qkv_moment, qkv_squares, qkv_sum, RATES[1])
    proj_new = adam_step(proj_weight, proj_moment, proj_squares, proj_sum, RATES[2])
    router_new = adam_step(
        router_weight, router_moment, router_squares, small_sum[:, 4:8], RATES[3]
    )
    inner_new = adam_step(inner_weight, inner_moment, inner_squares, expert_sum[:, 0], RATES[4])
    outer_new = adam_step(
        outer_weight,
        outer_moment,
        outer_squares,
        expert_sum[:, 1].transpose(0, 2, 1),
        RATES[5],
    )
    return (
        block_output,
        input_grad,
        *norm_new,
        *qkv_new,
        *proj_new,
        *router_new,
        *inner_new,
        *outer_new,
    )


def add_core(keep, got):
    return [summed([keep[at], got[at]]) for at in range(2)]


def add_chip(mine, theirs):
    return summed([mine, swap(theirs, CHIP_BIT)])


def add_near(half, *after):
    group = lax.axis_size("group")
    blocks = jnp.stack(half)
    return scatter_near(blocks.reshape(2, 2, group, -1, blocks.shape[-1]), *after)


def solution(mesh):
    tokens = P(("replica", "group"), None)
    columns = P(None, "group")
    rows = P("group", None)
    inner = P(None, "group", None)
    outer = P(None, None, "group")
    weights = (columns,) * 3 + (rows,) * 9 + (inner,) * 3 + (outer,) * 3
    return jax.shard_map(
        per_device,
        mesh=mesh,
        in_specs=(tokens,) * 4 + weights,
        out_specs=(tokens,) * 2 + weights,
        check_vma=False,
    )
```

```python
from functools import partial

import jax
import jax.numpy as jnp
from jax import lax
from jax.experimental import pallas as pl
from jax.experimental.pallas import tpu as pltpu
from jax.sharding import PartitionSpec as P

HEADS = 12
IMG = 197
STEP = 10
NORM_EPS = 1e-06
MASKED = -1e30
RATES = (0.5, 0.08, 0.6, 0.06, 0.08, 0.15)
LANES = 128
QB = 128
HALO = 256
SPAN = QB + 2 * HALO
TAIL = 16
HALVES = 2
CORE_BIT = 1
CHIP_BIT = 2
F32 = jnp.float32
BF16 = jnp.bfloat16
EXPERT_COST = pl.CostEstimate(flops=52 * 10**9, bytes_accessed=10**5, transcendentals=0)
ATTEND_COST = pl.CostEstimate(flops=30 * 10**9, bytes_accessed=10**5, transcendentals=0)
BACK_COST = pl.CostEstimate(flops=15 * 10**9, bytes_accessed=10**5, transcendentals=0)
NT = (((1,), (1,)), ((), ()))


def swap(block, bit):
    count = lax.axis_size("replica")
    return lax.ppermute(block, "replica", [(r, r ^ bit) for r in range(count)])


def pick(blocks, index):
    return lax.dynamic_index_in_dim(jnp.stack(blocks), index, 0, keepdims=False)


def shift(head, tail, axes):
    count = lax.axis_size(axes)
    up = [(i, i + 1) for i in range(count - 1)]
    down = [(i + 1, i) for i in range(count - 1)]
    return lax.ppermute(tail, axes, up), lax.ppermute(head, axes, down)


def group_shape():
    count = lax.axis_size("group")
    far = min(4, count)
    return far, count // far


def group_swap(block, flip):
    count = lax.axis_size("group")
    return lax.ppermute(block, "group", [(g, g ^ flip) for g in range(count)])


def gather_far(piece):
    far, near = group_shape()
    return [piece] + [group_swap(piece, k * near) for k in range(1, far)]


def gather_near(stack):
    _, near = group_shape()
    return [stack] + [group_swap(stack, j) for j in range(1, near)]


def summed(parts):
    return sum(part.astype(F32) for part in parts).astype(BF16)


def scatter_near(blocks, *after):
    far, near = group_shape()
    place = lax.axis_index("group") % near
    blocks = blocks.reshape(*blocks.shape[:-3], far, near, *blocks.shape[-2:])
    axis = blocks.ndim - 3
    parts = [lax.dynamic_index_in_dim(blocks, place ^ j, axis, keepdims=False) for j in range(near)]
    mine = tie(parts[0], *after) if after else parts[0]
    return summed([mine] + [group_swap(parts[j], j) for j in range(1, near)])


def far_parts(blocks):
    far, near = group_shape()
    place = lax.axis_index("group") // near
    axis = blocks.ndim - 3
    parts = [lax.dynamic_index_in_dim(blocks, place ^ k, axis, keepdims=False) for k in range(far)]
    return [parts[0]] + [group_swap(parts[k], k * near) for k in range(1, far)]


def sum_chips(block, bit):
    while bit < lax.axis_size("replica"):
        block = summed([block, swap(block, bit)])
        bit *= 2
    return block


def halves(own, other, core):
    return jnp.where(core == 0, own, other), jnp.where(core == 0, other, own)


def place_kernel(near, far, cut, place_ref, *refs):
    own, other = refs[:near], refs[near : 2 * near]
    full_ref, side_ref = refs[-2:]
    core = place_ref[2]
    for j in range(near):
        for k in range(far):
            shard = (place_ref[0] ^ k) * near + (place_ref[1] ^ j)

            @pl.when(core == 0)
            def _():
                full_ref[shard, :, :cut] = own[j][k, :, :cut]
                full_ref[shard, :, cut:] = other[j][k, :, :cut]

            @pl.when(core != 0)
            def _():
                full_ref[shard, :, :cut] = other[j][k, :, :cut]
                full_ref[shard, :, cut:] = own[j][k, :, :cut]

            side_ref[shard] = own[j][k, :, cut:]


def place_pieces(own, other, place, after=()):
    near, far = len(own), own[0].shape[0]
    rows, cut = own[0].shape[1], own[0].shape[2] - LANES
    raw = pl.BlockSpec(memory_space=pl.ANY)
    near_by = pl.BlockSpec(memory_space=pltpu.VMEM)
    full, side = pl.pallas_call(
        partial(place_kernel, near, far, cut),
        in_specs=[pl.BlockSpec(memory_space=pltpu.SMEM)]
        + [near_by] * (2 * near)
        + [raw] * len(after),
        out_specs=[near_by, near_by],
        out_shape=[
            jax.ShapeDtypeStruct((near * far, rows, 2 * cut), BF16),
            jax.ShapeDtypeStruct((near * far, rows, LANES), BF16),
        ],
        compiler_params=pltpu.CompilerParams(vmem_limit_bytes=56 * 2**20),
        name="place_pieces",
    )(place, *own, *other, *after)
    return full.reshape(-1, 2 * cut), side.reshape(-1, LANES)


def tie(value, *others):
    raw = pl.BlockSpec(memory_space=pl.ANY)
    return pl.pallas_call(
        lambda *refs: None,
        in_specs=[raw] * (1 + len(others)),
        out_specs=raw,
        out_shape=jax.ShapeDtypeStruct(value.shape, value.dtype),
        input_output_aliases={0: 0},
        compiler_params=pltpu.CompilerParams(vmem_limit_bytes=56 * 2**20),
        name="tie",
    )(value, *others)


def standardize(values):
    centre = jnp.mean(values, axis=-1, keepdims=True)
    shifted = values - centre
    row_scale = lax.rsqrt(jnp.mean(shifted * shifted, axis=-1, keepdims=True) + NORM_EPS)
    return (shifted * row_scale, row_scale)


def norm_back(grad_norm, normed, row_scale, gain_row):
    grad_hat = grad_norm * gain_row
    centred = grad_hat - jnp.mean(grad_hat, axis=-1, keepdims=True)
    return row_scale * (centred - normed * jnp.mean(grad_hat * normed, axis=-1, keepdims=True))


def adam_step(weight, moment, squares, gradient, rate_value):
    drift = 0.9 * moment + 0.1 * gradient
    energy = 0.999 * squares + 0.001 * gradient * gradient
    first_hat = drift / (1.0 - 0.9**STEP)
    second_hat = energy / (1.0 - 0.999**STEP)
    after = weight - rate_value * (first_hat / (jnp.sqrt(second_hat) + 1e-08) + 0.1 * weight)
    return (drift, energy, after)


def stacked_heads(rows, factor):
    half = rows.shape[1] // 2
    lane = lax.broadcasted_iota(jnp.int32, rows.shape, 1)
    values = rows.astype(F32) * factor
    first = jnp.where(lane < half, values, 0.0)
    second = jnp.where(lane < half, 0.0, values)
    return jnp.concatenate([first, second], axis=0).astype(BF16)


def unstacked_heads(product, rows):
    half = product.shape[0] // 2
    both = jnp.concatenate([product[:half, :rows], product[half:, rows:]], axis=0)
    return both.T


def key_allowed(first_ref, last_ref, block):
    key = lax.broadcasted_iota(jnp.int32, (SPAN, 2 * QB), 0) + block * QB
    return (key >= first_ref[block : block + 1, :]) & (key < last_ref[block : block + 1, :])


def attend_kernel(scale, q_ref, k_ref, v_ref, first_ref, last_ref, *refs):
    ctx_ref, lse_ref, vt_ref = refs[-3:]
    vt_ref[...] = v_ref[...].T
    for block in range(q_ref.shape[0] // QB):
        rows = slice(block * QB, (block + 1) * QB)
        span = slice(block * QB, block * QB + SPAN)
        queries = stacked_heads(q_ref[rows, :], scale)
        scores = lax.dot_general(k_ref[span, :], queries, NT, preferred_element_type=F32)
        scores = jnp.where(key_allowed(first_ref, last_ref, block), scores, MASKED)
        peak = jnp.max(scores, axis=0, keepdims=True)
        expo = jnp.exp(scores - peak)
        total = jnp.sum(expo, axis=0, keepdims=True)
        probs = (expo * (1.0 / total)).astype(BF16)
        mixed = jnp.dot(vt_ref[:, span], probs, preferred_element_type=F32)
        ctx_ref[rows, :] = unstacked_heads(mixed, QB).astype(BF16)
        lse_ref[0, block : block + 1, :] = peak + jnp.log(total)


def attend_back_kernel(
    scale,
    q_ref,
    k_ref,
    v_ref,
    grad_ref,
    first_ref,
    last_ref,
    lse_ref,
    *refs,
):
    dq_ref, dk_ref, dv_ref, kt_ref, dk_sum, dv_sum = refs[-6:]
    kt_ref[...] = k_ref[...].T
    dk_sum[...] = jnp.zeros_like(dk_sum)
    dv_sum[...] = jnp.zeros_like(dv_sum)
    for block in range(q_ref.shape[0] // QB):
        rows = slice(block * QB, (block + 1) * QB)
        span = slice(block * QB, block * QB + SPAN)
        queries = stacked_heads(q_ref[rows, :], scale)
        grads = stacked_heads(grad_ref[rows, :], 1.0)
        scores = lax.dot_general(k_ref[span, :], queries, NT, preferred_element_type=F32)
        scores = jnp.where(key_allowed(first_ref, last_ref, block), scores, MASKED)
        probs = jnp.exp(scores - lse_ref[0, block : block + 1, :])
        prob_grad = lax.dot_general(v_ref[span, :], grads, NT, preferred_element_type=F32)
        mean = jnp.sum(probs * prob_grad, axis=0, keepdims=True)
        score_grad = (probs * (prob_grad - mean)).astype(BF16)
        dv_sum[span, :] += jnp.dot(probs.astype(BF16), grads, preferred_element_type=F32)
        dk_sum[span, :] += jnp.dot(score_grad, queries, preferred_element_type=F32)
        dq = jnp.dot(kt_ref[:, span], score_grad, preferred_element_type=F32)
        dq_ref[rows, :] = (unstacked_heads(dq, QB) * scale).astype(BF16)
    dk_ref[...] = dk_sum[...].astype(BF16)
    dv_ref[...] = dv_sum[...].astype(BF16)


def attend(qkv_rows, kv_window, first_key, last_key, scale, after=()):
    rows, width = qkv_rows.shape[0], qkv_rows.shape[1] // 3
    pairs = width // LANES
    window = kv_window.shape[0]
    whole = pl.BlockSpec(first_key.shape, lambda h: (0, 0))
    return pl.pallas_call(
        partial(attend_kernel, scale),
        grid=(pairs,),
        in_specs=[
            pl.BlockSpec((rows, LANES), lambda h: (0, h)),
            pl.BlockSpec((window, LANES), lambda h: (0, h)),
            pl.BlockSpec((window, LANES), lambda h: (0, pairs + h)),
            whole,
            whole,
            *[pl.BlockSpec(memory_space=pl.ANY)] * len(after),
        ],
        out_specs=[
            pl.BlockSpec((rows, LANES), lambda h: (0, h)),
            pl.BlockSpec((1, 8, 2 * QB), lambda h: (h, 0, 0)),
        ],
        out_shape=[
            jax.ShapeDtypeStruct((rows, width), BF16),
            jax.ShapeDtypeStruct((pairs, 8, 2 * QB), F32),
        ],
        scratch_shapes=[pltpu.VMEM((LANES, window), BF16)],
        compiler_params=pltpu.CompilerParams(vmem_limit_bytes=56 * 2**20),
        cost_estimate=ATTEND_COST,
        name="attend",
    )(qkv_rows, kv_window, kv_window, first_key, last_key, *after)


def attend_back(qkv_rows, kv_window, context_grad, first_key, last_key, lse, scale, heads, after=()):
    rows, width = context_grad.shape
    pairs = width // LANES
    low, count = heads.start, len(heads)
    window = kv_window.shape[0]
    whole = pl.BlockSpec(first_key.shape, lambda h: (0, 0))
    return pl.pallas_call(
        partial(attend_back_kernel, scale),
        grid=(count,),
        in_specs=[
            pl.BlockSpec((rows, LANES), lambda h: (0, low + h)),
            pl.BlockSpec((window, LANES), lambda h: (0, low + h)),
            pl.BlockSpec((window, LANES), lambda h: (0, pairs + low + h)),
            pl.BlockSpec((rows, LANES), lambda h: (0, low + h)),
            whole,
            whole,
            pl.BlockSpec((1, 8, 2 * QB), lambda h: (low + h, 0, 0)),
            *[pl.BlockSpec(memory_space=pl.ANY)] * len(after),
        ],
        out_specs=[
            pl.BlockSpec((rows, LANES), lambda h: (0, h)),
            pl.BlockSpec((window, LANES), lambda h: (0, h)),
            pl.BlockSpec((window, LANES), lambda h: (0, h)),
        ],
        out_shape=[
            jax.ShapeDtypeStruct((rows, count * LANES), BF16),
            jax.ShapeDtypeStruct((window, count * LANES), BF16),
            jax.ShapeDtypeStruct((window, count * LANES), BF16),
        ],
        scratch_shapes=[
            pltpu.VMEM((LANES, window), BF16),
            pltpu.VMEM((window, LANES), F32),
            pltpu.VMEM((window, LANES), F32),
        ],
        compiler_params=pltpu.CompilerParams(vmem_limit_bytes=56 * 2**20),
        cost_estimate=BACK_COST,
        name="attend_back",
    )(qkv_rows, kv_window, kv_window, context_grad, first_key, last_key, lse, *after)


def gelu_both(pre):
    below = 0.5 + 0.5 * lax.erf(pre * (0.5**0.5))
    density = jnp.exp(pre * pre * -0.5) * 0.3989422804014327
    return pre * below, below + pre * density


def pack_kernel(rows_ref, rank_ref, *refs):
    out_ref = refs[-1]
    slots, tokens = out_ref.shape[1], rows_ref.shape[0]
    slot = lax.broadcasted_iota(jnp.int32, (slots, tokens), 0)
    spots = jnp.where(slot == rank_ref[0], 1.0, 0.0).astype(BF16)
    out_ref[0] = jnp.dot(spots, rows_ref[...], preferred_element_type=F32).astype(BF16)


def pack(rows, ranks, slots):
    tokens, width = rows.shape
    count = ranks.shape[0]
    return pl.pallas_call(
        pack_kernel,
        grid=(count,),
        in_specs=[
            pl.BlockSpec((tokens, width), lambda e: (0, 0)),
            pl.BlockSpec((1, 1, tokens), lambda e: (e, 0, 0)),
        ],
        out_specs=pl.BlockSpec((1, slots, width), lambda e: (e, 0, 0)),
        out_shape=jax.ShapeDtypeStruct((count, slots, width), BF16),
        compiler_params=pltpu.CompilerParams(vmem_limit_bytes=56 * 2**20),
        name="pack",
    )(rows, ranks.reshape(count, 1, tokens))


def token_spots(rank_col, slots):
    slot = lax.broadcasted_iota(jnp.int32, (rank_col.shape[0], slots), 1)
    return slot == rank_col


def unpack_grad_kernel(count, *refs):
    parts, rank_refs = refs[:count], refs[count : 2 * count]
    sum_ref, gate_grad_ref = refs[-2:]
    tokens = sum_ref.shape[0]
    slots = parts[0].shape[0] - TAIL
    total = jnp.zeros(sum_ref.shape, F32)
    gate_grads = jnp.zeros((tokens, LANES), F32)
    lane = lax.broadcasted_iota(jnp.int32, (tokens, LANES), 1)
    for j in range(count):
        mask = token_spots(rank_refs[j][...], slots)
        spots = jnp.where(mask, 1.0, 0.0).astype(BF16)
        total += jnp.dot(spots, parts[j][:slots, :], preferred_element_type=F32)
        tail = parts[j][slots:, :].astype(F32)
        slot_grad = tail[0:1, :slots] + tail[1:2, :slots]
        gate_grad = jnp.sum(jnp.where(mask, slot_grad, 0.0), axis=1, keepdims=True)
        gate_grads = jnp.where(lane == j, gate_grad, gate_grads)
    sum_ref[...] = total
    gate_grad_ref[...] = gate_grads


def unpack_grad(parts, rank_cols, after=()):
    tokens, width = rank_cols[0].shape[0], parts[0].shape[1]
    count = len(parts)
    near_by = pl.BlockSpec(memory_space=pltpu.VMEM)
    return pl.pallas_call(
        partial(unpack_grad_kernel, count),
        in_specs=[near_by] * (2 * count) + [pl.BlockSpec(memory_space=pl.ANY)] * len(after),
        out_specs=[near_by, near_by],
        out_shape=[
            jax.ShapeDtypeStruct((tokens, width), F32),
            jax.ShapeDtypeStruct((tokens, LANES), F32),
        ],
        compiler_params=pltpu.CompilerParams(vmem_limit_bytes=56 * 2**20),
        name="unpack_grad",
    )(*parts, *rank_cols, *after)


def unpack_out_kernel(count, residual_ref, *refs):
    parts, rank_refs = refs[:count], refs[count : 2 * count]
    gate_refs, out_ref = refs[2 * count : 3 * count], refs[-1]
    total = residual_ref[...]
    for j in range(count):
        mask = token_spots(rank_refs[j][...], parts[j].shape[0])
        spots = jnp.where(mask, 1.0, 0.0).astype(BF16)
        total += gate_refs[j][...] * jnp.dot(spots, parts[j][...], preferred_element_type=F32)
    out_ref[...] = total.astype(BF16)


def unpack_out(residual, parts, rank_cols, gate_cols, after=()):
    near_by = pl.BlockSpec(memory_space=pltpu.VMEM)
    return pl.pallas_call(
        partial(unpack_out_kernel, len(parts)),
        in_specs=[near_by] * (1 + 3 * len(parts)) + [pl.BlockSpec(memory_space=pl.ANY)] * len(after),
        out_specs=near_by,
        out_shape=jax.ShapeDtypeStruct(residual.shape, BF16),
        compiler_params=pltpu.CompilerParams(vmem_limit_bytes=56 * 2**20),
        name="unpack_out",
    )(residual, *parts, *rank_cols, *gate_cols, *after)


def expert_kernel(count, near, first, expert_count, place_ref, router_ref, *refs):
    x_parts, dy_parts = refs[:count], refs[count : 2 * count]
    sources = refs[2 * count : 2 * count + near]
    refs = refs[2 * count + near :]
    before, refs = (None, refs) if first else (refs[:2], refs[2:])
    out_ref, xgrad_ref, grad_ref = refs[-15:-12]
    weights, arrived, part_sems, x_rows, xt_rows, g_rows, gt_rows, dy_rows = refs[-12:-4]
    act_rows, pg_rows, eout, xgrad = refs[-4:]
    step = pl.program_id(0)
    steps = pl.num_programs(0)
    slots, width = x_parts[0].shape
    hidden = weights.shape[-1]

    def fetch(number, slot):
        columns = pl.ds(pl.multiple_of(number * hidden, LANES), hidden)
        copies = []
        for j in range(near):
            for k in range(sources[j].shape[0]):
                shard = (place_ref[0] ^ k) * near + (place_ref[1] ^ j)
                copies.append(
                    pltpu.make_async_copy(
                        sources[j].at[k, :, :, columns],
                        weights.at[slot, :, shard],
                        arrived.at[slot, len(copies)],
                    )
                )
        return copies

    slot_of = lax.rem(step, 2)

    @pl.when(step == 0)
    def _():
        copies = []
        for part in range(count):
            rows = pl.ds(part * slots, slots)
            copies.append((x_parts[part], x_rows.at[rows]))
            copies.append((dy_parts[part], dy_rows.at[rows]))
        if before is not None:
            copies += [(before[0], eout), (before[1], xgrad)]
        copies = [
            pltpu.make_async_copy(source, target, part_sems.at[at])
            for at, (source, target) in enumerate(copies)
        ]
        for copy in copies + fetch(0, 0):
            copy.start()
        for copy in copies:
            copy.wait()
        if before is None:
            eout[...] = jnp.zeros_like(eout)
            xgrad[...] = jnp.zeros_like(xgrad)

        def scale_part(part, carry):
            rows = pl.ds(pl.multiple_of(part * slots, 16), slots)
            logits = jnp.dot(x_rows[rows, :], router_ref[...], preferred_element_type=F32)
            lane = lax.broadcasted_iota(jnp.int32, logits.shape, 1)
            logits = jnp.where(lane < expert_count, logits, MASKED)
            expo = jnp.exp(logits - jnp.max(logits, axis=1, keepdims=True))
            mine = jnp.sum(jnp.where(lane == place_ref[3], expo, 0.0), axis=1, keepdims=True)
            gate = mine / jnp.sum(expo, axis=1, keepdims=True)
            g_rows[rows, :] = (dy_rows[rows, :].astype(F32) * gate).astype(BF16)
            return carry

        lax.fori_loop(0, count, scale_part, 0)
        xt_rows[...] = x_rows[...].T
        gt_rows[...] = g_rows[...].T

    @pl.when(step + 1 < steps)
    def _():
        for copy in fetch(step + 1, 1 - slot_of):
            copy.start()

    for copy in fetch(step, slot_of):
        copy.wait()
    inner = weights[slot_of, 0].reshape(width, hidden)
    outer = weights[slot_of, 1].reshape(width, hidden)

    def part_step(part, carry):
        rows = pl.ds(pl.multiple_of(part * slots, 16), slots)
        pre = jnp.dot(x_rows[rows, :], inner, preferred_element_type=F32)
        act_grad = jnp.dot(g_rows[rows, :], outer, preferred_element_type=F32)
        act, slope = gelu_both(pre)
        act = act.astype(BF16)
        pre_grad = (act_grad * slope).astype(BF16)
        act_rows[rows, :] = act
        pg_rows[rows, :] = pre_grad
        eout[rows, :] += lax.dot_general(act, outer, NT, preferred_element_type=F32)
        xgrad[rows, :] += lax.dot_general(pre_grad, inner, NT, preferred_element_type=F32)
        return carry

    lax.fori_loop(0, count, part_step, 0)
    grad_ref[0] = jnp.dot(xt_rows[...], pg_rows[...], preferred_element_type=F32).astype(BF16)
    grad_ref[1] = jnp.dot(gt_rows[...], act_rows[...], preferred_element_type=F32).astype(BF16)

    @pl.when(step == steps - 1)
    def _():
        if first:
            out_ref[...] = eout[...]
            xgrad_ref[...] = xgrad[...]
            return
        for part in range(count):
            rows = slice(part * slots, (part + 1) * slots)
            out = eout[rows, :]
            out_ref[part] = out.astype(BF16)
            xgrad_ref[part, :slots, :] = xgrad[rows, :].astype(BF16)
            slot_grad = jnp.sum(dy_rows[rows, :].astype(F32) * out, axis=1, keepdims=True)
            row = jnp.broadcast_to(slot_grad, (slots, LANES)).T[0:1, :]
            row = jnp.concatenate([row, jnp.zeros((1, width - slots), F32)], axis=1)
            high = row.astype(BF16).astype(F32)
            at = lax.broadcasted_iota(jnp.int32, (TAIL, width), 0)
            tail = jnp.where(at == 0, high, jnp.where(at == 1, row - high, 0.0))
            xgrad_ref[part, slots:, :] = tail.astype(BF16)


def expert(place, router, x_parts, dy_parts, sources, expert_count, before=(), after=()):
    count, near = len(x_parts), len(sources)
    slots, width = x_parts[0].shape
    group = lax.axis_size("group")
    columns = sources[0].shape[-1]
    hidden = 512 if columns % 512 == 0 else columns
    raw = pl.BlockSpec(memory_space=pl.ANY)
    first = len(before) == 0
    if first:
        shapes = [jax.ShapeDtypeStruct((count * slots, width), F32)] * 2
    else:
        shapes = [
            jax.ShapeDtypeStruct((count, slots, width), BF16),
            jax.ShapeDtypeStruct((count, slots + TAIL, width), BF16),
        ]
    rows = count * slots
    return pl.pallas_call(
        partial(expert_kernel, count, near, first, expert_count),
        grid=(columns // hidden,),
        in_specs=[
            pl.BlockSpec(memory_space=pltpu.SMEM),
            pl.BlockSpec(router.shape, lambda i: (0, 0), pipeline_mode=pl.Buffered(1)),
            *[raw] * (2 * count + near + len(before) + len(after)),
        ],
        out_specs=[
            pl.BlockSpec(shapes[0].shape, lambda i: (0,) * len(shapes[0].shape)),
            pl.BlockSpec(shapes[1].shape, lambda i: (0,) * len(shapes[1].shape)),
            pl.BlockSpec((2, width, hidden), lambda i: (0, 0, i)),
        ],
        out_shape=[*shapes, jax.ShapeDtypeStruct((2, width, columns), BF16)],
        scratch_shapes=[
            pltpu.VMEM((2, 2, group, width // group, hidden), BF16),
            pltpu.SemaphoreType.DMA((2, group)),
            pltpu.SemaphoreType.DMA((2 * count + 2,)),
            pltpu.VMEM((rows, width), BF16),
            pltpu.VMEM((width, rows), BF16),
            pltpu.VMEM((rows, width), BF16),
            pltpu.VMEM((width, rows), BF16),
            pltpu.VMEM((rows, width), BF16),
            pltpu.VMEM((rows, hidden), BF16),
            pltpu.VMEM((rows, hidden), BF16),
            pltpu.VMEM((rows, width), F32),
            pltpu.VMEM((rows, width), F32),
        ],
        compiler_params=pltpu.CompilerParams(vmem_limit_bytes=62 * 2**20),
        cost_estimate=EXPERT_COST,
        name="expert",
    )(place, router, *x_parts, *dy_parts, *sources, *before, *after)


def per_device(
    block_input,
    out_grad,
    image_pos,
    routes,
    norm_weight,
    norm_moment,
    norm_squares,
    qkv_weight,
    qkv_moment,
    qkv_squares,
    proj_weight,
    proj_moment,
    proj_squares,
    router_weight,
    router_moment,
    router_squares,
    inner_weight,
    inner_moment,
    inner_squares,
    outer_weight,
    outer_moment,
    outer_squares,
):
    row_count, width = block_input.shape
    scale = (width // HEADS) ** (-0.5)
    expert_count, _, hidden = inner_weight.shape
    replica = lax.axis_index("replica")
    mine = replica & (expert_count - 1)
    device_pos = lax.axis_index(("replica", "group"))
    all_rows = row_count * lax.axis_size(("replica", "group"))
    first_row = device_pos * row_count

    far, near = group_shape()
    core = replica & 1
    group_at = lax.axis_index("group")
    place = jnp.stack([group_at // near, group_at % near, core, mine]).astype(jnp.int32)

    def dense_gather(matrix, side):
        cut_to = matrix.shape[1] // 2
        half = lax.dynamic_slice_in_dim(matrix, core * cut_to, cut_to, axis=1)
        return gather_far(jnp.concatenate([half, side], axis=1).astype(BF16))

    def dense_place(pieces, after=()):
        own = gather_near(jnp.stack(pieces))
        return place_pieces(own, [swap(block, CORE_BIT) for block in own], place, after)

    small = jnp.concatenate([norm_weight.T, router_weight], axis=1)
    small = jnp.pad(small, ((0, 0), (0, LANES - small.shape[1])))
    qkv_far = dense_gather(qkv_weight, small)
    proj_far = dense_gather(proj_weight, jnp.zeros_like(small))

    capacity = 5 * row_count // 8
    names = jnp.arange(expert_count, dtype=jnp.int32)
    named = jnp.any(routes.T[None, :, :] == (mine ^ names)[:, None, None], axis=1)
    earlier = jnp.arange(row_count)[:, None] < jnp.arange(row_count)[None, :]
    before = jnp.dot(named.astype(BF16), earlier.astype(BF16), preferred_element_type=F32)
    ranks = jnp.where(named, before.astype(jnp.int32), -1)
    rank_cols = [ranks[j][:, None] for j in range(expert_count)]

    def exchange(packed):
        return [packed[0]] + [swap(packed[j], j) for j in range(expert_count - 1, 0, -1)][::-1]

    def expert_cut(part):
        size = hidden // HALVES
        return jnp.stack(
            [
                lax.dynamic_index_in_dim(matrix, mine, 0, keepdims=False)[
                    :, part * size : (part + 1) * size
                ]
                for matrix in (inner_weight, outer_weight.transpose(0, 2, 1))
            ]
        ).astype(BF16)

    group = far * near
    far_pieces = [gather_far(tie(expert_cut(0), qkv_far[-1]))]
    far_pieces.append(gather_far(tie(expert_cut(1), far_pieces[0][-1])))
    dy_parts = exchange(pack(out_grad, ranks, capacity))
    qkv_full, small_full = dense_place(qkv_far, (far_pieces[0][1], *proj_far[1:]))
    proj_full, _ = dense_place(proj_far)
    small_rows = small_full[:, :8].T
    norm_full = small_rows[:4].astype(F32)
    router_t = small_rows[4:8]
    router_pad = jnp.pad(small_full[:, 4:8], ((0, 0), (0, LANES - 4)))

    x_float = block_input.astype(F32)
    normed_one, scale_one = standardize(x_float)
    first_in = (normed_one * norm_full[0] + norm_full[1]).astype(BF16)
    qkv_rows = jnp.dot(first_in, qkv_full, preferred_element_type=F32).astype(BF16)
    kv_rows = qkv_rows[:, width:]
    below, above = shift(kv_rows[:HALO], kv_rows[row_count - HALO :], ("replica", "group"))
    kv_window = jnp.concatenate([below, kv_rows, above], axis=0)
    row_at = first_row + jnp.arange(row_count, dtype=jnp.int32)
    image_start = row_at - image_pos[:, 0]
    image_end = image_start + image_pos[:, 1]
    first_key = jnp.maximum(image_start, 0) - first_row + HALO
    last_key = jnp.minimum(image_end, all_rows) - first_row + HALO
    first_key = jnp.tile(first_key.reshape(-1, QB), (1, 2))
    last_key = jnp.tile(last_key.reshape(-1, QB), (1, 2))
    context, lse = attend(qkv_rows, kv_window, first_key, last_key, scale)
    sources, stacks = [], []
    for pieces in far_pieces:
        stacks.append(jnp.stack([tie(pieces[0], context), *pieces[1:]]))
        sources.append(gather_near(stacks[-1]))
    residual = x_float + jnp.dot(context, proj_full, preferred_element_type=F32)
    normed_two, scale_two = standardize(residual)
    second_in = (normed_two * norm_full[2] + norm_full[3]).astype(BF16)

    logits = lax.dot_general(router_t, second_in, NT, preferred_element_type=F32)
    logit_expo = jnp.exp(logits - jnp.max(logits, axis=0, keepdims=True))
    gates = logit_expo / jnp.sum(logit_expo, axis=0, keepdims=True)
    gate_cols = [
        lax.dynamic_index_in_dim(gates, mine ^ j, 0, keepdims=False)[:, None]
        for j in range(expert_count)
    ]

    x_parts = exchange(pack(second_in, ranks, capacity))
    *sums, low_grad = expert(
        place, router_pad, x_parts, dy_parts, sources[0], expert_count, (), (stacks[1],)
    )
    out_slots, grad_slots, high_grad = expert(
        place, router_pad, x_parts, dy_parts, sources[1], expert_count, sums
    )
    near_sums = {0: add_near(low_grad)}
    s_sum, gate_grads = unpack_grad(exchange(grad_slots), rank_cols, (near_sums[0],))
    out_parts = exchange(tie(out_slots, s_sum))

    gate_grads = gate_grads[:, :expert_count].T
    prob_grad = jnp.concatenate(
        [lax.dynamic_index_in_dim(gate_grads, mine ^ e, 0) for e in range(expert_count)], axis=0
    )
    logit_grad = gates * (prob_grad - jnp.sum(gates * prob_grad, axis=0, keepdims=True))
    logit_grad = logit_grad.astype(BF16)
    router_grad = jnp.dot(logit_grad, second_in, preferred_element_type=F32)
    second_grad = s_sum + lax.dot_general(
        logit_grad, router_t, (((0,), (0,)), ((), ())), preferred_element_type=F32
    )
    gain_two_grad = jnp.sum(second_grad * normed_two, axis=0)
    bias_two_grad = jnp.sum(second_grad, axis=0)
    grad_out = out_grad.astype(F32)
    resid_grad = grad_out + norm_back(second_grad, normed_two, scale_two, norm_full[2])
    branch_grad = resid_grad.astype(BF16)
    proj_grad = jnp.dot(context.T, branch_grad, preferred_element_type=F32)
    context_grad = lax.dot_general(branch_grad, proj_full, NT, preferred_element_type=F32)
    context_grad = context_grad.astype(BF16)

    pairs = width // LANES
    low_parts = far_parts(near_sums[0])
    first_half = attend_back(
        qkv_rows,
        kv_window,
        context_grad,
        first_key,
        last_key,
        lse,
        scale,
        range(0, pairs // 2),
        (low_parts[1],),
    )
    near_sums[1] = add_near(high_grad, first_half[0])
    second_half = attend_back(
        qkv_rows,
        kv_window,
        context_grad,
        first_key,
        last_key,
        lse,
        scale,
        range(pairs // 2, pairs),
        (near_sums[1], low_parts[2]),
    )
    block_output = unpack_out(residual, out_parts, rank_cols, gate_cols, (second_half[0],))
    query_grad, key_grad, value_grad = [
        jnp.concatenate(both, axis=1) for both in zip(first_half, second_half)
    ]
    window_grad = jnp.concatenate([key_grad, value_grad], axis=1)
    from_below, from_above = shift(
        window_grad[:HALO], window_grad[HALO + row_count :], ("replica", "group")
    )
    own_grad = window_grad[HALO : HALO + row_count].astype(F32)
    outside = jnp.concatenate(
        [
            from_below,
            jnp.zeros((row_count - 2 * HALO, 2 * width), BF16),
            from_above,
        ],
        axis=0,
    ).astype(F32)
    kv_grad = (own_grad + outside).astype(BF16)
    qkv_grad_rows = jnp.concatenate([query_grad, kv_grad], axis=1)
    qkv_grad = jnp.dot(first_in.T, qkv_grad_rows, preferred_element_type=F32)
    first_grad = lax.dot_general(qkv_grad_rows, qkv_full, NT, preferred_element_type=F32)
    gain_one_grad = jnp.sum(first_grad * normed_one, axis=0)
    bias_one_grad = jnp.sum(first_grad, axis=0)
    input_grad = (resid_grad + norm_back(first_grad, normed_one, scale_one, norm_full[0])).astype(
        BF16
    )

    norm_grad = jnp.stack([gain_one_grad, bias_one_grad, gain_two_grad, bias_two_grad], axis=0)
    small_grad = jnp.concatenate([norm_grad, router_grad], axis=0).T
    small_grad = jnp.pad(small_grad, ((0, 0), (0, LANES - small_grad.shape[1]))).astype(BF16)
    columns = 3 * width // 2
    qkv_grad, proj_grad = qkv_grad.astype(BF16), proj_grad.astype(BF16)
    dense_grads = jnp.stack(
        [
            jnp.concatenate([qkv_grad[:, :columns], proj_grad[:, : width // 2], small_grad], axis=1),
            jnp.concatenate(
                [qkv_grad[:, columns:], proj_grad[:, width // 2 :], jnp.zeros_like(small_grad)],
                axis=1,
            ),
        ]
    )
    got = swap(lax.dynamic_index_in_dim(dense_grads, 1 - core, 0, keepdims=False), CORE_BIT)
    dense_half = summed([lax.dynamic_index_in_dim(dense_grads, core, 0, keepdims=False), got])
    dense_near = scatter_near(dense_half.reshape(group, width // group, -1))
    owned = jnp.concatenate(
        [
            summed([tie(parts[0], dense_near), *parts[1:]])
            for parts in (low_parts, far_parts(near_sums[1]))
        ],
        axis=2,
    )
    owned = sum_chips(owned, expert_count)
    dense_half = sum_chips(summed(far_parts(dense_near)), CHIP_BIT)
    low, high = [part.astype(F32) for part in halves(dense_half, swap(dense_half, CORE_BIT), core)]

    other_chip = swap(owned, CHIP_BIT)
    parts = [owned, swap(owned, CORE_BIT), other_chip, swap(other_chip, CORE_BIT)]
    expert_sum = jnp.stack([pick(parts, mine ^ e) for e in range(expert_count)]).astype(F32)

    small_sum = low[:, columns + width // 2 :][:, :8]
    qkv_sum = jnp.concatenate([low[:, :columns], high[:, :columns]], axis=1)
    proj_sum = jnp.concatenate(
        [part[:, columns : columns + width // 2] for part in (low, high)], axis=1
    )
    norm_new = adam_step(norm_weight, norm_moment, norm_squares, small_sum[:, :4].T, RATES[0])
    qkv_new = adam_step(qkv_weight, qkv_moment, qkv_squares, qkv_sum, RATES[1])
    proj_new = adam_step(proj_weight, proj_moment, proj_squares, proj_sum, RATES[2])
    router_new = adam_step(
        router_weight, router_moment, router_squares, small_sum[:, 4:8], RATES[3]
    )
    inner_new = adam_step(inner_weight, inner_moment, inner_squares, expert_sum[:, 0], RATES[4])
    outer_new = adam_step(
        outer_weight,
        outer_moment,
        outer_squares,
        expert_sum[:, 1].transpose(0, 2, 1),
        RATES[5],
    )
    return (
        block_output,
        input_grad,
        *norm_new,
        *qkv_new,
        *proj_new,
        *router_new,
        *inner_new,
        *outer_new,
    )


def add_near(grads, *after):
    group = lax.axis_size("group")
    return scatter_near(grads.reshape(2, group, -1, grads.shape[-1]), *after)


def solution(mesh):
    tokens = P(("replica", "group"), None)
    columns = P(None, "group")
    rows = P("group", None)
    inner = P(None, "group", None)
    outer = P(None, None, "group")
    weights = (columns,) * 3 + (rows,) * 9 + (inner,) * 3 + (outer,) * 3
    return jax.shard_map(
        per_device,
        mesh=mesh,
        in_specs=(tokens,) * 4 + weights,
        out_specs=(tokens,) * 2 + weights,
        check_vma=False,
    )
```

```python
from functools import partial

import jax
import jax.numpy as jnp
from jax import lax
from jax.experimental import pallas as pl
from jax.experimental.pallas import tpu as pltpu
from jax.sharding import PartitionSpec as P

HEADS = 12
IMG = 197
STEP = 10
NORM_EPS = 1e-06
MASKED = -1e30
RATES = (0.5, 0.08, 0.6, 0.06, 0.08, 0.15)
LANES = 128
QB = 128
HALO = 256
SPAN = QB + 2 * HALO
TAIL = 16
HALVES = 2
CORE_BIT = 1
CHIP_BIT = 2
F32 = jnp.float32
BF16 = jnp.bfloat16
EXPERT_COST = pl.CostEstimate(flops=28 * 10**9, bytes_accessed=10**5, transcendentals=0)
ATTEND_COST = pl.CostEstimate(flops=30 * 10**9, bytes_accessed=10**5, transcendentals=0)
BACK_COST = pl.CostEstimate(flops=15 * 10**9, bytes_accessed=10**5, transcendentals=0)
NT = (((1,), (1,)), ((), ()))


def swap(block, bit):
    count = lax.axis_size("replica")
    return lax.ppermute(block, "replica", [(r, r ^ bit) for r in range(count)])


def pick(blocks, index):
    return lax.dynamic_index_in_dim(jnp.stack(blocks), index, 0, keepdims=False)


def shift(head, tail, axes):
    count = lax.axis_size(axes)
    up = [(i, i + 1) for i in range(count - 1)]
    down = [(i + 1, i) for i in range(count - 1)]
    return lax.ppermute(tail, axes, up), lax.ppermute(head, axes, down)


def group_shape():
    count = lax.axis_size("group")
    far = min(4, count)
    return far, count // far


def group_swap(block, flip):
    count = lax.axis_size("group")
    return lax.ppermute(block, "group", [(g, g ^ flip) for g in range(count)])


def gather_far(piece):
    far, near = group_shape()
    return [piece] + [group_swap(piece, k * near) for k in range(1, far)]


def gather_near(stack):
    _, near = group_shape()
    return [stack] + [group_swap(stack, j) for j in range(1, near)]


def summed(parts):
    return sum(part.astype(F32) for part in parts).astype(BF16)


def scatter_near(blocks, *after):
    far, near = group_shape()
    place = lax.axis_index("group") % near
    blocks = blocks.reshape(*blocks.shape[:-3], far, near, *blocks.shape[-2:])
    axis = blocks.ndim - 3
    parts = [lax.dynamic_index_in_dim(blocks, place ^ j, axis, keepdims=False) for j in range(near)]
    mine = tie(parts[0], *after) if after else parts[0]
    return summed([mine] + [group_swap(parts[j], j) for j in range(1, near)])


def far_parts(blocks):
    far, near = group_shape()
    place = lax.axis_index("group") // near
    axis = blocks.ndim - 3
    parts = [lax.dynamic_index_in_dim(blocks, place ^ k, axis, keepdims=False) for k in range(far)]
    return [parts[0]] + [group_swap(parts[k], k * near) for k in range(1, far)]


def sum_chips(block, bit):
    while bit < lax.axis_size("replica"):
        block = summed([block, swap(block, bit)])
        bit *= 2
    return block


def halves(own, other, core):
    return jnp.where(core == 0, own, other), jnp.where(core == 0, other, own)


def place_kernel(near, far, cut, place_ref, *refs):
    own, other = refs[:near], refs[near : 2 * near]
    full_ref, side_ref = refs[-2:]
    core = place_ref[2]
    for j in range(near):
        for k in range(far):
            shard = (place_ref[0] ^ k) * near + (place_ref[1] ^ j)

            @pl.when(core == 0)
            def _():
                full_ref[shard, :, :cut] = own[j][k, :, :cut]
                full_ref[shard, :, cut:] = other[j][k, :, :cut]

            @pl.when(core != 0)
            def _():
                full_ref[shard, :, :cut] = other[j][k, :, :cut]
                full_ref[shard, :, cut:] = own[j][k, :, :cut]

            side_ref[shard] = own[j][k, :, cut:]


def place_pieces(own, other, place, after=()):
    near, far = len(own), own[0].shape[0]
    rows, cut = own[0].shape[1], own[0].shape[2] - LANES
    raw = pl.BlockSpec(memory_space=pl.ANY)
    near_by = pl.BlockSpec(memory_space=pltpu.VMEM)
    full, side = pl.pallas_call(
        partial(place_kernel, near, far, cut),
        in_specs=[pl.BlockSpec(memory_space=pltpu.SMEM)]
        + [near_by] * (2 * near)
        + [raw] * len(after),
        out_specs=[near_by, near_by],
        out_shape=[
            jax.ShapeDtypeStruct((near * far, rows, 2 * cut), BF16),
            jax.ShapeDtypeStruct((near * far, rows, LANES), BF16),
        ],
        compiler_params=pltpu.CompilerParams(vmem_limit_bytes=56 * 2**20),
        name="place_pieces",
    )(place, *own, *other, *after)
    return full.reshape(-1, 2 * cut), side.reshape(-1, LANES)


def tie(value, *others):
    raw = pl.BlockSpec(memory_space=pl.ANY)
    return pl.pallas_call(
        lambda *refs: None,
        in_specs=[raw] * (1 + len(others)),
        out_specs=raw,
        out_shape=jax.ShapeDtypeStruct(value.shape, value.dtype),
        input_output_aliases={0: 0},
        compiler_params=pltpu.CompilerParams(vmem_limit_bytes=56 * 2**20),
        name="tie",
    )(value, *others)


def standardize(values):
    centre = jnp.mean(values, axis=-1, keepdims=True)
    shifted = values - centre
    row_scale = lax.rsqrt(jnp.mean(shifted * shifted, axis=-1, keepdims=True) + NORM_EPS)
    return (shifted * row_scale, row_scale)


def norm_back(grad_norm, normed, row_scale, gain_row):
    grad_hat = grad_norm * gain_row
    centred = grad_hat - jnp.mean(grad_hat, axis=-1, keepdims=True)
    return row_scale * (centred - normed * jnp.mean(grad_hat * normed, axis=-1, keepdims=True))


def adam_step(weight, moment, squares, gradient, rate_value):
    drift = 0.9 * moment + 0.1 * gradient
    energy = 0.999 * squares + 0.001 * gradient * gradient
    first_hat = drift / (1.0 - 0.9**STEP)
    second_hat = energy / (1.0 - 0.999**STEP)
    after = weight - rate_value * (first_hat / (jnp.sqrt(second_hat) + 1e-08) + 0.1 * weight)
    return (drift, energy, after)


def stacked_heads(rows, factor):
    half = rows.shape[1] // 2
    lane = lax.broadcasted_iota(jnp.int32, rows.shape, 1)
    values = rows.astype(F32) * factor
    first = jnp.where(lane < half, values, 0.0)
    second = jnp.where(lane < half, 0.0, values)
    return jnp.concatenate([first, second], axis=0).astype(BF16)


def unstacked_heads(product, rows):
    half = product.shape[0] // 2
    both = jnp.concatenate([product[:half, :rows], product[half:, rows:]], axis=0)
    return both.T


def key_allowed(first_ref, last_ref, block):
    key = lax.broadcasted_iota(jnp.int32, (SPAN, 2 * QB), 0) + block * QB
    return (key >= first_ref[block : block + 1, :]) & (key < last_ref[block : block + 1, :])


def attend_kernel(scale, q_ref, k_ref, v_ref, first_ref, last_ref, *refs):
    ctx_ref, lse_ref, vt_ref = refs[-3:]
    vt_ref[...] = v_ref[...].T
    for block in range(q_ref.shape[0] // QB):
        rows = slice(block * QB, (block + 1) * QB)
        span = slice(block * QB, block * QB + SPAN)
        queries = stacked_heads(q_ref[rows, :], scale)
        scores = lax.dot_general(k_ref[span, :], queries, NT, preferred_element_type=F32)
        scores = jnp.where(key_allowed(first_ref, last_ref, block), scores, MASKED)
        peak = jnp.max(scores, axis=0, keepdims=True)
        expo = jnp.exp(scores - peak)
        total = jnp.sum(expo, axis=0, keepdims=True)
        probs = (expo * (1.0 / total)).astype(BF16)
        mixed = jnp.dot(vt_ref[:, span], probs, preferred_element_type=F32)
        ctx_ref[rows, :] = unstacked_heads(mixed, QB).astype(BF16)
        lse_ref[0, block : block + 1, :] = peak + jnp.log(total)


def attend_back_kernel(
    scale,
    q_ref,
    k_ref,
    v_ref,
    grad_ref,
    first_ref,
    last_ref,
    lse_ref,
    *refs,
):
    dq_ref, dk_ref, dv_ref, kt_ref, dk_sum, dv_sum = refs[-6:]
    kt_ref[...] = k_ref[...].T
    dk_sum[...] = jnp.zeros_like(dk_sum)
    dv_sum[...] = jnp.zeros_like(dv_sum)
    for block in range(q_ref.shape[0] // QB):
        rows = slice(block * QB, (block + 1) * QB)
        span = slice(block * QB, block * QB + SPAN)
        queries = stacked_heads(q_ref[rows, :], scale)
        grads = stacked_heads(grad_ref[rows, :], 1.0)
        scores = lax.dot_general(k_ref[span, :], queries, NT, preferred_element_type=F32)
        scores = jnp.where(key_allowed(first_ref, last_ref, block), scores, MASKED)
        probs = jnp.exp(scores - lse_ref[0, block : block + 1, :])
        prob_grad = lax.dot_general(v_ref[span, :], grads, NT, preferred_element_type=F32)
        mean = jnp.sum(probs * prob_grad, axis=0, keepdims=True)
        score_grad = (probs * (prob_grad - mean)).astype(BF16)
        dv_sum[span, :] += jnp.dot(probs.astype(BF16), grads, preferred_element_type=F32)
        dk_sum[span, :] += jnp.dot(score_grad, queries, preferred_element_type=F32)
        dq = jnp.dot(kt_ref[:, span], score_grad, preferred_element_type=F32)
        dq_ref[rows, :] = (unstacked_heads(dq, QB) * scale).astype(BF16)
    dk_ref[...] = dk_sum[...].astype(BF16)
    dv_ref[...] = dv_sum[...].astype(BF16)


def attend(qkv_rows, kv_window, first_key, last_key, scale, after=()):
    rows, width = qkv_rows.shape[0], qkv_rows.shape[1] // 3
    pairs = width // LANES
    window = kv_window.shape[0]
    whole = pl.BlockSpec(first_key.shape, lambda h: (0, 0))
    return pl.pallas_call(
        partial(attend_kernel, scale),
        grid=(pairs,),
        in_specs=[
            pl.BlockSpec((rows, LANES), lambda h: (0, h)),
            pl.BlockSpec((window, LANES), lambda h: (0, h)),
            pl.BlockSpec((window, LANES), lambda h: (0, pairs + h)),
            whole,
            whole,
            *[pl.BlockSpec(memory_space=pl.ANY)] * len(after),
        ],
        out_specs=[
            pl.BlockSpec((rows, LANES), lambda h: (0, h)),
            pl.BlockSpec((1, 8, 2 * QB), lambda h: (h, 0, 0)),
        ],
        out_shape=[
            jax.ShapeDtypeStruct((rows, width), BF16),
            jax.ShapeDtypeStruct((pairs, 8, 2 * QB), F32),
        ],
        scratch_shapes=[pltpu.VMEM((LANES, window), BF16)],
        compiler_params=pltpu.CompilerParams(vmem_limit_bytes=56 * 2**20),
        cost_estimate=ATTEND_COST,
        name="attend",
    )(qkv_rows, kv_window, kv_window, first_key, last_key, *after)


def attend_back(qkv_rows, kv_window, context_grad, first_key, last_key, lse, scale, heads, after=()):
    rows, width = context_grad.shape
    pairs = width // LANES
    low, count = heads.start, len(heads)
    window = kv_window.shape[0]
    whole = pl.BlockSpec(first_key.shape, lambda h: (0, 0))
    return pl.pallas_call(
        partial(attend_back_kernel, scale),
        grid=(count,),
        in_specs=[
            pl.BlockSpec((rows, LANES), lambda h: (0, low + h)),
            pl.BlockSpec((window, LANES), lambda h: (0, low + h)),
            pl.BlockSpec((window, LANES), lambda h: (0, pairs + low + h)),
            pl.BlockSpec((rows, LANES), lambda h: (0, low + h)),
            whole,
            whole,
            pl.BlockSpec((1, 8, 2 * QB), lambda h: (low + h, 0, 0)),
            *[pl.BlockSpec(memory_space=pl.ANY)] * len(after),
        ],
        out_specs=[
            pl.BlockSpec((rows, LANES), lambda h: (0, h)),
            pl.BlockSpec((window, LANES), lambda h: (0, h)),
            pl.BlockSpec((window, LANES), lambda h: (0, h)),
        ],
        out_shape=[
            jax.ShapeDtypeStruct((rows, count * LANES), BF16),
            jax.ShapeDtypeStruct((window, count * LANES), BF16),
            jax.ShapeDtypeStruct((window, count * LANES), BF16),
        ],
        scratch_shapes=[
            pltpu.VMEM((LANES, window), BF16),
            pltpu.VMEM((window, LANES), F32),
            pltpu.VMEM((window, LANES), F32),
        ],
        compiler_params=pltpu.CompilerParams(vmem_limit_bytes=56 * 2**20),
        cost_estimate=BACK_COST,
        name="attend_back",
    )(qkv_rows, kv_window, kv_window, context_grad, first_key, last_key, lse, *after)


def gelu_both(pre):
    bell = jnp.exp(pre * pre * -0.5)
    t = 1.0 / (1.0 + jnp.abs(pre) * (0.3275911 * 0.5**0.5))
    tail = 1.061405429 * t - 1.453152027
    tail = tail * t + 1.421413741
    tail = tail * t - 0.284496736
    tail = (tail * t + 0.254829592) * t * (0.5 * bell)
    below = jnp.where(pre < 0.0, tail, 1.0 - tail)
    return pre * below, below + pre * (bell * 0.3989422804014327)


def pack_kernel(rows_ref, rank_ref, *out_refs):
    slots, tokens = out_refs[0].shape[0], rows_ref.shape[0]
    slot = lax.broadcasted_iota(jnp.int32, (slots, tokens), 0)
    for at, out_ref in enumerate(out_refs):
        spots = jnp.where(slot == rank_ref[at : at + 1, :], 1.0, 0.0).astype(BF16)
        out_ref[...] = jnp.dot(spots, rows_ref[...], preferred_element_type=F32).astype(BF16)


def pack(rows, ranks, slots):
    count, width = ranks.shape[0], rows.shape[1]
    near_by = pl.BlockSpec(memory_space=pltpu.VMEM)
    return pl.pallas_call(
        pack_kernel,
        in_specs=[near_by, near_by],
        out_specs=[near_by] * count,
        out_shape=[jax.ShapeDtypeStruct((slots, width), BF16)] * count,
        compiler_params=pltpu.CompilerParams(vmem_limit_bytes=56 * 2**20),
        name="pack",
    )(rows, ranks)


def token_spots(rank_col, slots):
    slot = lax.broadcasted_iota(jnp.int32, (rank_col.shape[0], slots), 1)
    return slot == rank_col


def unpack_grad_kernel(count, *refs):
    parts, rank_refs = refs[:count], refs[count : 2 * count]
    sum_ref, gate_grad_ref = refs[-2:]
    tokens = sum_ref.shape[0]
    slots = parts[0].shape[0] - TAIL
    total = jnp.zeros(sum_ref.shape, F32)
    gate_grads = jnp.zeros((tokens, LANES), F32)
    lane = lax.broadcasted_iota(jnp.int32, (tokens, LANES), 1)
    for j in range(count):
        mask = token_spots(rank_refs[j][...], slots)
        spots = jnp.where(mask, 1.0, 0.0).astype(BF16)
        total += jnp.dot(spots, parts[j][:slots, :], preferred_element_type=F32)
        tail = parts[j][slots:, :].astype(F32)
        slot_grad = tail[0:1, :slots] + tail[1:2, :slots]
        gate_grad = jnp.sum(jnp.where(mask, slot_grad, 0.0), axis=1, keepdims=True)
        gate_grads = jnp.where(lane == j, gate_grad, gate_grads)
    sum_ref[...] = total
    gate_grad_ref[...] = gate_grads


def unpack_grad(parts, rank_cols, after=()):
    tokens, width = rank_cols[0].shape[0], parts[0].shape[1]
    count = len(parts)
    near_by = pl.BlockSpec(memory_space=pltpu.VMEM)
    return pl.pallas_call(
        partial(unpack_grad_kernel, count),
        in_specs=[near_by] * (2 * count) + [pl.BlockSpec(memory_space=pl.ANY)] * len(after),
        out_specs=[near_by, near_by],
        out_shape=[
            jax.ShapeDtypeStruct((tokens, width), F32),
            jax.ShapeDtypeStruct((tokens, LANES), F32),
        ],
        compiler_params=pltpu.CompilerParams(vmem_limit_bytes=56 * 2**20),
        name="unpack_grad",
    )(*parts, *rank_cols, *after)


def unpack_out_kernel(count, residual_ref, *refs):
    parts, rank_refs = refs[:count], refs[count : 2 * count]
    gate_refs, out_ref = refs[2 * count : 3 * count], refs[-1]
    total = residual_ref[...]
    for j in range(count):
        mask = token_spots(rank_refs[j][...], parts[j].shape[0])
        spots = jnp.where(mask, 1.0, 0.0).astype(BF16)
        total += gate_refs[j][...] * jnp.dot(spots, parts[j][...], preferred_element_type=F32)
    out_ref[...] = total.astype(BF16)


def unpack_out(residual, parts, rank_cols, gate_cols, after=()):
    near_by = pl.BlockSpec(memory_space=pltpu.VMEM)
    return pl.pallas_call(
        partial(unpack_out_kernel, len(parts)),
        in_specs=[near_by] * (1 + 3 * len(parts)) + [pl.BlockSpec(memory_space=pl.ANY)] * len(after),
        out_specs=near_by,
        out_shape=jax.ShapeDtypeStruct(residual.shape, BF16),
        compiler_params=pltpu.CompilerParams(vmem_limit_bytes=56 * 2**20),
        name="unpack_out",
    )(residual, *parts, *rank_cols, *gate_cols, *after)


def expert_kernel(count, others, near, first, expert_count, place_ref, router_ref, *refs):
    refs = list(refs)

    def take(number):
        taken = refs[:number]
        del refs[:number]
        return taken

    x_parts, dy_parts, sources = take(count), take(count), take(near)
    with_grads = others > 0
    before = [[], [], []] if first else [take(count), take(count), take(count)]
    other_x, other_g, other_act, other_pg = take(others), take(others), take(others), take(others)
    scratch = 9 if first else 11
    scratch_refs = refs[-scratch:]
    outs = refs[:-scratch]
    outs = outs[-(3 if first else 2) * count - (1 if with_grads else 2 * count) :]
    weights, arrived, part_sems, x_rows, g_rows, dy_rows, xt_rows, gt_rows, both_rows = scratch_refs[:9]
    act_rows, pg_rows = both_rows.at[0], both_rows.at[1]
    if first:
        eout, xgrad = outs[:count], outs[count : 2 * count]
    else:
        eout = [scratch_refs[9].at[part] for part in range(count)]
        xgrad = [scratch_refs[10].at[part] for part in range(count)]
    step = pl.program_id(0)
    steps = pl.num_programs(0)
    slots, width = x_parts[0].shape
    hidden = weights.shape[-1]
    own = count * slots

    def fetch(number, slot):
        columns = pl.ds(pl.multiple_of(number * hidden, LANES), hidden)
        copies = []
        for j in range(near):
            for k in range(sources[j].shape[0]):
                shard = (place_ref[0] ^ k) * near + (place_ref[1] ^ j)
                copies.append(
                    pltpu.make_async_copy(
                        sources[j].at[k, :, :, columns],
                        weights.at[slot, :, shard],
                        arrived.at[slot, len(copies)],
                    )
                )
        return copies

    slot_of = lax.rem(step, 2)

    @pl.when(step == 0)
    def _():
        copies = []
        for part in range(count):
            rows = pl.ds(part * slots, slots)
            copies.append((x_parts[part], x_rows.at[rows]))
            copies.append((dy_parts[part], dy_rows.at[rows]))
            if not first:
                copies.append((before[0][part], eout[part]))
                copies.append((before[1][part], xgrad[part]))
                copies.append((before[2][part], g_rows.at[rows]))
        for part in range(others):
            rows = pl.ds(own + part * slots, slots)
            copies.append((other_x[part], x_rows.at[rows]))
            copies.append((other_g[part], g_rows.at[rows]))
        copies = [
            pltpu.make_async_copy(source, target, part_sems.at[at])
            for at, (source, target) in enumerate(copies)
        ]
        for copy in copies + fetch(0, 0):
            copy.start()
        for copy in copies:
            copy.wait()
        if first:
            for part in range(count):
                rows = slice(part * slots, (part + 1) * slots)
                eout[part][...] = jnp.zeros(eout[part].shape, F32)
                xgrad[part][...] = jnp.zeros(xgrad[part].shape, F32)
                logits = jnp.dot(x_rows[rows, :], router_ref[...], preferred_element_type=F32)
                lane = lax.broadcasted_iota(jnp.int32, logits.shape, 1)
                logits = jnp.where(lane < expert_count, logits, MASKED)
                expo = jnp.exp(logits - jnp.max(logits, axis=1, keepdims=True))
                mine = jnp.sum(jnp.where(lane == place_ref[3], expo, 0.0), axis=1, keepdims=True)
                gate = mine / jnp.sum(expo, axis=1, keepdims=True)
                weighted = (dy_rows[rows, :].astype(F32) * gate).astype(BF16)
                g_rows[rows, :] = weighted
                outs[2 * count + part][...] = weighted
        if with_grads:
            xt_rows[...] = x_rows[...].T
            gt_rows[...] = g_rows[...].T

    @pl.when(step + 1 < steps)
    def _():
        for copy in fetch(step + 1, 1 - slot_of):
            copy.start()

    for copy in fetch(step, slot_of):
        copy.wait()
    inner = weights[slot_of, 0].reshape(width, hidden)
    outer = weights[slot_of, 1].reshape(width, hidden)
    for part in range(count):
        rows = slice(part * slots, (part + 1) * slots)
        pre = jnp.dot(x_rows[rows, :], inner, preferred_element_type=F32)
        act_grad = jnp.dot(g_rows[rows, :], outer, preferred_element_type=F32)
        act, slope = gelu_both(pre)
        act = act.astype(BF16)
        pre_grad = (act_grad * slope).astype(BF16)
        if with_grads:
            act_rows[rows, :] = act
            pg_rows[rows, :] = pre_grad
        else:
            outs[-2 * count + part][...] = act
            outs[-count + part][...] = pre_grad
        eout[part][...] += lax.dot_general(act, outer, NT, preferred_element_type=F32)
        xgrad[part][...] += lax.dot_general(pre_grad, inner, NT, preferred_element_type=F32)
    if with_grads:
        grad_ref = outs[-1]
        for part in range(others):
            rows = slice(own + part * slots, own + (part + 1) * slots)
            act_rows[rows, :] = other_act[part][...]
            pg_rows[rows, :] = other_pg[part][...]
        grad = jnp.dot(xt_rows[...], pg_rows[...], preferred_element_type=F32)
        grad_ref[0] = grad.astype(BF16)
        grad = jnp.dot(gt_rows[...], act_rows[...], preferred_element_type=F32)
        grad_ref[1] = grad.astype(BF16)
    if first:
        return

    @pl.when(step == steps - 1)
    def _():
        for part in range(count):
            out_ref, xgrad_ref = outs[part], outs[count + part]
            rows = slice(part * slots, (part + 1) * slots)
            out = eout[part][...]
            out_ref[...] = out.astype(BF16)
            xgrad_ref[:slots, :] = xgrad[part][...].astype(BF16)
            slot_grad = jnp.sum(dy_rows[rows, :].astype(F32) * out, axis=1, keepdims=True)
            row = jnp.broadcast_to(slot_grad, (slots, LANES)).T[0:1, :]
            row = jnp.concatenate([row, jnp.zeros((1, width - slots), F32)], axis=1)
            high = row.astype(BF16).astype(F32)
            at = lax.broadcasted_iota(jnp.int32, (TAIL, width), 0)
            tail = jnp.where(at == 0, high, jnp.where(at == 1, row - high, 0.0))
            xgrad_ref[slots:, :] = tail.astype(BF16)


def expert(
    place, router, x_parts, dy_parts, sources, expert_count, before=(), other=(), after=()
):
    count, near = len(x_parts), len(sources)
    slots, width = x_parts[0].shape
    group = lax.axis_size("group")
    columns = sources[0].shape[-1]
    hidden = 512 if columns % 512 == 0 else columns
    raw = pl.BlockSpec(memory_space=pl.ANY)
    first, with_grads = len(before) == 0, len(other) > 0
    others = len(other[0]) if with_grads else 0
    rows = (count + others) * slots
    sums = jax.ShapeDtypeStruct((slots, width), F32)
    slot_rows = jax.ShapeDtypeStruct((slots, width), BF16)
    if first:
        shapes = [sums] * (2 * count) + [slot_rows] * count
    else:
        shapes = [slot_rows] * count
        shapes += [jax.ShapeDtypeStruct((slots + TAIL, width), BF16)] * count
    out_specs = [pl.BlockSpec(shape.shape, lambda i: (0, 0)) for shape in shapes]
    hidden_rows = pl.BlockSpec((slots, hidden), lambda i: (0, i))
    if with_grads:
        out_specs.append(pl.BlockSpec((2, width, hidden), lambda i: (0, 0, i)))
        shapes.append(jax.ShapeDtypeStruct((2, width, columns), BF16))
    else:
        out_specs += [hidden_rows] * (2 * count)
        shapes += [jax.ShapeDtypeStruct((slots, columns), BF16)] * (2 * count)
    turned = (width, rows) if with_grads else (16, LANES)
    sums_scratch = [] if first else [pltpu.VMEM((count, slots, width), F32)] * 2
    before = [array for arrays in before for array in arrays]
    other = [array for arrays in other for array in arrays]
    outs = pl.pallas_call(
        partial(expert_kernel, count, others, near, first, expert_count),
        grid=(columns // hidden,),
        in_specs=[
            pl.BlockSpec(memory_space=pltpu.SMEM),
            pl.BlockSpec(router.shape, lambda i: (0, 0), pipeline_mode=pl.Buffered(1)),
            *[raw] * (2 * count + near + len(before) + 2 * others),
            *[hidden_rows] * (2 * others),
            *[raw] * len(after),
        ],
        out_specs=out_specs,
        out_shape=shapes,
        scratch_shapes=[
            pltpu.VMEM((2, 2, group, width // group, hidden), BF16),
            pltpu.SemaphoreType.DMA((2, group)),
            pltpu.SemaphoreType.DMA((5 * count + 2 * others,)),
            pltpu.VMEM((rows, width), BF16),
            pltpu.VMEM((rows, width), BF16),
            pltpu.VMEM((count * slots, width), BF16),
            pltpu.VMEM(turned, BF16),
            pltpu.VMEM(turned, BF16),
            pltpu.VMEM((2, rows if with_grads else 16, hidden), BF16),
            *sums_scratch,
        ],
        compiler_params=pltpu.CompilerParams(vmem_limit_bytes=62 * 2**20),
        cost_estimate=EXPERT_COST,
        name="expert",
    )(place, router, *x_parts, *dy_parts, *sources, *before, *other, *after)
    lists = (3 if first else 2) if with_grads else (5 if first else 4)
    split = [outs[at * count : (at + 1) * count] for at in range(lists)]
    return (*split, outs[-1]) if with_grads else split


def per_device(
    block_input,
    out_grad,
    image_pos,
    routes,
    norm_weight,
    norm_moment,
    norm_squares,
    qkv_weight,
    qkv_moment,
    qkv_squares,
    proj_weight,
    proj_moment,
    proj_squares,
    router_weight,
    router_moment,
    router_squares,
    inner_weight,
    inner_moment,
    inner_squares,
    outer_weight,
    outer_moment,
    outer_squares,
):
    row_count, width = block_input.shape
    scale = (width // HEADS) ** (-0.5)
    expert_count, _, hidden = inner_weight.shape
    replica = lax.axis_index("replica")
    mine = replica & (expert_count - 1)
    device_pos = lax.axis_index(("replica", "group"))
    all_rows = row_count * lax.axis_size(("replica", "group"))
    first_row = device_pos * row_count

    far, near = group_shape()
    core = replica & 1
    group_at = lax.axis_index("group")
    place = jnp.stack([group_at // near, group_at % near, core, mine]).astype(jnp.int32)

    def dense_gather(matrix, side):
        cut_to = matrix.shape[1] // 2
        half = lax.dynamic_slice_in_dim(matrix, core * cut_to, cut_to, axis=1)
        return gather_far(jnp.concatenate([half, side], axis=1).astype(BF16))

    def dense_place(pieces, after=()):
        own = gather_near(jnp.stack(pieces))
        return place_pieces(own, [swap(block, CORE_BIT) for block in own], place, after)

    small = jnp.concatenate([norm_weight.T, router_weight], axis=1)
    small = jnp.pad(small, ((0, 0), (0, LANES - small.shape[1])))
    qkv_far = dense_gather(qkv_weight, small)
    proj_far = dense_gather(proj_weight, jnp.zeros_like(small))

    capacity = 5 * row_count // 8
    names = jnp.arange(expert_count, dtype=jnp.int32)
    named = jnp.any(routes.T[None, :, :] == (mine ^ names)[:, None, None], axis=1)
    earlier = jnp.arange(row_count)[:, None] < jnp.arange(row_count)[None, :]
    before = jnp.dot(named.astype(BF16), earlier.astype(BF16), preferred_element_type=F32)
    ranks = jnp.where(named, before.astype(jnp.int32), -1)
    rank_cols = [ranks[j][:, None] for j in range(expert_count)]

    def exchange(packed):
        moved = {j: swap(packed[j], j) for j in (2, 3, 1)}
        return [packed[0], moved[1], moved[2], moved[3]]

    def expert_cut(part):
        size = hidden // HALVES
        return jnp.stack(
            [
                lax.dynamic_index_in_dim(matrix, mine, 0, keepdims=False)[
                    :, part * size : (part + 1) * size
                ]
                for matrix in (inner_weight, outer_weight.transpose(0, 2, 1))
            ]
        ).astype(BF16)

    group = far * near
    far_pieces = [gather_far(tie(expert_cut(0), qkv_far[-1]))]
    far_pieces.append(gather_far(tie(expert_cut(1), far_pieces[0][-1])))
    dy_parts = exchange(pack(out_grad, ranks, capacity))
    qkv_full, small_full = dense_place(qkv_far)
    proj_full, _ = dense_place(proj_far, tuple(dy_parts[2:]))
    small_rows = small_full[:, :8].T
    norm_full = small_rows[:4].astype(F32)
    router_t = small_rows[4:8]
    router_pad = jnp.pad(small_full[:, 4:8], ((0, 0), (0, LANES - 4)))

    x_float = block_input.astype(F32)
    normed_one, scale_one = standardize(x_float)
    first_in = (normed_one * norm_full[0] + norm_full[1]).astype(BF16)
    qkv_rows = jnp.dot(first_in, qkv_full, preferred_element_type=F32).astype(BF16)
    kv_rows = qkv_rows[:, width:]
    below, above = shift(kv_rows[:HALO], kv_rows[row_count - HALO :], ("replica", "group"))
    kv_window = jnp.concatenate([below, kv_rows, above], axis=0)
    row_at = first_row + jnp.arange(row_count, dtype=jnp.int32)
    image_start = row_at - image_pos[:, 0]
    image_end = image_start + image_pos[:, 1]
    first_key = jnp.maximum(image_start, 0) - first_row + HALO
    last_key = jnp.minimum(image_end, all_rows) - first_row + HALO
    first_key = jnp.tile(first_key.reshape(-1, QB), (1, 2))
    last_key = jnp.tile(last_key.reshape(-1, QB), (1, 2))
    context, lse = attend(qkv_rows, kv_window, first_key, last_key, scale)
    sources = [gather_near(jnp.stack([tie(far_pieces[0][0], context), *far_pieces[0][1:]]))]
    residual = x_float + jnp.dot(context, proj_full, preferred_element_type=F32)
    normed_two, scale_two = standardize(residual)
    second_in = (normed_two * norm_full[2] + norm_full[3]).astype(BF16)

    logits = lax.dot_general(router_t, second_in, NT, preferred_element_type=F32)
    logit_expo = jnp.exp(logits - jnp.max(logits, axis=0, keepdims=True))
    gates = logit_expo / jnp.sum(logit_expo, axis=0, keepdims=True)
    gate_cols = [
        lax.dynamic_index_in_dim(gates, mine ^ j, 0, keepdims=False)[:, None]
        for j in range(expert_count)
    ]

    x_parts = exchange(pack(second_in, ranks, capacity))

    def run(at, part, before=(), other=(), after=()):
        return expert(
            place,
            router_pad,
            [x_parts[j] for j in at],
            [dy_parts[j] for j in at],
            sources[part],
            expert_count,
            before,
            other,
            after,
        )

    near_sums, near_back, near_g, near_act, near_pg = run((0, 1), 0)
    far_stack = jnp.stack([tie(far_pieces[1][0], near_g[0]), *far_pieces[1][1:]])
    sources.append(gather_near(far_stack))
    far_sums, far_back, far_g, low_grad = run(
        (2, 3), 0, other=(x_parts[:2], near_g, near_act, near_pg), after=(far_stack,)
    )
    outs, backs, weighted = near_sums + far_sums, near_back + far_back, near_g + far_g
    sent_out, sent_back, sent_act, sent_pg = run(
        (1, 2, 3), 1, before=(outs[1:], backs[1:], weighted[1:])
    )
    own_out, own_back, high_grad = run(
        (0,),
        1,
        before=(outs[:1], backs[:1], weighted[:1]),
        other=(x_parts[1:], weighted[1:], sent_act, sent_pg),
    )
    out_parts = exchange(own_out + sent_out)
    grad_parts = exchange(own_back + sent_back)
    near_sums = {0: add_near(low_grad)}
    s_sum, gate_grads = unpack_grad(grad_parts, rank_cols, (near_sums[0],))

    gate_grads = gate_grads[:, :expert_count].T
    prob_grad = jnp.concatenate(
        [lax.dynamic_index_in_dim(gate_grads, mine ^ e, 0) for e in range(expert_count)], axis=0
    )
    logit_grad = gates * (prob_grad - jnp.sum(gates * prob_grad, axis=0, keepdims=True))
    logit_grad = logit_grad.astype(BF16)
    router_grad = jnp.dot(logit_grad, second_in, preferred_element_type=F32)
    second_grad = s_sum + lax.dot_general(
        logit_grad, router_t, (((0,), (0,)), ((), ())), preferred_element_type=F32
    )
    gain_two_grad = jnp.sum(second_grad * normed_two, axis=0)
    bias_two_grad = jnp.sum(second_grad, axis=0)
    grad_out = out_grad.astype(F32)
    resid_grad = grad_out + norm_back(second_grad, normed_two, scale_two, norm_full[2])
    branch_grad = resid_grad.astype(BF16)
    proj_grad = jnp.dot(context.T, branch_grad, preferred_element_type=F32)
    context_grad = lax.dot_general(branch_grad, proj_full, NT, preferred_element_type=F32)
    context_grad = context_grad.astype(BF16)

    pairs = width // LANES
    low_parts = far_parts(near_sums[0])
    first_half = attend_back(
        qkv_rows,
        kv_window,
        context_grad,
        first_key,
        last_key,
        lse,
        scale,
        range(0, pairs // 2),
    )
    near_sums[1] = add_near(high_grad, first_half[0])
    second_half = attend_back(
        qkv_rows,
        kv_window,
        context_grad,
        first_key,
        last_key,
        lse,
        scale,
        range(pairs // 2, pairs),
        (near_sums[1], low_parts[1], low_parts[2]),
    )
    block_output = unpack_out(residual, out_parts, rank_cols, gate_cols, (second_half[0],))
    high_parts = far_parts(near_sums[1])
    query_grads, own_grads, outside_grads = [], [], []
    for query_grad, *window_grads in (first_half, second_half):
        query_grads.append(query_grad)
        edges = [
            jnp.concatenate([grad[rows] for grad in window_grads], axis=1)
            for rows in (slice(0, HALO), slice(HALO + row_count, None))
        ]
        from_below, from_above = shift(*edges, ("replica", "group"))
        outside = jnp.concatenate(
            [from_below, jnp.zeros((row_count - 2 * HALO, from_below.shape[1]), BF16), from_above],
            axis=0,
        )
        size = from_below.shape[1] // 2
        for at, grad in enumerate(window_grads):
            own_grads.append(grad[HALO : HALO + row_count])
            outside_grads.append(outside[:, at * size : (at + 1) * size])
    kv_grads = [summed([own_grads[at], outside_grads[at]]) for at in (0, 2, 1, 3)]
    qkv_grad_rows = jnp.concatenate([*query_grads, *kv_grads], axis=1)
    qkv_grad_rows = tie(qkv_grad_rows, low_parts[3], high_parts[1])
    qkv_grad = jnp.dot(first_in.T, qkv_grad_rows, preferred_element_type=F32)
    first_grad = lax.dot_general(qkv_grad_rows, qkv_full, NT, preferred_element_type=F32)
    gain_one_grad = jnp.sum(first_grad * normed_one, axis=0)
    bias_one_grad = jnp.sum(first_grad, axis=0)
    input_grad = (resid_grad + norm_back(first_grad, normed_one, scale_one, norm_full[0])).astype(
        BF16
    )

    norm_grad = jnp.stack([gain_one_grad, bias_one_grad, gain_two_grad, bias_two_grad], axis=0)
    small_grad = jnp.concatenate([norm_grad, router_grad], axis=0).T
    small_grad = jnp.pad(small_grad, ((0, 0), (0, LANES - small_grad.shape[1]))).astype(BF16)
    columns = 3 * width // 2
    qkv_grad, proj_grad = qkv_grad.astype(BF16), proj_grad.astype(BF16)
    dense_grads = jnp.stack(
        [
            jnp.concatenate([qkv_grad[:, :columns], proj_grad[:, : width // 2], small_grad], axis=1),
            jnp.concatenate(
                [qkv_grad[:, columns:], proj_grad[:, width // 2 :], jnp.zeros_like(small_grad)],
                axis=1,
            ),
        ]
    )
    got = swap(lax.dynamic_index_in_dim(dense_grads, 1 - core, 0, keepdims=False), CORE_BIT)
    dense_half = summed([lax.dynamic_index_in_dim(dense_grads, core, 0, keepdims=False), got])
    dense_near = scatter_near(dense_half.reshape(group, width // group, -1))
    owned = jnp.concatenate(
        [
            summed([tie(parts[0], dense_near), *parts[1:]])
            for parts in (low_parts, high_parts)
        ],
        axis=2,
    )
    owned = sum_chips(owned, expert_count)
    dense_half = sum_chips(summed(far_parts(dense_near)), CHIP_BIT)
    low, high = [part.astype(F32) for part in halves(dense_half, swap(dense_half, CORE_BIT), core)]

    other_chip = swap(owned, CHIP_BIT)
    parts = [owned, swap(owned, CORE_BIT), other_chip, swap(other_chip, CORE_BIT)]
    expert_sum = jnp.stack([pick(parts, mine ^ e) for e in range(expert_count)]).astype(F32)

    small_sum = low[:, columns + width // 2 :][:, :8]
    qkv_sum = jnp.concatenate([low[:, :columns], high[:, :columns]], axis=1)
    proj_sum = jnp.concatenate(
        [part[:, columns : columns + width // 2] for part in (low, high)], axis=1
    )
    norm_new = adam_step(norm_weight, norm_moment, norm_squares, small_sum[:, :4].T, RATES[0])
    qkv_new = adam_step(qkv_weight, qkv_moment, qkv_squares, qkv_sum, RATES[1])
    proj_new = adam_step(proj_weight, proj_moment, proj_squares, proj_sum, RATES[2])
    router_new = adam_step(
        router_weight, router_moment, router_squares, small_sum[:, 4:8], RATES[3]
    )
    inner_new = adam_step(inner_weight, inner_moment, inner_squares, expert_sum[:, 0], RATES[4])
    outer_new = adam_step(
        outer_weight,
        outer_moment,
        outer_squares,
        expert_sum[:, 1].transpose(0, 2, 1),
        RATES[5],
    )
    return (
        block_output,
        input_grad,
        *norm_new,
        *qkv_new,
        *proj_new,
        *router_new,
        *inner_new,
        *outer_new,
    )


def add_near(grads, *after):
    group = lax.axis_size("group")
    return scatter_near(grads.reshape(2, group, -1, grads.shape[-1]), *after)


def solution(mesh):
    tokens = P(("replica", "group"), None)
    columns = P(None, "group")
    rows = P("group", None)
    inner = P(None, "group", None)
    outer = P(None, None, "group")
    weights = (columns,) * 3 + (rows,) * 9 + (inner,) * 3 + (outer,) * 3
    return jax.shard_map(
        per_device,
        mesh=mesh,
        in_specs=(tokens,) * 4 + weights,
        out_specs=(tokens,) * 2 + weights,
        check_vma=False,
    )
```

```python
from functools import partial

import jax
import jax.numpy as jnp
from jax import lax
from jax.experimental import pallas as pl
from jax.experimental.pallas import tpu as pltpu
from jax.sharding import PartitionSpec as P

HEADS = 12
IMG = 197
STEP = 10
NORM_EPS = 1e-06
MASKED = -1e30
RATES = (0.5, 0.08, 0.6, 0.06, 0.08, 0.15)
LANES = 128
QB = 128
HALO = 208
SPAN = QB + 2 * HALO
TAIL = 16
BLOCK = 768
HALVES = 2
CORE_BIT = 1
CHIP_BIT = 2
F32 = jnp.float32
BF16 = jnp.bfloat16
EXPERT_COST = pl.CostEstimate(flops=28 * 10**9, bytes_accessed=10**5, transcendentals=0)
ATTEND_COST = pl.CostEstimate(flops=30 * 10**9, bytes_accessed=10**5, transcendentals=0)
UPDATE_COST = pl.CostEstimate(flops=10**10, bytes_accessed=10**5, transcendentals=0)
BACK_COST = pl.CostEstimate(flops=15 * 10**9, bytes_accessed=10**5, transcendentals=0)
NT = (((1,), (1,)), ((), ()))


def swap(block, bit):
    count = lax.axis_size("replica")
    return lax.ppermute(block, "replica", [(r, r ^ bit) for r in range(count)])


def pick(blocks, index):
    return lax.dynamic_index_in_dim(jnp.stack(blocks), index, 0, keepdims=False)


def shift(head, tail, axes):
    count = lax.axis_size(axes)
    up = [(i, i + 1) for i in range(count - 1)]
    down = [(i + 1, i) for i in range(count - 1)]
    return lax.ppermute(tail, axes, up), lax.ppermute(head, axes, down)


def group_shape():
    count = lax.axis_size("group")
    far = min(4, count)
    return far, count // far


def group_swap(block, flip):
    count = lax.axis_size("group")
    return lax.ppermute(block, "group", [(g, g ^ flip) for g in range(count)])


def gather_far(piece):
    far, near = group_shape()
    return [piece] + [group_swap(piece, k * near) for k in range(1, far)]


def gather_near(stack):
    _, near = group_shape()
    return [stack] + [group_swap(stack, j) for j in range(1, near)]


def summed(parts):
    return sum(part.astype(F32) for part in parts).astype(BF16)


def scatter_near(blocks, *after):
    far, near = group_shape()
    place = lax.axis_index("group") % near
    blocks = blocks.reshape(*blocks.shape[:-3], far, near, *blocks.shape[-2:])
    axis = blocks.ndim - 3
    parts = [lax.dynamic_index_in_dim(blocks, place ^ j, axis, keepdims=False) for j in range(near)]
    mine = tie(parts[0], *after) if after else parts[0]
    return summed([mine] + [group_swap(parts[j], j) for j in range(1, near)])


def far_parts(blocks):
    far, near = group_shape()
    place = lax.axis_index("group") // near
    axis = blocks.ndim - 3
    parts = [lax.dynamic_index_in_dim(blocks, place ^ k, axis, keepdims=False) for k in range(far)]
    return [parts[0]] + [group_swap(parts[k], k * near) for k in range(1, far)]


def sum_chips(block, bit):
    while bit < lax.axis_size("replica"):
        block = summed([block, swap(block, bit)])
        bit *= 2
    return block


def halves(own, other, core):
    return jnp.where(core == 0, own, other), jnp.where(core == 0, other, own)


def place_kernel(near, far, cut, place_ref, *refs):
    own, other = refs[:near], refs[near : 2 * near]
    full_ref, side_ref = refs[-2:]
    core = place_ref[2]
    for j in range(near):
        for k in range(far):
            shard = (place_ref[0] ^ k) * near + (place_ref[1] ^ j)

            @pl.when(core == 0)
            def _():
                full_ref[shard, :, :cut] = own[j][k, :, :cut]
                full_ref[shard, :, cut:] = other[j][k, :, :cut]

            @pl.when(core != 0)
            def _():
                full_ref[shard, :, :cut] = other[j][k, :, :cut]
                full_ref[shard, :, cut:] = own[j][k, :, :cut]

            side_ref[shard] = own[j][k, :, cut:]


def place_pieces(own, other, place, after=()):
    near, far = len(own), own[0].shape[0]
    rows, cut = own[0].shape[1], own[0].shape[2] - LANES
    raw = pl.BlockSpec(memory_space=pl.ANY)
    near_by = pl.BlockSpec(memory_space=pltpu.VMEM)
    full, side = pl.pallas_call(
        partial(place_kernel, near, far, cut),
        in_specs=[pl.BlockSpec(memory_space=pltpu.SMEM)]
        + [near_by] * (2 * near)
        + [raw] * len(after),
        out_specs=[near_by, near_by],
        out_shape=[
            jax.ShapeDtypeStruct((near * far, rows, 2 * cut), BF16),
            jax.ShapeDtypeStruct((near * far, rows, LANES), BF16),
        ],
        compiler_params=pltpu.CompilerParams(vmem_limit_bytes=56 * 2**20),
        name="place_pieces",
    )(place, *own, *other, *after)
    return full.reshape(-1, 2 * cut), side.reshape(-1, LANES)


def tie(value, *others):
    raw = pl.BlockSpec(memory_space=pl.ANY)
    return pl.pallas_call(
        lambda *refs: None,
        in_specs=[raw] * (1 + len(others)),
        out_specs=raw,
        out_shape=jax.ShapeDtypeStruct(value.shape, value.dtype),
        input_output_aliases={0: 0},
        compiler_params=pltpu.CompilerParams(vmem_limit_bytes=56 * 2**20),
        name="tie",
    )(value, *others)


def standardize(values):
    centre = jnp.mean(values, axis=-1, keepdims=True)
    shifted = values - centre
    row_scale = lax.rsqrt(jnp.mean(shifted * shifted, axis=-1, keepdims=True) + NORM_EPS)
    return (shifted * row_scale, row_scale)


def norm_back(grad_norm, normed, row_scale, gain_row):
    grad_hat = grad_norm * gain_row
    centred = grad_hat - jnp.mean(grad_hat, axis=-1, keepdims=True)
    return row_scale * (centred - normed * jnp.mean(grad_hat * normed, axis=-1, keepdims=True))


def adam_step(weight, moment, squares, gradient, rate_value):
    drift = 0.9 * moment + 0.1 * gradient
    energy = 0.999 * squares + 0.001 * gradient * gradient
    first_hat = drift / (1.0 - 0.9**STEP)
    second_hat = energy / (1.0 - 0.999**STEP)
    after = weight - rate_value * (first_hat / (jnp.sqrt(second_hat) + 1e-08) + 0.1 * weight)
    return (drift, energy, after)


def stacked_heads(rows, factor):
    half = rows.shape[1] // 2
    lane = lax.broadcasted_iota(jnp.int32, rows.shape, 1)
    values = rows.astype(F32) * factor
    first = jnp.where(lane < half, values, 0.0)
    second = jnp.where(lane < half, 0.0, values)
    return jnp.concatenate([first, second], axis=0).astype(BF16)


def unstacked_heads(product, rows):
    half = product.shape[0] // 2
    both = jnp.concatenate([product[:half, :rows], product[half:, rows:]], axis=0)
    return both.T


def key_allowed(first_ref, last_ref, block):
    key = lax.broadcasted_iota(jnp.int32, (SPAN, 2 * QB), 0) + block * QB
    return (key >= first_ref[block : block + 1, :]) & (key < last_ref[block : block + 1, :])


def attend_kernel(scale, q_ref, k_ref, v_ref, first_ref, last_ref, *refs):
    ctx_ref, lse_ref, vt_ref = refs[-3:]
    vt_ref[...] = v_ref[...].T
    for block in range(q_ref.shape[0] // QB):
        rows = slice(block * QB, (block + 1) * QB)
        span = slice(block * QB, block * QB + SPAN)
        queries = stacked_heads(q_ref[rows, :], scale)
        scores = lax.dot_general(k_ref[span, :], queries, NT, preferred_element_type=F32)
        scores = jnp.where(key_allowed(first_ref, last_ref, block), scores, MASKED)
        peak = jnp.max(scores, axis=0, keepdims=True)
        expo = jnp.exp(scores - peak)
        total = jnp.sum(expo, axis=0, keepdims=True)
        probs = (expo * (1.0 / total)).astype(BF16)
        mixed = jnp.dot(vt_ref[:, span], probs, preferred_element_type=F32)
        ctx_ref[rows, :] = unstacked_heads(mixed, QB).astype(BF16)
        lse_ref[0, block : block + 1, :] = peak + jnp.log(total)


def attend_back_kernel(
    scale,
    q_ref,
    k_ref,
    v_ref,
    grad_ref,
    first_ref,
    last_ref,
    lse_ref,
    *refs,
):
    dq_ref, dk_ref, dv_ref, kt_ref, dk_sum, dv_sum = refs[-6:]
    kt_ref[...] = k_ref[...].T
    dk_sum[...] = jnp.zeros_like(dk_sum)
    dv_sum[...] = jnp.zeros_like(dv_sum)
    for block in range(q_ref.shape[0] // QB):
        rows = slice(block * QB, (block + 1) * QB)
        span = slice(block * QB, block * QB + SPAN)
        queries = stacked_heads(q_ref[rows, :], scale)
        grads = stacked_heads(grad_ref[rows, :], 1.0)
        scores = lax.dot_general(k_ref[span, :], queries, NT, preferred_element_type=F32)
        scores = jnp.where(key_allowed(first_ref, last_ref, block), scores, MASKED)
        probs = jnp.exp(scores - lse_ref[0, block : block + 1, :])
        prob_grad = lax.dot_general(v_ref[span, :], grads, NT, preferred_element_type=F32)
        mean = jnp.sum(probs * prob_grad, axis=0, keepdims=True)
        score_grad = (probs * (prob_grad - mean)).astype(BF16)
        dv_sum[span, :] += jnp.dot(probs.astype(BF16), grads, preferred_element_type=F32)
        dk_sum[span, :] += jnp.dot(score_grad, queries, preferred_element_type=F32)
        dq = jnp.dot(kt_ref[:, span], score_grad, preferred_element_type=F32)
        dq_ref[rows, :] = (unstacked_heads(dq, QB) * scale).astype(BF16)
    dk_ref[...] = dk_sum[...].astype(BF16)
    dv_ref[...] = dv_sum[...].astype(BF16)


def attend(qkv_rows, kv_window, first_key, last_key, scale, after=()):
    rows, width = qkv_rows.shape[0], qkv_rows.shape[1] // 3
    pairs = width // LANES
    window = kv_window.shape[0]
    whole = pl.BlockSpec(first_key.shape, lambda h: (0, 0))
    return pl.pallas_call(
        partial(attend_kernel, scale),
        grid=(pairs,),
        in_specs=[
            pl.BlockSpec((rows, LANES), lambda h: (0, h)),
            pl.BlockSpec((window, LANES), lambda h: (0, h)),
            pl.BlockSpec((window, LANES), lambda h: (0, pairs + h)),
            whole,
            whole,
            *[pl.BlockSpec(memory_space=pl.ANY)] * len(after),
        ],
        out_specs=[
            pl.BlockSpec((rows, LANES), lambda h: (0, h)),
            pl.BlockSpec((1, 8, 2 * QB), lambda h: (h, 0, 0)),
        ],
        out_shape=[
            jax.ShapeDtypeStruct((rows, width), BF16),
            jax.ShapeDtypeStruct((pairs, 8, 2 * QB), F32),
        ],
        scratch_shapes=[pltpu.VMEM((LANES, window), BF16)],
        compiler_params=pltpu.CompilerParams(vmem_limit_bytes=56 * 2**20),
        cost_estimate=ATTEND_COST,
        name="attend",
    )(qkv_rows, kv_window, kv_window, first_key, last_key, *after)


def attend_back(qkv_rows, kv_window, context_grad, first_key, last_key, lse, scale, heads, after=()):
    rows, width = context_grad.shape
    pairs = width // LANES
    low, count = heads.start, len(heads)
    window = kv_window.shape[0]
    whole = pl.BlockSpec(first_key.shape, lambda h: (0, 0))
    return pl.pallas_call(
        partial(attend_back_kernel, scale),
        grid=(count,),
        in_specs=[
            pl.BlockSpec((rows, LANES), lambda h: (0, low + h)),
            pl.BlockSpec((window, LANES), lambda h: (0, low + h)),
            pl.BlockSpec((window, LANES), lambda h: (0, pairs + low + h)),
            pl.BlockSpec((rows, LANES), lambda h: (0, low + h)),
            whole,
            whole,
            pl.BlockSpec((1, 8, 2 * QB), lambda h: (low + h, 0, 0)),
            *[pl.BlockSpec(memory_space=pl.ANY)] * len(after),
        ],
        out_specs=[
            pl.BlockSpec((rows, LANES), lambda h: (0, h)),
            pl.BlockSpec((window, LANES), lambda h: (0, h)),
            pl.BlockSpec((window, LANES), lambda h: (0, h)),
        ],
        out_shape=[
            jax.ShapeDtypeStruct((rows, count * LANES), BF16),
            jax.ShapeDtypeStruct((window, count * LANES), BF16),
            jax.ShapeDtypeStruct((window, count * LANES), BF16),
        ],
        scratch_shapes=[
            pltpu.VMEM((LANES, window), BF16),
            pltpu.VMEM((window, LANES), F32),
            pltpu.VMEM((window, LANES), F32),
        ],
        compiler_params=pltpu.CompilerParams(vmem_limit_bytes=56 * 2**20),
        cost_estimate=BACK_COST,
        name="attend_back",
    )(qkv_rows, kv_window, kv_window, context_grad, first_key, last_key, lse, *after)


def gelu_both(pre):
    bell = jnp.exp(pre * pre * -0.5)
    t = 1.0 / (1.0 + jnp.abs(pre) * (0.3275911 * 0.5**0.5))
    tail = 1.061405429 * t - 1.453152027
    tail = tail * t + 1.421413741
    tail = tail * t - 0.284496736
    tail = (tail * t + 0.254829592) * t * (0.5 * bell)
    below = jnp.where(pre < 0.0, tail, 1.0 - tail)
    return pre * below, below + pre * (bell * 0.3989422804014327)


def pack_kernel(count, rows_ref, rank_ref, *refs):
    out_refs = refs[-count:]
    slots, tokens = out_refs[0].shape[0], rows_ref.shape[0]
    slot = lax.broadcasted_iota(jnp.int32, (slots, tokens), 0)
    for at, out_ref in enumerate(out_refs):
        spots = jnp.where(slot == rank_ref[at : at + 1, :], 1.0, 0.0).astype(BF16)
        out_ref[...] = jnp.dot(spots, rows_ref[...], preferred_element_type=F32).astype(BF16)


def pack(rows, ranks, slots, after=()):
    count, width = ranks.shape[0], rows.shape[1]
    near_by = pl.BlockSpec(memory_space=pltpu.VMEM)
    return pl.pallas_call(
        partial(pack_kernel, count),
        in_specs=[near_by, near_by] + [pl.BlockSpec(memory_space=pl.ANY)] * len(after),
        out_specs=[near_by] * count,
        out_shape=[jax.ShapeDtypeStruct((slots, width), BF16)] * count,
        compiler_params=pltpu.CompilerParams(vmem_limit_bytes=56 * 2**20),
        name="pack",
    )(rows, ranks, *after)


def token_spots(rank_col, slots):
    slot = lax.broadcasted_iota(jnp.int32, (rank_col.shape[0], slots), 1)
    return slot == rank_col


def unpack_grad_kernel(count, *refs):
    parts, rank_refs = refs[:count], refs[count : 2 * count]
    sum_ref, gate_grad_ref = refs[-2:]
    tokens = sum_ref.shape[0]
    slots = parts[0].shape[0] - TAIL
    total = jnp.zeros(sum_ref.shape, F32)
    gate_grads = jnp.zeros((tokens, LANES), F32)
    lane = lax.broadcasted_iota(jnp.int32, (tokens, LANES), 1)
    for j in range(count):
        mask = token_spots(rank_refs[j][...], slots)
        spots = jnp.where(mask, 1.0, 0.0).astype(BF16)
        total += jnp.dot(spots, parts[j][:slots, :], preferred_element_type=F32)
        tail = parts[j][slots:, :].astype(F32)
        slot_grad = tail[0:1, :slots] + tail[1:2, :slots]
        gate_grad = jnp.sum(jnp.where(mask, slot_grad, 0.0), axis=1, keepdims=True)
        gate_grads = jnp.where(lane == j, gate_grad, gate_grads)
    sum_ref[...] = total
    gate_grad_ref[...] = gate_grads


def unpack_grad(parts, rank_cols, after=()):
    tokens, width = rank_cols[0].shape[0], parts[0].shape[1]
    count = len(parts)
    near_by = pl.BlockSpec(memory_space=pltpu.VMEM)
    return pl.pallas_call(
        partial(unpack_grad_kernel, count),
        in_specs=[near_by] * (2 * count) + [pl.BlockSpec(memory_space=pl.ANY)] * len(after),
        out_specs=[near_by, near_by],
        out_shape=[
            jax.ShapeDtypeStruct((tokens, width), F32),
            jax.ShapeDtypeStruct((tokens, LANES), F32),
        ],
        compiler_params=pltpu.CompilerParams(vmem_limit_bytes=56 * 2**20),
        name="unpack_grad",
    )(*parts, *rank_cols, *after)


def unpack_out_kernel(count, residual_ref, *refs):
    parts, rank_refs = refs[:count], refs[count : 2 * count]
    gate_refs, out_ref = refs[2 * count : 3 * count], refs[-1]
    total = residual_ref[...]
    for j in range(count):
        mask = token_spots(rank_refs[j][...], parts[j].shape[0])
        spots = jnp.where(mask, 1.0, 0.0).astype(BF16)
        total += gate_refs[j][...] * jnp.dot(spots, parts[j][...], preferred_element_type=F32)
    out_ref[...] = total.astype(BF16)


def unpack_out(residual, parts, rank_cols, gate_cols, after=()):
    near_by = pl.BlockSpec(memory_space=pltpu.VMEM)
    return pl.pallas_call(
        partial(unpack_out_kernel, len(parts)),
        in_specs=[near_by] * (1 + 3 * len(parts)) + [pl.BlockSpec(memory_space=pl.ANY)] * len(after),
        out_specs=near_by,
        out_shape=jax.ShapeDtypeStruct(residual.shape, BF16),
        compiler_params=pltpu.CompilerParams(vmem_limit_bytes=56 * 2**20),
        name="unpack_out",
    )(residual, *parts, *rank_cols, *gate_cols, *after)


def expert_kernel(count, others, near, first, expert_count, place_ref, router_ref, *refs):
    refs = list(refs)

    def take(number):
        taken = refs[:number]
        del refs[:number]
        return taken

    x_parts, dy_parts, sources = take(count), take(count), take(near)
    with_grads = others > 0
    before = [[], [], []] if first else [take(count), take(count), take(count)]
    other_x, other_g, other_act, other_pg = take(others), take(others), take(others), take(others)
    scratch = 9 if first else 11
    scratch_refs = refs[-scratch:]
    outs = refs[:-scratch]
    outs = outs[-(3 if first else 2) * count - (1 if with_grads else 2 * count) :]
    weights, arrived, part_sems, x_rows, g_rows, dy_rows, xt_rows, gt_rows, both_rows = scratch_refs[:9]
    act_rows, pg_rows = both_rows.at[0], both_rows.at[1]
    if first:
        eout, xgrad = outs[:count], outs[count : 2 * count]
    else:
        eout = [scratch_refs[9].at[part] for part in range(count)]
        xgrad = [scratch_refs[10].at[part] for part in range(count)]
    step = pl.program_id(0)
    steps = pl.num_programs(0)
    slots, width = x_parts[0].shape
    hidden = weights.shape[-1]
    own = count * slots

    def fetch(number, slot):
        columns = pl.ds(pl.multiple_of(number * hidden, LANES), hidden)
        copies = []
        for j in range(near):
            for k in range(sources[j].shape[0]):
                shard = (place_ref[0] ^ k) * near + (place_ref[1] ^ j)
                copies.append(
                    pltpu.make_async_copy(
                        sources[j].at[k, :, :, columns],
                        weights.at[slot, :, shard],
                        arrived.at[slot, len(copies)],
                    )
                )
        return copies

    slot_of = lax.rem(step, 2)

    @pl.when(step == 0)
    def _():
        copies = []
        for part in range(count):
            rows = pl.ds(part * slots, slots)
            copies.append((x_parts[part], x_rows.at[rows]))
            copies.append((dy_parts[part], dy_rows.at[rows]))
            if not first:
                copies.append((before[0][part], eout[part]))
                copies.append((before[1][part], xgrad[part]))
                copies.append((before[2][part], g_rows.at[rows]))
        for part in range(others):
            rows = pl.ds(own + part * slots, slots)
            copies.append((other_x[part], x_rows.at[rows]))
            copies.append((other_g[part], g_rows.at[rows]))
        copies = [
            pltpu.make_async_copy(source, target, part_sems.at[at])
            for at, (source, target) in enumerate(copies)
        ]
        for copy in copies + fetch(0, 0):
            copy.start()
        for copy in copies:
            copy.wait()
        if first:
            for part in range(count):
                rows = slice(part * slots, (part + 1) * slots)
                eout[part][...] = jnp.zeros(eout[part].shape, F32)
                xgrad[part][...] = jnp.zeros(xgrad[part].shape, F32)
                logits = jnp.dot(x_rows[rows, :], router_ref[...], preferred_element_type=F32)
                lane = lax.broadcasted_iota(jnp.int32, logits.shape, 1)
                logits = jnp.where(lane < expert_count, logits, MASKED)
                expo = jnp.exp(logits - jnp.max(logits, axis=1, keepdims=True))
                mine = jnp.sum(jnp.where(lane == place_ref[3], expo, 0.0), axis=1, keepdims=True)
                gate = mine / jnp.sum(expo, axis=1, keepdims=True)
                weighted = (dy_rows[rows, :].astype(F32) * gate).astype(BF16)
                g_rows[rows, :] = weighted
                outs[2 * count + part][...] = weighted
        if with_grads:
            xt_rows[...] = x_rows[...].T
            gt_rows[...] = g_rows[...].T

    @pl.when(step + 1 < steps)
    def _():
        for copy in fetch(step + 1, 1 - slot_of):
            copy.start()

    for copy in fetch(step, slot_of):
        copy.wait()
    inner = weights[slot_of, 0].reshape(width, hidden)
    outer = weights[slot_of, 1].reshape(width, hidden)
    for part in range(count):
        rows = slice(part * slots, (part + 1) * slots)
        pre = jnp.dot(x_rows[rows, :], inner, preferred_element_type=F32)
        act_grad = jnp.dot(g_rows[rows, :], outer, preferred_element_type=F32)
        act, slope = gelu_both(pre)
        act = act.astype(BF16)
        pre_grad = (act_grad * slope).astype(BF16)
        if with_grads:
            act_rows[rows, :] = act
            pg_rows[rows, :] = pre_grad
        else:
            outs[-2 * count + part][...] = act
            outs[-count + part][...] = pre_grad
        eout[part][...] += lax.dot_general(act, outer, NT, preferred_element_type=F32)
        xgrad[part][...] += lax.dot_general(pre_grad, inner, NT, preferred_element_type=F32)
    if with_grads:
        grad_ref = outs[-1]
        for part in range(others):
            rows = slice(own + part * slots, own + (part + 1) * slots)
            act_rows[rows, :] = other_act[part][...]
            pg_rows[rows, :] = other_pg[part][...]
        grad = jnp.dot(xt_rows[...], pg_rows[...], preferred_element_type=F32)
        grad_ref[0] = grad.astype(BF16)
        grad = jnp.dot(gt_rows[...], act_rows[...], preferred_element_type=F32)
        grad_ref[1] = grad.astype(BF16)
    if first:
        return

    @pl.when(step == steps - 1)
    def _():
        for part in range(count):
            out_ref, xgrad_ref = outs[part], outs[count + part]
            rows = slice(part * slots, (part + 1) * slots)
            out = eout[part][...]
            out_ref[...] = out.astype(BF16)
            xgrad_ref[:slots, :] = xgrad[part][...].astype(BF16)
            slot_grad = jnp.sum(dy_rows[rows, :].astype(F32) * out, axis=1, keepdims=True)
            row = jnp.broadcast_to(slot_grad, (slots, LANES)).T[0:1, :]
            row = jnp.concatenate([row, jnp.zeros((1, width - slots), F32)], axis=1)
            high = row.astype(BF16).astype(F32)
            at = lax.broadcasted_iota(jnp.int32, (TAIL, width), 0)
            tail = jnp.where(at == 0, high, jnp.where(at == 1, row - high, 0.0))
            xgrad_ref[slots:, :] = tail.astype(BF16)


def expert(
    place, router, x_parts, dy_parts, sources, expert_count, before=(), other=(), after=()
):
    count, near = len(x_parts), len(sources)
    slots, width = x_parts[0].shape
    group = lax.axis_size("group")
    columns = sources[0].shape[-1]
    hidden = BLOCK if columns % BLOCK == 0 else columns
    raw = pl.BlockSpec(memory_space=pl.ANY)
    first, with_grads = len(before) == 0, len(other) > 0
    others = len(other[0]) if with_grads else 0
    rows = (count + others) * slots
    sums = jax.ShapeDtypeStruct((slots, width), F32)
    slot_rows = jax.ShapeDtypeStruct((slots, width), BF16)
    if first:
        shapes = [sums] * (2 * count) + [slot_rows] * count
    else:
        shapes = [slot_rows] * count
        shapes += [jax.ShapeDtypeStruct((slots + TAIL, width), BF16)] * count
    out_specs = [pl.BlockSpec(shape.shape, lambda i: (0, 0)) for shape in shapes]
    hidden_rows = pl.BlockSpec((slots, hidden), lambda i: (0, i))
    if with_grads:
        out_specs.append(pl.BlockSpec((2, width, hidden), lambda i: (0, 0, i)))
        shapes.append(jax.ShapeDtypeStruct((2, width, columns), BF16))
    else:
        out_specs += [hidden_rows] * (2 * count)
        shapes += [jax.ShapeDtypeStruct((slots, columns), BF16)] * (2 * count)
    turned = (width, rows) if with_grads else (16, LANES)
    sums_scratch = [] if first else [pltpu.VMEM((count, slots, width), F32)] * 2
    before = [array for arrays in before for array in arrays]
    other = [array for arrays in other for array in arrays]
    outs = pl.pallas_call(
        partial(expert_kernel, count, others, near, first, expert_count),
        grid=(columns // hidden,),
        in_specs=[
            pl.BlockSpec(memory_space=pltpu.SMEM),
            pl.BlockSpec(router.shape, lambda i: (0, 0), pipeline_mode=pl.Buffered(1)),
            *[raw] * (2 * count + near + len(before) + 2 * others),
            *[hidden_rows] * (2 * others),
            *[raw] * len(after),
        ],
        out_specs=out_specs,
        out_shape=shapes,
        scratch_shapes=[
            pltpu.VMEM((2, 2, group, width // group, hidden), BF16),
            pltpu.SemaphoreType.DMA((2, group)),
            pltpu.SemaphoreType.DMA((5 * count + 2 * others,)),
            pltpu.VMEM((rows, width), BF16),
            pltpu.VMEM((rows, width), BF16),
            pltpu.VMEM((count * slots, width), BF16),
            pltpu.VMEM(turned, BF16),
            pltpu.VMEM(turned, BF16),
            pltpu.VMEM((2, rows if with_grads else 16, hidden), BF16),
            *sums_scratch,
        ],
        compiler_params=pltpu.CompilerParams(vmem_limit_bytes=62 * 2**20),
        cost_estimate=EXPERT_COST,
        name="expert",
    )(place, router, *x_parts, *dy_parts, *sources, *before, *other, *after)
    lists = (3 if first else 2) if with_grads else (5 if first else 4)
    split = [outs[at * count : (at + 1) * count] for at in range(lists)]
    return (*split, outs[-1]) if with_grads else split


def update_kernel(base, mine_ref, *refs):
    states, grads, outs = refs[:6], refs[6:10], refs[-6:]
    half = grads[0].shape[-1]
    for at in range(2):

        @pl.when(pl.program_id(0) == at)
        def _():
            for matrix in range(2):
                weight, moment, squares = states[3 * matrix : 3 * matrix + 3]
                for part in range(2):
                    columns = slice(part * half, (part + 1) * half)
                    new = adam_step(
                        weight[0, :, columns],
                        moment[0, :, columns],
                        squares[0, :, columns],
                        grads[2 * at + part][matrix].astype(F32),
                        RATES[4 + matrix],
                    )
                    for out, value in zip(outs[3 * matrix : 3 * matrix + 3], new):
                        out[0, :, columns] = value


def update_experts(mine, base, states, grads, done=()):
    shape = states[0].shape
    block = pl.BlockSpec((1, *shape[1:]), lambda i, at: (at[0] ^ (base + i), 0, 0))
    whole = pl.BlockSpec(grads[0].shape, lambda i, at: (0, 0, 0))
    raw = pl.BlockSpec(memory_space=pl.ANY)
    return pl.pallas_call(
        partial(update_kernel, base),
        grid_spec=pltpu.PrefetchScalarGridSpec(
            num_scalar_prefetch=1,
            grid=(2,),
            in_specs=[block] * 6 + [whole] * 4 + [raw] * len(done),
            out_specs=[block] * 6,
        ),
        out_shape=[jax.ShapeDtypeStruct(shape, F32)] * 6,
        input_output_aliases={11 + at: at for at in range(len(done))},
        compiler_params=pltpu.CompilerParams(vmem_limit_bytes=56 * 2**20),
        cost_estimate=UPDATE_COST,
        name="update_experts",
    )(jnp.reshape(mine, (1,)), *states, *grads, *done)


def per_device(
    block_input,
    out_grad,
    image_pos,
    routes,
    norm_weight,
    norm_moment,
    norm_squares,
    qkv_weight,
    qkv_moment,
    qkv_squares,
    proj_weight,
    proj_moment,
    proj_squares,
    router_weight,
    router_moment,
    router_squares,
    inner_weight,
    inner_moment,
    inner_squares,
    outer_weight,
    outer_moment,
    outer_squares,
):
    row_count, width = block_input.shape
    scale = (width // HEADS) ** (-0.5)
    expert_count, _, hidden = inner_weight.shape
    replica = lax.axis_index("replica")
    mine = replica & (expert_count - 1)
    device_pos = lax.axis_index(("replica", "group"))
    all_rows = row_count * lax.axis_size(("replica", "group"))
    first_row = device_pos * row_count

    far, near = group_shape()
    core = replica & 1
    group_at = lax.axis_index("group")
    place = jnp.stack([group_at // near, group_at % near, core, mine]).astype(jnp.int32)

    def dense_gather(matrix, side):
        cut_to = matrix.shape[1] // 2
        half = lax.dynamic_slice_in_dim(matrix, core * cut_to, cut_to, axis=1)
        return gather_far(jnp.concatenate([half, side], axis=1).astype(BF16))

    def dense_place(pieces, after=()):
        own = gather_near(jnp.stack(pieces))
        return place_pieces(own, [swap(block, CORE_BIT) for block in own], place, after)

    small = jnp.concatenate([norm_weight.T, router_weight], axis=1)
    small = jnp.pad(small, ((0, 0), (0, LANES - small.shape[1])))
    qkv_far = dense_gather(qkv_weight, small)
    proj_far = dense_gather(proj_weight, jnp.zeros_like(small))

    capacity = 5 * row_count // 8
    names = jnp.arange(expert_count, dtype=jnp.int32)
    named = jnp.any(routes.T[None, :, :] == (mine ^ names)[:, None, None], axis=1)
    earlier = jnp.arange(row_count)[:, None] < jnp.arange(row_count)[None, :]
    before = jnp.dot(named.astype(BF16), earlier.astype(BF16), preferred_element_type=F32)
    ranks = jnp.where(named, before.astype(jnp.int32), -1)
    rank_cols = [ranks[j][:, None] for j in range(expert_count)]

    def exchange(packed):
        moved = {j: swap(packed[j], j) for j in (2, 3, 1)}
        return [packed[0], moved[1], moved[2], moved[3]]

    def expert_cut(part):
        size = hidden // HALVES
        return jnp.stack(
            [
                lax.dynamic_index_in_dim(matrix, mine, 0, keepdims=False)[
                    :, part * size : (part + 1) * size
                ]
                for matrix in (inner_weight, outer_weight.transpose(0, 2, 1))
            ]
        ).astype(BF16)

    group = far * near
    far_pieces = [gather_far(tie(expert_cut(0), qkv_far[-1]))]
    far_pieces.append(gather_far(tie(expert_cut(1), far_pieces[0][-1])))
    dy_parts = exchange(
        pack(out_grad, ranks, capacity, (far_pieces[0][1], far_pieces[0][3]))
    )
    qkv_full, small_full = dense_place(qkv_far)
    proj_full, _ = dense_place(proj_far, tuple(dy_parts[2:]))
    small_rows = small_full[:, :8].T
    norm_full = small_rows[:4].astype(F32)
    router_t = small_rows[4:8]
    router_pad = jnp.pad(small_full[:, 4:8], ((0, 0), (0, LANES - 4)))

    x_float = block_input.astype(F32)
    normed_one, scale_one = standardize(x_float)
    first_in = (normed_one * norm_full[0] + norm_full[1]).astype(BF16)
    qkv_rows = jnp.dot(first_in, qkv_full, preferred_element_type=F32).astype(BF16)
    kv_rows = qkv_rows[:, width:]
    below, above = shift(kv_rows[:HALO], kv_rows[row_count - HALO :], ("replica", "group"))
    kv_window = jnp.concatenate([below, kv_rows, above], axis=0)
    row_at = first_row + jnp.arange(row_count, dtype=jnp.int32)
    image_start = row_at - image_pos[:, 0]
    image_end = image_start + image_pos[:, 1]
    first_key = jnp.maximum(image_start, 0) - first_row + HALO
    last_key = jnp.minimum(image_end, all_rows) - first_row + HALO
    first_key = jnp.tile(first_key.reshape(-1, QB), (1, 2))
    last_key = jnp.tile(last_key.reshape(-1, QB), (1, 2))
    context, lse = attend(qkv_rows, kv_window, first_key, last_key, scale)
    sources = [gather_near(jnp.stack([tie(far_pieces[0][0], context), *far_pieces[0][1:]]))]
    residual = x_float + jnp.dot(context, proj_full, preferred_element_type=F32)
    normed_two, scale_two = standardize(residual)
    second_in = (normed_two * norm_full[2] + norm_full[3]).astype(BF16)

    logits = lax.dot_general(router_t, second_in, NT, preferred_element_type=F32)
    logit_expo = jnp.exp(logits - jnp.max(logits, axis=0, keepdims=True))
    gates = logit_expo / jnp.sum(logit_expo, axis=0, keepdims=True)
    gate_cols = [
        lax.dynamic_index_in_dim(gates, mine ^ j, 0, keepdims=False)[:, None]
        for j in range(expert_count)
    ]

    x_parts = exchange(pack(second_in, ranks, capacity, (far_pieces[1][1],)))

    def run(at, part, before=(), other=(), after=()):
        return expert(
            place,
            router_pad,
            [x_parts[j] for j in at],
            [dy_parts[j] for j in at],
            sources[part],
            expert_count,
            before,
            other,
            after,
        )

    near_sums, near_back, near_g, near_act, near_pg = run((0, 1), 0)
    far_stack = jnp.stack([tie(far_pieces[1][0], near_g[0]), *far_pieces[1][1:]])
    sources.append(gather_near(far_stack))
    far_sums, far_back, far_g, low_grad = run(
        (2, 3), 0, other=(x_parts[:2], near_g, near_act, near_pg), after=(far_stack,)
    )
    outs, backs, weighted = near_sums + far_sums, near_back + far_back, near_g + far_g
    sent_out, sent_back, sent_act, sent_pg = run(
        (1, 2, 3), 1, before=(outs[1:], backs[1:], weighted[1:])
    )
    own_out, own_back, high_grad = run(
        (0,),
        1,
        before=(outs[:1], backs[:1], weighted[:1]),
        other=(x_parts[1:], weighted[1:], sent_act, sent_pg),
    )
    out_parts = exchange(own_out + sent_out)
    grad_parts = exchange(own_back + sent_back)
    near_sums = {0: add_near(low_grad)}
    s_sum, gate_grads = unpack_grad(grad_parts, rank_cols, (near_sums[0],))

    gate_grads = gate_grads[:, :expert_count].T
    prob_grad = jnp.concatenate(
        [lax.dynamic_index_in_dim(gate_grads, mine ^ e, 0) for e in range(expert_count)], axis=0
    )
    logit_grad = gates * (prob_grad - jnp.sum(gates * prob_grad, axis=0, keepdims=True))
    logit_grad = logit_grad.astype(BF16)
    router_grad = jnp.dot(logit_grad, second_in, preferred_element_type=F32)
    second_grad = s_sum + lax.dot_general(
        logit_grad, router_t, (((0,), (0,)), ((), ())), preferred_element_type=F32
    )
    gain_two_grad = jnp.sum(second_grad * normed_two, axis=0)
    bias_two_grad = jnp.sum(second_grad, axis=0)
    grad_out = out_grad.astype(F32)
    resid_grad = grad_out + norm_back(second_grad, normed_two, scale_two, norm_full[2])
    branch_grad = resid_grad.astype(BF16)
    proj_grad = jnp.dot(context.T, branch_grad, preferred_element_type=F32)
    context_grad = lax.dot_general(branch_grad, proj_full, NT, preferred_element_type=F32)
    context_grad = context_grad.astype(BF16)

    pairs = width // LANES
    low_parts = far_parts(near_sums[0])
    first_half = attend_back(
        qkv_rows,
        kv_window,
        context_grad,
        first_key,
        last_key,
        lse,
        scale,
        range(0, pairs // 2),
    )
    near_sums[1] = add_near(high_grad, first_half[0])
    second_half = attend_back(
        qkv_rows,
        kv_window,
        context_grad,
        first_key,
        last_key,
        lse,
        scale,
        range(pairs // 2, pairs),
        (near_sums[1], low_parts[1], low_parts[2]),
    )
    block_output = unpack_out(residual, out_parts, rank_cols, gate_cols, (second_half[0],))
    high_parts = far_parts(near_sums[1])
    query_grads, own_grads, outside_grads = [], [], []
    for query_grad, *window_grads in (first_half, second_half):
        query_grads.append(query_grad)
        edges = [
            jnp.concatenate([grad[rows] for grad in window_grads], axis=1)
            for rows in (slice(0, HALO), slice(HALO + row_count, None))
        ]
        from_below, from_above = shift(*edges, ("replica", "group"))
        outside = jnp.concatenate(
            [from_below, jnp.zeros((row_count - 2 * HALO, from_below.shape[1]), BF16), from_above],
            axis=0,
        )
        size = from_below.shape[1] // 2
        for at, grad in enumerate(window_grads):
            own_grads.append(grad[HALO : HALO + row_count])
            outside_grads.append(outside[:, at * size : (at + 1) * size])
    kv_grads = [summed([own_grads[at], outside_grads[at]]) for at in (0, 2, 1, 3)]
    qkv_grad_rows = jnp.concatenate([*query_grads, *kv_grads], axis=1)
    qkv_grad_rows = tie(qkv_grad_rows, low_parts[3], high_parts[1])
    qkv_grad = jnp.dot(first_in.T, qkv_grad_rows, preferred_element_type=F32)
    first_grad = lax.dot_general(qkv_grad_rows, qkv_full, NT, preferred_element_type=F32)
    gain_one_grad = jnp.sum(first_grad * normed_one, axis=0)
    bias_one_grad = jnp.sum(first_grad, axis=0)
    input_grad = (resid_grad + norm_back(first_grad, normed_one, scale_one, norm_full[0])).astype(
        BF16
    )

    norm_grad = jnp.stack([gain_one_grad, bias_one_grad, gain_two_grad, bias_two_grad], axis=0)
    small_grad = jnp.concatenate([norm_grad, router_grad], axis=0).T
    small_grad = jnp.pad(small_grad, ((0, 0), (0, LANES - small_grad.shape[1]))).astype(BF16)
    columns = 3 * width // 2
    qkv_grad, proj_grad = qkv_grad.astype(BF16), proj_grad.astype(BF16)
    dense_grads = jnp.stack(
        [
            jnp.concatenate([qkv_grad[:, :columns], proj_grad[:, : width // 2], small_grad], axis=1),
            jnp.concatenate(
                [qkv_grad[:, columns:], proj_grad[:, width // 2 :], jnp.zeros_like(small_grad)],
                axis=1,
            ),
        ]
    )
    got = swap(lax.dynamic_index_in_dim(dense_grads, 1 - core, 0, keepdims=False), CORE_BIT)
    dense_half = summed([lax.dynamic_index_in_dim(dense_grads, core, 0, keepdims=False), got])
    dense_near = scatter_near(dense_half.reshape(group, width // group, -1))
    owned = []
    for parts, wait_for in ((low_parts, qkv_grad), (high_parts, dense_near)):
        share = sum_chips(summed([tie(parts[0], wait_for), *parts[1:]]), expert_count)
        other_chip = swap(share, CHIP_BIT)
        owned.append([share, swap(share, CORE_BIT), other_chip, swap(other_chip, CORE_BIT)])
    dense_half = sum_chips(summed(far_parts(dense_near)), CHIP_BIT)
    low, high = [part.astype(F32) for part in halves(dense_half, swap(dense_half, CORE_BIT), core)]

    small_sum = low[:, columns + width // 2 :][:, :8]
    qkv_sum = jnp.concatenate([low[:, :columns], high[:, :columns]], axis=1)
    proj_sum = jnp.concatenate(
        [part[:, columns : columns + width // 2] for part in (low, high)], axis=1
    )
    norm_new = adam_step(norm_weight, norm_moment, norm_squares, small_sum[:, :4].T, RATES[0])
    qkv_new = adam_step(qkv_weight, qkv_moment, qkv_squares, qkv_sum, RATES[1])
    proj_new = adam_step(proj_weight, proj_moment, proj_squares, proj_sum, RATES[2])
    router_new = adam_step(
        router_weight, router_moment, router_squares, small_sum[:, 4:8], RATES[3]
    )
    states = (
        inner_weight,
        inner_moment,
        inner_squares,
        outer_weight.transpose(0, 2, 1),
        outer_moment.transpose(0, 2, 1),
        outer_squares.transpose(0, 2, 1),
    )
    done = ()
    for base in range(0, expert_count, 2):
        grads = [owned[part][base + at] for at in range(2) for part in range(2)]
        done = update_experts(mine, base, states, grads, done)
    inner_new = done[:3]
    outer_new = [array.transpose(0, 2, 1) for array in done[3:]]
    return (
        block_output,
        input_grad,
        *norm_new,
        *qkv_new,
        *proj_new,
        *router_new,
        *inner_new,
        *outer_new,
    )


def add_near(grads, *after):
    group = lax.axis_size("group")
    return scatter_near(grads.reshape(2, group, -1, grads.shape[-1]), *after)


def solution(mesh):
    tokens = P(("replica", "group"), None)
    columns = P(None, "group")
    rows = P("group", None)
    inner = P(None, "group", None)
    outer = P(None, None, "group")
    weights = (columns,) * 3 + (rows,) * 9 + (inner,) * 3 + (outer,) * 3
    return jax.shard_map(
        per_device,
        mesh=mesh,
        in_specs=(tokens,) * 4 + weights,
        out_specs=(tokens,) * 2 + weights,
        check_vma=False,
    )
```

```python
from functools import partial

import jax
import jax.numpy as jnp
from jax import lax
from jax.experimental import pallas as pl
from jax.experimental.pallas import tpu as pltpu
from jax.sharding import PartitionSpec as P

HEADS = 12
IMG = 197
STEP = 10
NORM_EPS = 1e-06
MASKED = -1e30
RATES = (0.5, 0.08, 0.6, 0.06, 0.08, 0.15)
LANES = 128
QB = 128
HALO = 208
SPAN = QB + 2 * HALO
TAIL = 16
BLOCK = 768
HALVES = 2
CORE_BIT = 1
CHIP_BIT = 2
F32 = jnp.float32
BF16 = jnp.bfloat16
EXPERT_COST = pl.CostEstimate(flops=28 * 10**9, bytes_accessed=10**5, transcendentals=0)
ATTEND_COST = pl.CostEstimate(flops=30 * 10**9, bytes_accessed=10**5, transcendentals=0)
UPDATE_COST = pl.CostEstimate(flops=10**10, bytes_accessed=10**5, transcendentals=0)
BACK_COST = pl.CostEstimate(flops=15 * 10**9, bytes_accessed=10**5, transcendentals=0)
NT = (((1,), (1,)), ((), ()))


def swap(block, bit):
    count = lax.axis_size("replica")
    return lax.ppermute(block, "replica", [(r, r ^ bit) for r in range(count)])


def pick(blocks, index):
    return lax.dynamic_index_in_dim(jnp.stack(blocks), index, 0, keepdims=False)


def shift(head, tail, axes):
    count = lax.axis_size(axes)
    up = [(i, i + 1) for i in range(count - 1)]
    down = [(i + 1, i) for i in range(count - 1)]
    return lax.ppermute(tail, axes, up), lax.ppermute(head, axes, down)


def group_shape():
    count = lax.axis_size("group")
    far = min(4, count)
    return far, count // far


def group_swap(block, flip):
    count = lax.axis_size("group")
    return lax.ppermute(block, "group", [(g, g ^ flip) for g in range(count)])


def gather_far(piece):
    far, near = group_shape()
    return [piece] + [group_swap(piece, k * near) for k in range(1, far)]


def gather_near(stack):
    _, near = group_shape()
    return [stack] + [group_swap(stack, j) for j in range(1, near)]


def summed(parts):
    return sum(part.astype(F32) for part in parts).astype(BF16)


def scatter_near(blocks, *after):
    far, near = group_shape()
    place = lax.axis_index("group") % near
    blocks = blocks.reshape(*blocks.shape[:-3], far, near, *blocks.shape[-2:])
    axis = blocks.ndim - 3
    parts = [lax.dynamic_index_in_dim(blocks, place ^ j, axis, keepdims=False) for j in range(near)]
    mine = tie(parts[0], *after) if after else parts[0]
    return summed([mine] + [group_swap(parts[j], j) for j in range(1, near)])


def far_parts(blocks):
    far, near = group_shape()
    place = lax.axis_index("group") // near
    axis = blocks.ndim - 3
    parts = [lax.dynamic_index_in_dim(blocks, place ^ k, axis, keepdims=False) for k in range(far)]
    return [parts[0]] + [group_swap(parts[k], k * near) for k in range(1, far)]


def sum_chips(block, bit):
    while bit < lax.axis_size("replica"):
        block = summed([block, swap(block, bit)])
        bit *= 2
    return block


def halves(own, other, core):
    return jnp.where(core == 0, own, other), jnp.where(core == 0, other, own)


def place_kernel(near, far, cut, place_ref, *refs):
    own, other = refs[:near], refs[near : 2 * near]
    full_ref, side_ref = refs[-2:]
    core = place_ref[2]
    for j in range(near):
        for k in range(far):
            shard = (place_ref[0] ^ k) * near + (place_ref[1] ^ j)

            @pl.when(core == 0)
            def _():
                full_ref[shard, :, :cut] = own[j][k, :, :cut]
                full_ref[shard, :, cut:] = other[j][k, :, :cut]

            @pl.when(core != 0)
            def _():
                full_ref[shard, :, :cut] = other[j][k, :, :cut]
                full_ref[shard, :, cut:] = own[j][k, :, :cut]

            side_ref[shard] = own[j][k, :, cut:]


def place_pieces(own, other, place, after=()):
    near, far = len(own), own[0].shape[0]
    rows, cut = own[0].shape[1], own[0].shape[2] - LANES
    raw = pl.BlockSpec(memory_space=pl.ANY)
    near_by = pl.BlockSpec(memory_space=pltpu.VMEM)
    full, side = pl.pallas_call(
        partial(place_kernel, near, far, cut),
        in_specs=[pl.BlockSpec(memory_space=pltpu.SMEM)]
        + [near_by] * (2 * near)
        + [raw] * len(after),
        out_specs=[near_by, near_by],
        out_shape=[
            jax.ShapeDtypeStruct((near * far, rows, 2 * cut), BF16),
            jax.ShapeDtypeStruct((near * far, rows, LANES), BF16),
        ],
        compiler_params=pltpu.CompilerParams(vmem_limit_bytes=56 * 2**20),
        name="place_pieces",
    )(place, *own, *other, *after)
    return full.reshape(-1, 2 * cut), side.reshape(-1, LANES)


def tie(value, *others):
    raw = pl.BlockSpec(memory_space=pl.ANY)
    return pl.pallas_call(
        lambda *refs: None,
        in_specs=[raw] * (1 + len(others)),
        out_specs=raw,
        out_shape=jax.ShapeDtypeStruct(value.shape, value.dtype),
        input_output_aliases={0: 0},
        compiler_params=pltpu.CompilerParams(vmem_limit_bytes=56 * 2**20),
        name="tie",
    )(value, *others)


def standardize(values):
    centre = jnp.mean(values, axis=-1, keepdims=True)
    shifted = values - centre
    row_scale = lax.rsqrt(jnp.mean(shifted * shifted, axis=-1, keepdims=True) + NORM_EPS)
    return (shifted * row_scale, row_scale)


def norm_back(grad_norm, normed, row_scale, gain_row):
    grad_hat = grad_norm * gain_row
    centred = grad_hat - jnp.mean(grad_hat, axis=-1, keepdims=True)
    return row_scale * (centred - normed * jnp.mean(grad_hat * normed, axis=-1, keepdims=True))


def adam_step(weight, moment, squares, gradient, rate_value):
    drift = 0.9 * moment + 0.1 * gradient
    energy = 0.999 * squares + 0.001 * gradient * gradient
    first_hat = drift / (1.0 - 0.9**STEP)
    second_hat = energy / (1.0 - 0.999**STEP)
    after = weight - rate_value * (first_hat / (jnp.sqrt(second_hat) + 1e-08) + 0.1 * weight)
    return (drift, energy, after)


def stacked_heads(rows, factor):
    half = rows.shape[1] // 2
    lane = lax.broadcasted_iota(jnp.int32, rows.shape, 1)
    values = rows.astype(F32) * factor
    first = jnp.where(lane < half, values, 0.0)
    second = jnp.where(lane < half, 0.0, values)
    return jnp.concatenate([first, second], axis=0).astype(BF16)


def unstacked_heads(product, rows):
    half = product.shape[0] // 2
    both = jnp.concatenate([product[:half, :rows], product[half:, rows:]], axis=0)
    return both.T


def key_allowed(first_ref, last_ref, block):
    key = lax.broadcasted_iota(jnp.int32, (SPAN, 2 * QB), 0) + block * QB
    return (key >= first_ref[block : block + 1, :]) & (key < last_ref[block : block + 1, :])


def attend_kernel(scale, q_ref, k_ref, v_ref, first_ref, last_ref, *refs):
    ctx_ref, lse_ref, vt_ref = refs[-3:]
    vt_ref[...] = v_ref[...].T
    for block in range(q_ref.shape[0] // QB):
        rows = slice(block * QB, (block + 1) * QB)
        span = slice(block * QB, block * QB + SPAN)
        queries = stacked_heads(q_ref[rows, :], scale)
        scores = lax.dot_general(k_ref[span, :], queries, NT, preferred_element_type=F32)
        scores = jnp.where(key_allowed(first_ref, last_ref, block), scores, MASKED)
        peak = jnp.max(scores, axis=0, keepdims=True)
        expo = jnp.exp(scores - peak)
        total = jnp.sum(expo, axis=0, keepdims=True)
        probs = (expo * (1.0 / total)).astype(BF16)
        mixed = jnp.dot(vt_ref[:, span], probs, preferred_element_type=F32)
        ctx_ref[rows, :] = unstacked_heads(mixed, QB).astype(BF16)
        lse_ref[0, block : block + 1, :] = peak + jnp.log(total)


def attend_back_kernel(
    scale,
    q_ref,
    k_ref,
    v_ref,
    grad_ref,
    first_ref,
    last_ref,
    lse_ref,
    *refs,
):
    dq_ref, dk_ref, dv_ref, kt_ref, dk_sum, dv_sum = refs[-6:]
    kt_ref[...] = k_ref[...].T
    dk_sum[...] = jnp.zeros_like(dk_sum)
    dv_sum[...] = jnp.zeros_like(dv_sum)
    for block in range(q_ref.shape[0] // QB):
        rows = slice(block * QB, (block + 1) * QB)
        span = slice(block * QB, block * QB + SPAN)
        queries = stacked_heads(q_ref[rows, :], scale)
        grads = stacked_heads(grad_ref[rows, :], 1.0)
        scores = lax.dot_general(k_ref[span, :], queries, NT, preferred_element_type=F32)
        scores = jnp.where(key_allowed(first_ref, last_ref, block), scores, MASKED)
        probs = jnp.exp(scores - lse_ref[0, block : block + 1, :])
        prob_grad = lax.dot_general(v_ref[span, :], grads, NT, preferred_element_type=F32)
        mean = jnp.sum(probs * prob_grad, axis=0, keepdims=True)
        score_grad = (probs * (prob_grad - mean)).astype(BF16)
        dv_sum[span, :] += jnp.dot(probs.astype(BF16), grads, preferred_element_type=F32)
        dk_sum[span, :] += jnp.dot(score_grad, queries, preferred_element_type=F32)
        dq = jnp.dot(kt_ref[:, span], score_grad, preferred_element_type=F32)
        dq_ref[rows, :] = (unstacked_heads(dq, QB) * scale).astype(BF16)
    dk_ref[...] = dk_sum[...].astype(BF16)
    dv_ref[...] = dv_sum[...].astype(BF16)


def attend(qkv_rows, kv_window, first_key, last_key, scale, after=()):
    rows, width = qkv_rows.shape[0], qkv_rows.shape[1] // 3
    pairs = width // LANES
    window = kv_window.shape[0]
    whole = pl.BlockSpec(first_key.shape, lambda h: (0, 0))
    return pl.pallas_call(
        partial(attend_kernel, scale),
        grid=(pairs,),
        in_specs=[
            pl.BlockSpec((rows, LANES), lambda h: (0, h)),
            pl.BlockSpec((window, LANES), lambda h: (0, h)),
            pl.BlockSpec((window, LANES), lambda h: (0, pairs + h)),
            whole,
            whole,
            *[pl.BlockSpec(memory_space=pl.ANY)] * len(after),
        ],
        out_specs=[
            pl.BlockSpec((rows, LANES), lambda h: (0, h)),
            pl.BlockSpec((1, 8, 2 * QB), lambda h: (h, 0, 0)),
        ],
        out_shape=[
            jax.ShapeDtypeStruct((rows, width), BF16),
            jax.ShapeDtypeStruct((pairs, 8, 2 * QB), F32),
        ],
        scratch_shapes=[pltpu.VMEM((LANES, window), BF16)],
        compiler_params=pltpu.CompilerParams(vmem_limit_bytes=56 * 2**20),
        cost_estimate=ATTEND_COST,
        name="attend",
    )(qkv_rows, kv_window, kv_window, first_key, last_key, *after)


def attend_back(qkv_rows, kv_window, context_grad, first_key, last_key, lse, scale, heads, after=()):
    rows, width = context_grad.shape
    pairs = width // LANES
    low, count = heads.start, len(heads)
    window = kv_window.shape[0]
    whole = pl.BlockSpec(first_key.shape, lambda h: (0, 0))
    return pl.pallas_call(
        partial(attend_back_kernel, scale),
        grid=(count,),
        in_specs=[
            pl.BlockSpec((rows, LANES), lambda h: (0, low + h)),
            pl.BlockSpec((window, LANES), lambda h: (0, low + h)),
            pl.BlockSpec((window, LANES), lambda h: (0, pairs + low + h)),
            pl.BlockSpec((rows, LANES), lambda h: (0, low + h)),
            whole,
            whole,
            pl.BlockSpec((1, 8, 2 * QB), lambda h: (low + h, 0, 0)),
            *[pl.BlockSpec(memory_space=pl.ANY)] * len(after),
        ],
        out_specs=[
            pl.BlockSpec((rows, LANES), lambda h: (0, h)),
            pl.BlockSpec((window, LANES), lambda h: (0, h)),
            pl.BlockSpec((window, LANES), lambda h: (0, h)),
        ],
        out_shape=[
            jax.ShapeDtypeStruct((rows, count * LANES), BF16),
            jax.ShapeDtypeStruct((window, count * LANES), BF16),
            jax.ShapeDtypeStruct((window, count * LANES), BF16),
        ],
        scratch_shapes=[
            pltpu.VMEM((LANES, window), BF16),
            pltpu.VMEM((window, LANES), F32),
            pltpu.VMEM((window, LANES), F32),
        ],
        compiler_params=pltpu.CompilerParams(vmem_limit_bytes=56 * 2**20),
        cost_estimate=BACK_COST,
        name="attend_back",
    )(qkv_rows, kv_window, kv_window, context_grad, first_key, last_key, lse, *after)


def gelu_both(pre):
    bell = jnp.exp(pre * pre * -0.5)
    t = 1.0 / (1.0 + jnp.abs(pre) * (0.3275911 * 0.5**0.5))
    tail = 1.061405429 * t - 1.453152027
    tail = tail * t + 1.421413741
    tail = tail * t - 0.284496736
    tail = (tail * t + 0.254829592) * t * (0.5 * bell)
    below = jnp.where(pre < 0.0, tail, 1.0 - tail)
    return pre * below, below + pre * (bell * 0.3989422804014327)


def pack_kernel(count, rows_ref, rank_ref, *refs):
    out_refs = refs[-count:]
    slots, tokens = out_refs[0].shape[0], rows_ref.shape[0]
    slot = lax.broadcasted_iota(jnp.int32, (slots, tokens), 0)
    for at, out_ref in enumerate(out_refs):
        spots = jnp.where(slot == rank_ref[at : at + 1, :], 1.0, 0.0).astype(BF16)
        out_ref[...] = jnp.dot(spots, rows_ref[...], preferred_element_type=F32).astype(BF16)


def pack(rows, ranks, slots, after=()):
    count, width = ranks.shape[0], rows.shape[1]
    near_by = pl.BlockSpec(memory_space=pltpu.VMEM)
    return pl.pallas_call(
        partial(pack_kernel, count),
        in_specs=[near_by, near_by] + [pl.BlockSpec(memory_space=pl.ANY)] * len(after),
        out_specs=[near_by] * count,
        out_shape=[jax.ShapeDtypeStruct((slots, width), BF16)] * count,
        compiler_params=pltpu.CompilerParams(vmem_limit_bytes=56 * 2**20),
        name="pack",
    )(rows, ranks, *after)


def token_spots(rank_col, slots):
    slot = lax.broadcasted_iota(jnp.int32, (rank_col.shape[0], slots), 1)
    return slot == rank_col


def unpack_grad_kernel(count, *refs):
    parts, rank_refs = refs[:count], refs[count : 2 * count]
    sum_ref, gate_grad_ref = refs[-2:]
    tokens = sum_ref.shape[0]
    slots = parts[0].shape[0] - TAIL
    total = jnp.zeros(sum_ref.shape, F32)
    gate_grads = jnp.zeros((tokens, LANES), F32)
    lane = lax.broadcasted_iota(jnp.int32, (tokens, LANES), 1)
    for j in range(count):
        mask = token_spots(rank_refs[j][...], slots)
        spots = jnp.where(mask, 1.0, 0.0).astype(BF16)
        total += jnp.dot(spots, parts[j][:slots, :], preferred_element_type=F32)
        tail = parts[j][slots:, :].astype(F32)
        slot_grad = tail[0:1, :slots] + tail[1:2, :slots]
        gate_grad = jnp.sum(jnp.where(mask, slot_grad, 0.0), axis=1, keepdims=True)
        gate_grads = jnp.where(lane == j, gate_grad, gate_grads)
    sum_ref[...] = total
    gate_grad_ref[...] = gate_grads


def unpack_grad(parts, rank_cols, after=()):
    tokens, width = rank_cols[0].shape[0], parts[0].shape[1]
    count = len(parts)
    near_by = pl.BlockSpec(memory_space=pltpu.VMEM)
    return pl.pallas_call(
        partial(unpack_grad_kernel, count),
        in_specs=[near_by] * (2 * count) + [pl.BlockSpec(memory_space=pl.ANY)] * len(after),
        out_specs=[near_by, near_by],
        out_shape=[
            jax.ShapeDtypeStruct((tokens, width), F32),
            jax.ShapeDtypeStruct((tokens, LANES), F32),
        ],
        compiler_params=pltpu.CompilerParams(vmem_limit_bytes=56 * 2**20),
        name="unpack_grad",
    )(*parts, *rank_cols, *after)


def unpack_out_kernel(count, residual_ref, *refs):
    parts, rank_refs = refs[:count], refs[count : 2 * count]
    gate_refs, out_ref = refs[2 * count : 3 * count], refs[-1]
    total = residual_ref[...]
    for j in range(count):
        mask = token_spots(rank_refs[j][...], parts[j].shape[0])
        spots = jnp.where(mask, 1.0, 0.0).astype(BF16)
        total += gate_refs[j][...] * jnp.dot(spots, parts[j][...], preferred_element_type=F32)
    out_ref[...] = total.astype(BF16)


def unpack_out(residual, parts, rank_cols, gate_cols, after=()):
    near_by = pl.BlockSpec(memory_space=pltpu.VMEM)
    return pl.pallas_call(
        partial(unpack_out_kernel, len(parts)),
        in_specs=[near_by] * (1 + 3 * len(parts)) + [pl.BlockSpec(memory_space=pl.ANY)] * len(after),
        out_specs=near_by,
        out_shape=jax.ShapeDtypeStruct(residual.shape, BF16),
        compiler_params=pltpu.CompilerParams(vmem_limit_bytes=56 * 2**20),
        name="unpack_out",
    )(residual, *parts, *rank_cols, *gate_cols, *after)


def expert_kernel(count, others, near, first, expert_count, place_ref, router_ref, *refs):
    refs = list(refs)

    def take(number):
        taken = refs[:number]
        del refs[:number]
        return taken

    x_parts, dy_parts, sources = take(count), take(count), take(near)
    with_grads = others > 0
    before = [[], [], []] if first else [take(count), take(count), take(count)]
    other_x, other_g, other_act, other_pg = take(others), take(others), take(others), take(others)
    scratch = 9 if first else 11
    scratch_refs = refs[-scratch:]
    outs = refs[:-scratch]
    outs = outs[-(3 if first else 2) * count - (1 if with_grads else 2 * count) :]
    weights, arrived, part_sems, x_rows, g_rows, dy_rows, xt_rows, gt_rows, both_rows = scratch_refs[:9]
    act_rows, pg_rows = both_rows.at[0], both_rows.at[1]
    if first:
        eout, xgrad = outs[:count], outs[count : 2 * count]
    else:
        eout = [scratch_refs[9].at[part] for part in range(count)]
        xgrad = [scratch_refs[10].at[part] for part in range(count)]
    step = pl.program_id(0)
    steps = pl.num_programs(0)
    slots, width = x_parts[0].shape
    hidden = weights.shape[-1]
    own = count * slots

    def fetch(number, slot):
        columns = pl.ds(pl.multiple_of(number * hidden, LANES), hidden)
        copies = []
        for j in range(near):
            for k in range(sources[j].shape[0]):
                shard = (place_ref[0] ^ k) * near + (place_ref[1] ^ j)
                copies.append(
                    pltpu.make_async_copy(
                        sources[j].at[k, :, :, columns],
                        weights.at[slot, :, shard],
                        arrived.at[slot, len(copies)],
                    )
                )
        return copies

    slot_of = lax.rem(step, 2)

    @pl.when(step == 0)
    def _():
        copies = []
        for part in range(count):
            rows = pl.ds(part * slots, slots)
            copies.append((x_parts[part], x_rows.at[rows]))
            copies.append((dy_parts[part], dy_rows.at[rows]))
            if not first:
                copies.append((before[0][part], eout[part]))
                copies.append((before[1][part], xgrad[part]))
                copies.append((before[2][part], g_rows.at[rows]))
        for part in range(others):
            rows = pl.ds(own + part * slots, slots)
            copies.append((other_x[part], x_rows.at[rows]))
            copies.append((other_g[part], g_rows.at[rows]))
        copies = [
            pltpu.make_async_copy(source, target, part_sems.at[at])
            for at, (source, target) in enumerate(copies)
        ]
        for copy in copies + fetch(0, 0):
            copy.start()
        for copy in copies:
            copy.wait()
        if first:
            for part in range(count):
                rows = slice(part * slots, (part + 1) * slots)
                eout[part][...] = jnp.zeros(eout[part].shape, F32)
                xgrad[part][...] = jnp.zeros(xgrad[part].shape, F32)
                logits = jnp.dot(x_rows[rows, :], router_ref[...], preferred_element_type=F32)
                lane = lax.broadcasted_iota(jnp.int32, logits.shape, 1)
                logits = jnp.where(lane < expert_count, logits, MASKED)
                expo = jnp.exp(logits - jnp.max(logits, axis=1, keepdims=True))
                mine = jnp.sum(jnp.where(lane == place_ref[3], expo, 0.0), axis=1, keepdims=True)
                gate = mine / jnp.sum(expo, axis=1, keepdims=True)
                weighted = (dy_rows[rows, :].astype(F32) * gate).astype(BF16)
                g_rows[rows, :] = weighted
                outs[2 * count + part][...] = weighted
        if with_grads:
            xt_rows[...] = x_rows[...].T
            gt_rows[...] = g_rows[...].T

    @pl.when(step + 1 < steps)
    def _():
        for copy in fetch(step + 1, 1 - slot_of):
            copy.start()

    for copy in fetch(step, slot_of):
        copy.wait()
    inner = weights[slot_of, 0].reshape(width, hidden)
    outer = weights[slot_of, 1].reshape(width, hidden)
    for part in range(count):
        rows = slice(part * slots, (part + 1) * slots)
        pre = jnp.dot(x_rows[rows, :], inner, preferred_element_type=F32)
        act_grad = jnp.dot(g_rows[rows, :], outer, preferred_element_type=F32)
        act, slope = gelu_both(pre)
        act = act.astype(BF16)
        pre_grad = (act_grad * slope).astype(BF16)
        if with_grads:
            act_rows[rows, :] = act
            pg_rows[rows, :] = pre_grad
        else:
            outs[-2 * count + part][...] = act
            outs[-count + part][...] = pre_grad
        eout[part][...] += lax.dot_general(act, outer, NT, preferred_element_type=F32)
        xgrad[part][...] += lax.dot_general(pre_grad, inner, NT, preferred_element_type=F32)
    if with_grads:
        grad_ref = outs[-1]
        for part in range(others):
            rows = slice(own + part * slots, own + (part + 1) * slots)
            act_rows[rows, :] = other_act[part][...]
            pg_rows[rows, :] = other_pg[part][...]
        grad = jnp.dot(xt_rows[...], pg_rows[...], preferred_element_type=F32)
        grad_ref[0] = grad.astype(BF16)
        grad = jnp.dot(gt_rows[...], act_rows[...], preferred_element_type=F32)
        grad_ref[1] = grad.astype(BF16)
    if first:
        return

    @pl.when(step == steps - 1)
    def _():
        for part in range(count):
            out_ref, xgrad_ref = outs[part], outs[count + part]
            rows = slice(part * slots, (part + 1) * slots)
            out = eout[part][...]
            out_ref[...] = out.astype(BF16)
            xgrad_ref[:slots, :] = xgrad[part][...].astype(BF16)
            slot_grad = jnp.sum(dy_rows[rows, :].astype(F32) * out, axis=1, keepdims=True)
            row = jnp.broadcast_to(slot_grad, (slots, LANES)).T[0:1, :]
            row = jnp.concatenate([row, jnp.zeros((1, width - slots), F32)], axis=1)
            high = row.astype(BF16).astype(F32)
            at = lax.broadcasted_iota(jnp.int32, (TAIL, width), 0)
            tail = jnp.where(at == 0, high, jnp.where(at == 1, row - high, 0.0))
            xgrad_ref[slots:, :] = tail.astype(BF16)


def expert(
    place, router, x_parts, dy_parts, sources, expert_count, before=(), other=(), after=()
):
    count, near = len(x_parts), len(sources)
    slots, width = x_parts[0].shape
    group = lax.axis_size("group")
    columns = sources[0].shape[-1]
    hidden = BLOCK if columns % BLOCK == 0 else columns
    raw = pl.BlockSpec(memory_space=pl.ANY)
    first, with_grads = len(before) == 0, len(other) > 0
    others = len(other[0]) if with_grads else 0
    rows = (count + others) * slots
    sums = jax.ShapeDtypeStruct((slots, width), F32)
    slot_rows = jax.ShapeDtypeStruct((slots, width), BF16)
    if first:
        shapes = [sums] * (2 * count) + [slot_rows] * count
    else:
        shapes = [slot_rows] * count
        shapes += [jax.ShapeDtypeStruct((slots + TAIL, width), BF16)] * count
    out_specs = [pl.BlockSpec(shape.shape, lambda i: (0, 0)) for shape in shapes]
    hidden_rows = pl.BlockSpec((slots, hidden), lambda i: (0, i))
    if with_grads:
        out_specs.append(pl.BlockSpec((2, width, hidden), lambda i: (0, 0, i)))
        shapes.append(jax.ShapeDtypeStruct((2, width, columns), BF16))
    else:
        out_specs += [hidden_rows] * (2 * count)
        shapes += [jax.ShapeDtypeStruct((slots, columns), BF16)] * (2 * count)
    turned = (width, rows) if with_grads else (16, LANES)
    sums_scratch = [] if first else [pltpu.VMEM((count, slots, width), F32)] * 2
    before = [array for arrays in before for array in arrays]
    other = [array for arrays in other for array in arrays]
    outs = pl.pallas_call(
        partial(expert_kernel, count, others, near, first, expert_count),
        grid=(columns // hidden,),
        in_specs=[
            pl.BlockSpec(memory_space=pltpu.SMEM),
            pl.BlockSpec(router.shape, lambda i: (0, 0), pipeline_mode=pl.Buffered(1)),
            *[raw] * (2 * count + near + len(before) + 2 * others),
            *[hidden_rows] * (2 * others),
            *[raw] * len(after),
        ],
        out_specs=out_specs,
        out_shape=shapes,
        scratch_shapes=[
            pltpu.VMEM((2, 2, group, width // group, hidden), BF16),
            pltpu.SemaphoreType.DMA((2, group)),
            pltpu.SemaphoreType.DMA((5 * count + 2 * others,)),
            pltpu.VMEM((rows, width), BF16),
            pltpu.VMEM((rows, width), BF16),
            pltpu.VMEM((count * slots, width), BF16),
            pltpu.VMEM(turned, BF16),
            pltpu.VMEM(turned, BF16),
            pltpu.VMEM((2, rows if with_grads else 16, hidden), BF16),
            *sums_scratch,
        ],
        compiler_params=pltpu.CompilerParams(vmem_limit_bytes=62 * 2**20),
        cost_estimate=EXPERT_COST,
        name="expert",
    )(place, router, *x_parts, *dy_parts, *sources, *before, *other, *after)
    lists = (3 if first else 2) if with_grads else (5 if first else 4)
    split = [outs[at * count : (at + 1) * count] for at in range(lists)]
    return (*split, outs[-1]) if with_grads else split


def update_kernel(base, mine_ref, *refs):
    states, grads, outs = refs[:6], refs[6:10], refs[-6:]
    half = grads[0].shape[-1]
    for at in range(2):

        @pl.when(pl.program_id(0) == at)
        def _():
            for matrix in range(2):
                weight, moment, squares = states[3 * matrix : 3 * matrix + 3]
                for part in range(2):
                    columns = slice(part * half, (part + 1) * half)
                    new = adam_step(
                        weight[0, :, columns],
                        moment[0, :, columns],
                        squares[0, :, columns],
                        grads[2 * at + part][matrix].astype(F32),
                        RATES[4 + matrix],
                    )
                    for out, value in zip(outs[3 * matrix : 3 * matrix + 3], new):
                        out[0, :, columns] = value


def update_experts(mine, base, states, grads, done=()):
    shape = states[0].shape
    block = pl.BlockSpec((1, *shape[1:]), lambda i, at: (at[0] ^ (base + i), 0, 0))
    whole = pl.BlockSpec(grads[0].shape, lambda i, at: (0, 0, 0))
    raw = pl.BlockSpec(memory_space=pl.ANY)
    return pl.pallas_call(
        partial(update_kernel, base),
        grid_spec=pltpu.PrefetchScalarGridSpec(
            num_scalar_prefetch=1,
            grid=(2,),
            in_specs=[block] * 6 + [whole] * 4 + [raw] * len(done),
            out_specs=[block] * 6,
        ),
        out_shape=[jax.ShapeDtypeStruct(shape, F32)] * 6,
        input_output_aliases={11 + at: at for at in range(len(done))},
        compiler_params=pltpu.CompilerParams(vmem_limit_bytes=56 * 2**20),
        cost_estimate=UPDATE_COST,
        name="update_experts",
    )(jnp.reshape(mine, (1,)), *states, *grads, *done)


def per_device(
    block_input,
    out_grad,
    image_pos,
    routes,
    norm_weight,
    norm_moment,
    norm_squares,
    qkv_weight,
    qkv_moment,
    qkv_squares,
    proj_weight,
    proj_moment,
    proj_squares,
    router_weight,
    router_moment,
    router_squares,
    inner_weight,
    inner_moment,
    inner_squares,
    outer_weight,
    outer_moment,
    outer_squares,
):
    row_count, width = block_input.shape
    scale = (width // HEADS) ** (-0.5)
    expert_count, _, hidden = inner_weight.shape
    replica = lax.axis_index("replica")
    mine = replica & (expert_count - 1)
    device_pos = lax.axis_index(("replica", "group"))
    all_rows = row_count * lax.axis_size(("replica", "group"))
    first_row = device_pos * row_count

    far, near = group_shape()
    core = replica & 1
    group_at = lax.axis_index("group")
    place = jnp.stack([group_at // near, group_at % near, core, mine]).astype(jnp.int32)

    def dense_gather(matrix, side):
        cut_to = matrix.shape[1] // 2
        half = lax.dynamic_slice_in_dim(matrix, core * cut_to, cut_to, axis=1)
        return gather_far(jnp.concatenate([half, side], axis=1).astype(BF16))

    def dense_place(own, after=()):
        return place_pieces(own, [swap(block, CORE_BIT) for block in own], place, after)

    small = jnp.concatenate([norm_weight.T, router_weight], axis=1)
    small = jnp.pad(small, ((0, 0), (0, LANES - small.shape[1])))
    qkv_far = dense_gather(qkv_weight, small)
    proj_far = dense_gather(proj_weight, jnp.zeros_like(small))

    capacity = 5 * row_count // 8
    names = jnp.arange(expert_count, dtype=jnp.int32)
    named = jnp.any(routes.T[None, :, :] == (mine ^ names)[:, None, None], axis=1)
    earlier = jnp.arange(row_count)[:, None] < jnp.arange(row_count)[None, :]
    before = jnp.dot(named.astype(BF16), earlier.astype(BF16), preferred_element_type=F32)
    ranks = jnp.where(named, before.astype(jnp.int32), -1)
    rank_cols = [ranks[j][:, None] for j in range(expert_count)]

    def exchange(packed):
        moved = {j: swap(packed[j], j) for j in (2, 3, 1)}
        return [packed[0], moved[1], moved[2], moved[3]]

    def expert_cut(part):
        size = hidden // HALVES
        return jnp.stack(
            [
                lax.dynamic_index_in_dim(matrix, mine, 0, keepdims=False)[
                    :, part * size : (part + 1) * size
                ]
                for matrix in (inner_weight, outer_weight.transpose(0, 2, 1))
            ]
        ).astype(BF16)

    group = far * near
    far_pieces = [gather_far(tie(expert_cut(0), qkv_far[-1]))]
    far_pieces.append(gather_far(tie(expert_cut(1), far_pieces[0][-1])))
    qkv_near, proj_near = [gather_near(jnp.stack(pieces)) for pieces in (qkv_far, proj_far)]
    qkv_full, small_full = dense_place(qkv_near, tuple(proj_near[1:]))
    small_rows = small_full[:, :8].T
    norm_full = small_rows[:4].astype(F32)
    router_t = small_rows[4:8]
    router_pad = jnp.pad(small_full[:, 4:8], ((0, 0), (0, LANES - 4)))

    x_float = block_input.astype(F32)
    normed_one, scale_one = standardize(x_float)
    first_in = (normed_one * norm_full[0] + norm_full[1]).astype(BF16)
    qkv_rows = jnp.dot(first_in, qkv_full, preferred_element_type=F32).astype(BF16)
    dy_parts = exchange(pack(out_grad, ranks, capacity, (*far_pieces[0][1:], qkv_rows)))
    proj_full, _ = dense_place(proj_near, tuple(dy_parts[2:]))
    kv_rows = qkv_rows[:, width:]
    below, above = shift(kv_rows[:HALO], kv_rows[row_count - HALO :], ("replica", "group"))
    kv_window = jnp.concatenate([below, kv_rows, above], axis=0)
    row_at = first_row + jnp.arange(row_count, dtype=jnp.int32)
    image_start = row_at - image_pos[:, 0]
    image_end = image_start + image_pos[:, 1]
    first_key = jnp.maximum(image_start, 0) - first_row + HALO
    last_key = jnp.minimum(image_end, all_rows) - first_row + HALO
    first_key = jnp.tile(first_key.reshape(-1, QB), (1, 2))
    last_key = jnp.tile(last_key.reshape(-1, QB), (1, 2))
    context, lse = attend(qkv_rows, kv_window, first_key, last_key, scale)
    sources = [gather_near(jnp.stack(far_pieces[0]))]
    residual = x_float + jnp.dot(context, proj_full, preferred_element_type=F32)
    normed_two, scale_two = standardize(residual)
    second_in = (normed_two * norm_full[2] + norm_full[3]).astype(BF16)

    logits = lax.dot_general(router_t, second_in, NT, preferred_element_type=F32)
    logit_expo = jnp.exp(logits - jnp.max(logits, axis=0, keepdims=True))
    gates = logit_expo / jnp.sum(logit_expo, axis=0, keepdims=True)
    gate_cols = [
        lax.dynamic_index_in_dim(gates, mine ^ j, 0, keepdims=False)[:, None]
        for j in range(expert_count)
    ]

    x_parts = exchange(pack(second_in, ranks, capacity, (far_pieces[1][1],)))

    def run(at, part, before=(), other=(), after=()):
        return expert(
            place,
            router_pad,
            [x_parts[j] for j in at],
            [dy_parts[j] for j in at],
            sources[part],
            expert_count,
            before,
            other,
            after,
        )

    near_sums, near_back, near_g, near_act, near_pg = run((0, 1), 0)
    far_stack = jnp.stack([tie(far_pieces[1][0], near_g[0]), *far_pieces[1][1:]])
    sources.append(gather_near(far_stack))
    far_sums, far_back, far_g, low_grad = run(
        (2, 3), 0, other=(x_parts[:2], near_g, near_act, near_pg), after=(far_stack,)
    )
    outs, backs, weighted = near_sums + far_sums, near_back + far_back, near_g + far_g
    sent_out, sent_back, sent_act, sent_pg = run(
        (1, 2, 3), 1, before=(outs[1:], backs[1:], weighted[1:])
    )
    own_out, own_back, high_grad = run(
        (0,),
        1,
        before=(outs[:1], backs[:1], weighted[:1]),
        other=(x_parts[1:], weighted[1:], sent_act, sent_pg),
    )
    out_parts = exchange(own_out + sent_out)
    grad_parts = exchange(own_back + sent_back)
    near_sums = {0: add_near(low_grad)}
    s_sum, gate_grads = unpack_grad(grad_parts, rank_cols, (near_sums[0],))

    gate_grads = gate_grads[:, :expert_count].T
    prob_grad = jnp.concatenate(
        [lax.dynamic_index_in_dim(gate_grads, mine ^ e, 0) for e in range(expert_count)], axis=0
    )
    logit_grad = gates * (prob_grad - jnp.sum(gates * prob_grad, axis=0, keepdims=True))
    logit_grad = logit_grad.astype(BF16)
    router_grad = jnp.dot(logit_grad, second_in, preferred_element_type=F32)
    second_grad = s_sum + lax.dot_general(
        logit_grad, router_t, (((0,), (0,)), ((), ())), preferred_element_type=F32
    )
    gain_two_grad = jnp.sum(second_grad * normed_two, axis=0)
    bias_two_grad = jnp.sum(second_grad, axis=0)
    grad_out = out_grad.astype(F32)
    resid_grad = grad_out + norm_back(second_grad, normed_two, scale_two, norm_full[2])
    branch_grad = resid_grad.astype(BF16)
    proj_grad = jnp.dot(context.T, branch_grad, preferred_element_type=F32)
    context_grad = lax.dot_general(branch_grad, proj_full, NT, preferred_element_type=F32)
    context_grad = context_grad.astype(BF16)

    pairs = width // LANES
    low_parts = far_parts(near_sums[0])
    first_half = attend_back(
        qkv_rows,
        kv_window,
        context_grad,
        first_key,
        last_key,
        lse,
        scale,
        range(0, pairs // 2),
    )
    near_sums[1] = add_near(high_grad, first_half[0])
    second_half = attend_back(
        qkv_rows,
        kv_window,
        context_grad,
        first_key,
        last_key,
        lse,
        scale,
        range(pairs // 2, pairs),
        (near_sums[1], low_parts[1], low_parts[2]),
    )
    block_output = unpack_out(residual, out_parts, rank_cols, gate_cols, (second_half[0],))
    high_parts = far_parts(near_sums[1])
    query_grads, own_grads, outside_grads = [], [], []
    for query_grad, *window_grads in (first_half, second_half):
        query_grads.append(query_grad)
        edges = [
            jnp.concatenate([grad[rows] for grad in window_grads], axis=1)
            for rows in (slice(0, HALO), slice(HALO + row_count, None))
        ]
        from_below, from_above = shift(*edges, ("replica", "group"))
        outside = jnp.concatenate(
            [from_below, jnp.zeros((row_count - 2 * HALO, from_below.shape[1]), BF16), from_above],
            axis=0,
        )
        size = from_below.shape[1] // 2
        for at, grad in enumerate(window_grads):
            own_grads.append(grad[HALO : HALO + row_count])
            outside_grads.append(outside[:, at * size : (at + 1) * size])
    kv_grads = [summed([own_grads[at], outside_grads[at]]) for at in (0, 2, 1, 3)]
    qkv_grad_rows = jnp.concatenate([*query_grads, *kv_grads], axis=1)
    qkv_grad_rows = tie(qkv_grad_rows, low_parts[3], high_parts[1])
    qkv_grad = jnp.dot(first_in.T, qkv_grad_rows, preferred_element_type=F32)
    first_grad = lax.dot_general(qkv_grad_rows, qkv_full, NT, preferred_element_type=F32)
    gain_one_grad = jnp.sum(first_grad * normed_one, axis=0)
    bias_one_grad = jnp.sum(first_grad, axis=0)
    input_grad = (resid_grad + norm_back(first_grad, normed_one, scale_one, norm_full[0])).astype(
        BF16
    )

    norm_grad = jnp.stack([gain_one_grad, bias_one_grad, gain_two_grad, bias_two_grad], axis=0)
    small_grad = jnp.concatenate([norm_grad, router_grad], axis=0).T
    small_grad = jnp.pad(small_grad, ((0, 0), (0, LANES - small_grad.shape[1]))).astype(BF16)
    columns = 3 * width // 2
    qkv_grad, proj_grad = qkv_grad.astype(BF16), proj_grad.astype(BF16)
    qkv_grad = tie(qkv_grad, high_parts[2])
    dense_grads = jnp.stack(
        [
            jnp.concatenate([qkv_grad[:, :columns], proj_grad[:, : width // 2], small_grad], axis=1),
            jnp.concatenate(
                [qkv_grad[:, columns:], proj_grad[:, width // 2 :], jnp.zeros_like(small_grad)],
                axis=1,
            ),
        ]
    )
    got = swap(lax.dynamic_index_in_dim(dense_grads, 1 - core, 0, keepdims=False), CORE_BIT)
    dense_half = summed([lax.dynamic_index_in_dim(dense_grads, core, 0, keepdims=False), got])
    dense_near = scatter_near(dense_half.reshape(group, width // group, -1))
    owned = []
    for parts, wait_for in ((low_parts, qkv_grad), (high_parts, dense_near)):
        share = sum_chips(summed([tie(parts[0], wait_for), *parts[1:]]), expert_count)
        other_chip = swap(share, CHIP_BIT)
        owned.append([share, swap(share, CORE_BIT), other_chip, swap(other_chip, CORE_BIT)])
    dense_half = sum_chips(summed(far_parts(dense_near)), CHIP_BIT)
    low, high = [part.astype(F32) for part in halves(dense_half, swap(dense_half, CORE_BIT), core)]

    small_sum = low[:, columns + width // 2 :][:, :8]
    qkv_sum = jnp.concatenate([low[:, :columns], high[:, :columns]], axis=1)
    proj_sum = jnp.concatenate(
        [part[:, columns : columns + width // 2] for part in (low, high)], axis=1
    )
    norm_new = adam_step(norm_weight, norm_moment, norm_squares, small_sum[:, :4].T, RATES[0])
    qkv_new = adam_step(qkv_weight, qkv_moment, qkv_squares, qkv_sum, RATES[1])
    proj_new = adam_step(proj_weight, proj_moment, proj_squares, proj_sum, RATES[2])
    router_new = adam_step(
        router_weight, router_moment, router_squares, small_sum[:, 4:8], RATES[3]
    )
    states = (
        inner_weight,
        inner_moment,
        inner_squares,
        outer_weight.transpose(0, 2, 1),
        outer_moment.transpose(0, 2, 1),
        outer_squares.transpose(0, 2, 1),
    )
    done = ()
    for base in range(0, expert_count, 2):
        grads = [owned[part][base + at] for at in range(2) for part in range(2)]
        done = update_experts(mine, base, states, grads, done)
    inner_new = done[:3]
    outer_new = [array.transpose(0, 2, 1) for array in done[3:]]
    return (
        block_output,
        input_grad,
        *norm_new,
        *qkv_new,
        *proj_new,
        *router_new,
        *inner_new,
        *outer_new,
    )


def add_near(grads, *after):
    group = lax.axis_size("group")
    return scatter_near(grads.reshape(2, group, -1, grads.shape[-1]), *after)


def solution(mesh):
    tokens = P(("replica", "group"), None)
    columns = P(None, "group")
    rows = P("group", None)
    inner = P(None, "group", None)
    outer = P(None, None, "group")
    weights = (columns,) * 3 + (rows,) * 9 + (inner,) * 3 + (outer,) * 3
    return jax.shard_map(
        per_device,
        mesh=mesh,
        in_specs=(tokens,) * 4 + weights,
        out_specs=(tokens,) * 2 + weights,
        check_vma=False,
    )
```
